128 devices in a mesh: lat: 4 (over z_lo, core), lon: 32 (over z_hi, x, y).
Axes of the slice: x: 4, y: 4, z: 4 (z_hi: 2, z_lo: 2; z = z_hi * 2 + z_lo), core: 2. Of those that a mesh axis runs over, the one named last changes fastest.
Arguments:
- tokens: bfloat16 [2, 72, 768, 1024], P(None, 'lat', 'lon'), may hold values from -6 to 6
- norm_gain: float32 [1024], replicated, may hold values from 0.1 to 1.9
- attention_in: bfloat16 [1024, 3072], replicated, may hold values from -0.1875 to 0.1875
- attention_out: bfloat16 [1024, 1024], replicated, may hold values from -0.1875 to 0.1875
- head_bias: float32 [16, 144, 144], replicated, may hold values from -3 to 400
- cotangent: bfloat16 [2, 72, 768, 1024], P(None, 'lat', 'lon'), may hold values from -6 to 6
Outputs:
- output: bfloat16 [2, 72, 768, 1024], P(None, 'lat', 'lon')
- grad_tokens: bfloat16 [2, 72, 768, 1024], P(None, 'lat', 'lon')
- grad_in: bfloat16 [1024, 3072], P(('lat', 'lon'))
- grad_out: bfloat16 [1024, 1024], P(('lat', 'lon'))
- grad_gain: float32 [1024], P(('lat', 'lon'))
The draws below stay inside these ranges and needn't reach their ends.
All inputs are finite; a program needn't handle non-finite values.
Results may differ from the reference program's by a relative error of at most 0.014.
Values may be sent and summed in bfloat16 or wider, within the bound.
A program may use at most 192 MiB of HBM per device.

```python
import math
import jax
import jax.numpy as jnp
from jax import lax

D = 1024
HEADS = 16
LEV = 2
WIN_LAT = 6
WIN_LON = 12
SH = 3
SW = 6
WIN = 144
NLAT = 72
NLON = 768


def draw_head_bias(key, part):
    key = jax.random.fold_in(key, 11)
    keys = jax.random.split(key, 1)
    base = jnp.clip(jax.random.normal(keys[0], (HEADS, WIN, WIN), jnp.float32), -3.0, 3.0)
    return base.astype(jnp.float32)


def raised(entries, key, source, target, parts, factor):
    def block_of(axis_at):
        return (jnp.arange(entries.shape[axis_at]) // (entries.shape[axis_at] // parts)).reshape((-1,) + (1,) * (entries.ndim - 1 - axis_at))

    near = jax.random.permutation(key, parts)[block_of(target)]
    far = (block_of(target) + parts // 2) % parts
    return jnp.where((block_of(source) == near) | (block_of(source) == far), factor * entries, entries)


def level_of(key, extent, cuts, smallest, largest):
    def one(dim, shards_of):
        steps = jax.random.uniform(jax.random.fold_in(jax.random.fold_in(key, 6), dim), (shards_of,), jnp.float32, smallest / len(cuts), largest / len(cuts))
        return jnp.repeat(jnp.exp(steps), extent[dim] // shards_of).reshape((-1,) + (1,) * (len(extent) - dim - 1))

    factor_of = one(*cuts[0])
    for cut in cuts[1:]:
        factor_of = factor_of * one(*cut)
    return factor_of


def normal_values(key, extent, scale, bound, cuts=(), kind=jnp.bfloat16):
    entries = jax.random.normal(key, extent, jnp.float32) * scale
    if len(cuts) > 0:
        entries = level_of(key, extent, cuts, -0.22, 0.18) * entries
    return jnp.clip(entries, min=-bound, max=bound).astype(kind)


def bell_draw_with(rng, dims, scale, reach, shards, heavy, kind=jnp.bfloat16):
    drawn = scale * jax.random.normal(rng, dims, jnp.float32)
    if shards:
        drawn = drawn * level_of(rng, dims, shards, -0.22, 0.18)
    return jnp.clip(raised(drawn, jax.random.fold_in(rng, 3), *heavy), -reach, reach).astype(kind)


def setup_inputs(seed: int = 0) -> dict:
    key_list = jax.random.split(jax.random.key(seed), 7)
    return {
        "tokens": bell_draw_with(key_list[0], (LEV, NLAT, NLON, D), 1.0, 6.0, ((1, 4), (2, 32)), (2, 3, 32, 2.75)),
        "norm_gain": jnp.clip(1.0 + 0.18 * jax.random.normal(key_list[1], (D,), jnp.float32), 0.1, 1.9),
        "attention_in": normal_values(key_list[2], (D, 3 * D), D ** -0.5, 0.1875),
        "attention_out": normal_values(key_list[3], (D, D), D ** -0.5, 0.1875),
        "head_bias": draw_head_bias(jax.random.fold_in(key_list[6], 71), 0),
        "cotangent": normal_values(key_list[5], (LEV, NLAT, NLON, D), 1.0, 6.0, ((1, 4), (2, 32))),
    }


def rounded(value):
    return lax.optimization_barrier(value.astype(jnp.bfloat16))

def layer_stats(tokens):
    values = tokens.astype(jnp.float32)
    average = lax.optimization_barrier(jnp.mean(values, axis=-1, keepdims=True))
    centred = values - average
    variance = lax.optimization_barrier(jnp.mean(centred * centred, axis=-1, keepdims=True))
    inverse = lax.rsqrt(variance + 1e-05)
    return (centred * inverse, inverse)

def norm_back(cotangent, grad_normed, standard, inverse, norm_gain):
    grad_float = grad_normed.astype(jnp.float32)
    grad_gain = lax.optimization_barrier(jnp.sum(grad_float * standard, axis=(0, 1, 2)))
    grad_scaled = grad_float * norm_gain
    first = lax.optimization_barrier(jnp.mean(grad_scaled, axis=-1, keepdims=True))
    second = lax.optimization_barrier(jnp.mean(grad_scaled * standard, axis=-1, keepdims=True))
    grad_local = inverse * (grad_scaled - first - standard * second)
    return ((cotangent.astype(jnp.float32) + grad_local).astype(jnp.bfloat16), grad_gain)

def region_grid(lat_rows, nlat, breadth):
    labels = (lat_rows >= nlat - 2 * SH).astype(jnp.int32) + (lat_rows >= nlat - SH).astype(jnp.int32)
    return jnp.broadcast_to(labels[None, :, None, None], (LEV, lat_rows.shape[0], breadth, 1))

def to_windows(grid):
    levels, height, breadth, depth = grid.shape
    shaped = grid.reshape(levels, height // WIN_LAT, WIN_LAT, breadth // WIN_LON, WIN_LON, depth)
    return shaped.transpose(1, 3, 0, 2, 4, 5).reshape(-1, levels * WIN_LAT * WIN_LON, depth)

def from_windows(blocks, height, breadth):
    depth = blocks.shape[-1]
    shaped = blocks.reshape(height // WIN_LAT, breadth // WIN_LON, LEV, WIN_LAT, WIN_LON, depth)
    return shaped.transpose(2, 0, 3, 1, 4, 5).reshape(LEV, height, breadth, depth)

def attend(shifted, grad_back, region, attention_in, attention_out, head_bias):
    blocks, window, width = shifted.shape
    head_count = head_bias.shape[0]
    head_size = width // head_count
    scaling = 1.0 / math.sqrt(head_size)
    token_rows = shifted.reshape(blocks * window, width)
    projected = rounded(jnp.dot(token_rows, attention_in, preferred_element_type=jnp.float32))
    projected = projected.astype(jnp.float32).reshape(blocks, window, 3, head_count, head_size)
    query_part = projected[:, :, 0]
    key_part = projected[:, :, 1]
    value_part = projected[:, :, 2]
    scores = jnp.einsum('bqhe,bkhe->bhqk', query_part, key_part) * scaling + head_bias[None]
    allowed = (region[:, :, None] == region[:, None, :])[:, None]
    scores = jnp.where(allowed, scores, -1000000000.0)
    highest = lax.optimization_barrier(jnp.max(scores, axis=-1, keepdims=True))
    powers = jnp.exp(scores - highest)
    weights = powers / lax.optimization_barrier(jnp.sum(powers, axis=-1, keepdims=True))
    weights_b = rounded(weights).astype(jnp.float32)
    context = rounded(jnp.einsum('bhqk,bkhe->bqhe', weights_b, value_part)).reshape(blocks * window, width)
    attended = jnp.dot(context, attention_out, preferred_element_type=jnp.float32).astype(jnp.bfloat16)
    flat_grad = grad_back.reshape(blocks * window, width)
    grad_context = rounded(jnp.dot(flat_grad, attention_out.T, preferred_element_type=jnp.float32))
    grad_out = jnp.dot(context.T, flat_grad, preferred_element_type=jnp.float32)
    grad_context = grad_context.astype(jnp.float32).reshape(blocks, window, head_count, head_size)
    grad_weights = jnp.einsum('bqhe,bkhe->bhqk', grad_context, value_part)
    grad_value = jnp.einsum('bhqk,bqhe->bkhe', weights_b, grad_context).astype(jnp.bfloat16)
    inner = lax.optimization_barrier(jnp.sum(grad_weights * weights, axis=-1, keepdims=True))
    grad_scores = rounded(weights * (grad_weights - inner)).astype(jnp.float32)
    grad_query = (jnp.einsum('bhqk,bkhe->bqhe', grad_scores, key_part) * scaling).astype(jnp.bfloat16)
    grad_key = (jnp.einsum('bhqk,bqhe->bkhe', grad_scores, query_part) * scaling).astype(jnp.bfloat16)
    grad_projected = jnp.stack([grad_query, grad_key, grad_value], axis=2).reshape(blocks * window, 3 * width)
    grad_rows = jnp.dot(grad_projected, attention_in.T, preferred_element_type=jnp.float32).astype(jnp.bfloat16)
    grad_in = jnp.dot(token_rows.T, grad_projected, preferred_element_type=jnp.float32)
    return (attended.reshape(blocks, window, width), grad_rows.reshape(blocks, window, width), grad_in, grad_out)

def reference(tokens, norm_gain, attention_in, attention_out, head_bias, cotangent):
    nlat = tokens.shape[1]
    nlon = tokens.shape[2]
    width = tokens.shape[3]
    standard, inverse = layer_stats(tokens)
    normed = (standard * norm_gain).astype(jnp.bfloat16)
    shifted = jnp.roll(normed, (-SH, -SW), axis=(1, 2))
    grad_shifted = jnp.roll(cotangent, (-SH, -SW), axis=(1, 2))
    region = region_grid(jnp.arange(nlat, dtype=jnp.int32), nlat, nlon)
    shifted_win = to_windows(shifted)
    grad_win = to_windows(grad_shifted)
    region_win = to_windows(region)[..., 0]
    total = shifted_win.shape[0]
    batch = math.gcd(total, 16)
    turns = total // batch
    window = shifted_win.shape[1]

    def one_batch(carry, item):
        attended, grad_rows, grad_in, grad_out = attend(item[0], item[1], item[2], attention_in, attention_out, head_bias)
        return ((carry[0] + grad_in, carry[1] + grad_out), (attended, grad_rows))
    start = (jnp.zeros((width, 3 * width), jnp.float32), jnp.zeros((width, width), jnp.float32))
    items = (shifted_win.reshape(turns, batch, window, width), grad_win.reshape(turns, batch, window, width), region_win.reshape(turns, batch, window))
    sums, outs = lax.scan(one_batch, start, items)
    attended = from_windows(outs[0].reshape(total, window, width), nlat, nlon)
    grad_rows = from_windows(outs[1].reshape(total, window, width), nlat, nlon)
    back_attn = jnp.roll(attended, (SH, SW), axis=(1, 2))
    grad_normed = jnp.roll(grad_rows, (SH, SW), axis=(1, 2))
    output = (tokens.astype(jnp.float32) + back_attn.astype(jnp.float32)).astype(jnp.bfloat16)
    grad_tokens, grad_gain = norm_back(cotangent, grad_normed, standard, inverse, norm_gain)
    return (output, grad_tokens, sums[0].astype(jnp.bfloat16), sums[1].astype(jnp.bfloat16), grad_gain)
```

```python
import jax
import jax.numpy as jnp
import numpy as np
from jax import lax
from jax.experimental import pallas as pl
from jax.experimental.pallas import tpu as pltpu
from jax.sharding import PartitionSpec as P

SH = 3
SW = 6

D=1024; WINT=144; PAIR=288
NT=(((1,),(1,)),((),()))
TN=(((0,),(0,)),((),()))
def dg(a,b,dn): return lax.dot_general(a,b,dn,preferred_element_type=jnp.float32)

def perm_matrix():
    m=np.zeros((PAIR,PAIR),np.float32)
    for j in range(2):
        for l in range(2):
            for r in range(6):
                for c in range(12):
                    m[((j*2+l)*6+r)*12+c,(l*6+r)*24+j*12+c]=1
    return m

def kernel(masked_ref, x_ref, c_ref, gain_ref, win_ref, wout_ref, bias_ref, perm_ref, permt_ref, mask_ref,
           out_ref, gt_ref, xw_ref, cw_ref, ctx_ref, gp_ref, gg_ref,
           proj, gctx, bias):
    i=pl.program_id(0)
    @pl.when(i==0)
    def _():
        bias[...]=bias_ref[...]
        gg_ref[...]=jnp.zeros_like(gg_ref)
    @pl.when((i==2)&(masked_ref[0]>0))
    def _():
        def body(p,_):
            bias[p]=bias[p]+mask_ref[...]
            return 0
        lax.fori_loop(0,8,body,0)
    x=x_ref[...].reshape(PAIR,D).astype(jnp.float32)
    mean=jnp.mean(x,axis=-1,keepdims=True)
    cen=x-mean
    inv=lax.rsqrt(jnp.mean(cen*cen,axis=-1,keepdims=True)+1e-5)
    normed=(cen*inv*gain_ref[...]).astype(jnp.bfloat16)
    xw_ref[...]=jnp.dot(perm_ref[...],normed,preferred_element_type=jnp.float32).astype(jnp.bfloat16)
    cw_ref[...]=jnp.dot(perm_ref[...],c_ref[...].reshape(PAIR,D),preferred_element_type=jnp.float32).astype(jnp.bfloat16)
    for n in range(6):
        s=slice(n*512,(n+1)*512)
        v=jnp.dot(xw_ref[...],win_ref[:,s],preferred_element_type=jnp.float32)
        if n<2: v=v*0.125
        proj[:,s]=v.astype(jnp.bfloat16)
    for n in range(2):
        s=slice(n*512,(n+1)*512)
        gctx[:,s]=dg(cw_ref[...],wout_ref[s,:],NT).astype(jnp.bfloat16)
    m0=lax.broadcasted_iota(jnp.int32,(WINT,128),1)<64
    zero=jnp.zeros((WINT,128),jnp.bfloat16)
    def unit(j,p):
        rows=pl.ds(j*WINT,WINT)
        o=pl.multiple_of(p*128,128)
        q=proj[rows,pl.ds(o,128)]
        k=proj[rows,pl.ds(pl.multiple_of(1024+o,128),128)]
        v=proj[rows,pl.ds(pl.multiple_of(2048+o,128),128)]
        d=gctx[rows,pl.ds(o,128)]
        ks=jnp.concatenate([jnp.where(m0,k,zero),jnp.where(m0,zero,k)],0)
        vs=jnp.concatenate([jnp.where(m0,v,zero),jnp.where(m0,zero,v)],0)
        st=(dg(ks,q,NT)+bias[p]).reshape(2,WINT,WINT)
        pw=jnp.exp(st-jnp.max(st,axis=1,keepdims=True))
        w=pw*(1.0/jnp.sum(pw,axis=1,keepdims=True))
        wb=w.astype(jnp.bfloat16).reshape(PAIR,WINT)
        ctx_ref[rows,pl.ds(o,128)]=dg(wb,vs,TN).astype(jnp.bfloat16)
        dw=dg(vs,d,NT).reshape(2,WINT,WINT)
        inner=jnp.sum(dw*w,axis=1,keepdims=True)
        ds=(w*(dw-inner)).astype(jnp.bfloat16).reshape(PAIR,WINT)
        gv=jnp.dot(wb,d,preferred_element_type=jnp.float32)
        gk=jnp.dot(ds,q,preferred_element_type=jnp.float32)
        gq=dg(ds,ks,TN)*0.125
        gp_ref[rows,pl.ds(o,128)]=gq.astype(jnp.bfloat16)
        gp_ref[rows,pl.ds(pl.multiple_of(1024+o,128),128)]=jnp.where(m0,gk[:WINT],gk[WINT:]).astype(jnp.bfloat16)
        gp_ref[rows,pl.ds(pl.multiple_of(2048+o,128),128)]=jnp.where(m0,gv[:WINT],gv[WINT:]).astype(jnp.bfloat16)
    def body(p,_):
        unit(0,p); unit(1,p)
        return 0
    lax.fori_loop(0,8,body,0)
    att=jnp.dot(ctx_ref[...],wout_ref[...],preferred_element_type=jnp.float32).astype(jnp.bfloat16)
    att=jnp.dot(permt_ref[...],att,preferred_element_type=jnp.float32)
    out_ref[...]=(x_ref[...].reshape(PAIR,D).astype(jnp.float32)+att).astype(jnp.bfloat16).reshape(2,WINT,D)
    gr=dg(gp_ref[...],win_ref[...],NT).astype(jnp.bfloat16)
    gr=jnp.dot(permt_ref[...],gr,preferred_element_type=jnp.float32)
    std=cen*inv
    gg_ref[...]+=jnp.sum(gr*std,axis=0,keepdims=True)
    gs=gr*gain_ref[...]
    first=jnp.mean(gs,axis=-1,keepdims=True)
    second=jnp.mean(gs*std,axis=-1,keepdims=True)
    gt_ref[...]=(c_ref[...].reshape(PAIR,D).astype(jnp.float32)+inv*(gs-first-std*second)).astype(jnp.bfloat16).reshape(2,WINT,D)

def k2(masked,x,c,gain,win,wout,biasT,mask):
    bf=jnp.bfloat16
    vm=pl.BlockSpec(memory_space=pltpu.VMEM)
    blk=pl.BlockSpec((2,WINT,D),lambda i:(0,i,0))
    row=lambda n: pl.BlockSpec((PAIR,n),lambda i:(i,0))
    P=perm_matrix()
    return pl.pallas_call(kernel,grid=(3,),
      in_specs=[pl.BlockSpec(memory_space=pltpu.SMEM),blk,blk,vm,vm,vm,vm,vm,vm,vm],
      out_specs=[blk,blk,row(1024),row(1024),row(1024),row(3072),pl.BlockSpec((1,D),lambda i:(0,0))],
      out_shape=[jax.ShapeDtypeStruct((2,432,D),bf)]*2+[jax.ShapeDtypeStruct((864,n),bf) for n in (1024,1024,1024,3072)]+[jax.ShapeDtypeStruct((1,D),jnp.float32)],
      scratch_shapes=[pltpu.VMEM((PAIR,3072),bf),pltpu.VMEM((PAIR,1024),bf),pltpu.VMEM((8,PAIR,WINT),jnp.float32)],
      compiler_params=pltpu.CompilerParams(vmem_limit_bytes=60*2**20),
    )(masked,x,c,gain.reshape(1,D),win,wout,biasT,jnp.asarray(P,bf),jnp.asarray(P.T,bf),mask)

def prep_bias(head_bias):
    return jnp.swapaxes(head_bias,1,2).reshape(8,PAIR,WINT)
def mask_np():
    reg=np.array([0 if r<3 else 1 for l in range(2) for r in range(6) for c in range(12)])
    m=np.where(reg[:,None]==reg[None,:],0.0,-1e9).astype(np.float32)
    return np.concatenate([m,m],0)


AXES = ("x", "y", "z")
ORDERS = (("x", "y", "z"), ("y", "z", "x"), ("z", "x", "y"))
LANES = (768, 640, 640)
FIRST = (384, 384, 256)


def mesh_place(coords):
    core, x, y, z = coords
    return ((z % 2) * 2 + core, (z // 2) * 16 + x * 4 + y)


def sums_kernel(xw_ref, cw_ref, ctx_ref, gp_ref, gg_ref, gi_out, go_out, gg_out, xt, ct, *scratch):
    scratch = list(scratch)

    def take(count):
        out = scratch[:count]
        del scratch[:count]
        return out

    sends, owns, halves, bases = take(3), take(3), take(3), take(3)
    landing = {}
    for g in range(3):
        for phase in range(3):
            landing[g, phase] = take(8)
    finals = take(6)
    gain_mine, gain_land = take(2)
    core_send, core_recv, ring_send, ring_recv, gain_send, gain_recv = take(6)

    lat = lax.axis_index("lat")
    lon = lax.axis_index("lon")
    core = lat % 2
    me = {"x": (lon // 4) % 4, "y": lon % 4, "z": (lon // 16) * 2 + lat // 2}

    def device(axis, step):
        at = dict(me)
        at[axis] = (me[axis] + step + 4) % 4
        return mesh_place((core, at["x"], at["y"], at["z"]))

    sibling = mesh_place((1 - core, me["x"], me["y"], me["z"]))
    barrier = pltpu.get_barrier_semaphore()
    neighbours = [sibling] + [device(a, s) for a in AXES for s in (1, -1)]
    for other in neighbours:
        pl.semaphore_signal(barrier, inc=1, device_id=other, device_id_type=pl.DeviceIdType.MESH)
    pl.semaphore_wait(barrier, len(neighbours))

    def remote(src, dst, send, recv, place):
        copy = pltpu.make_async_remote_copy(
            src_ref=src,
            dst_ref=dst,
            send_sem=send,
            recv_sem=recv,
            device_id=place,
            device_id_type=pl.DeviceIdType.MESH,
        )
        copy.start()
        return copy

    def gain_step(stage, total):
        gain_mine[stage] = total
        if stage == 0:
            copy = remote(gain_mine.at[0], gain_land.at[0], gain_send.at[0], gain_recv.at[0], sibling)
            return [copy]
        axis = AXES[stage - 1]
        slot = 3 * stage - 2
        up = remote(gain_mine.at[stage], gain_land.at[slot], gain_send.at[slot], gain_recv.at[slot], device(axis, 1))
        down = remote(
            gain_mine.at[stage], gain_land.at[slot + 1], gain_send.at[slot + 1], gain_recv.at[slot + 1], device(axis, -1)
        )
        return [up, down]

    def gain_relay(stage, copies):
        if stage == 0:
            return copies
        axis = AXES[stage - 1]
        slot = 3 * stage - 2
        copies[0].wait_recv()
        far = remote(
            gain_land.at[slot], gain_land.at[slot + 2], gain_send.at[slot + 2], gain_recv.at[slot + 2], device(axis, 1)
        )
        return copies + [far]

    def gain_end(stage, copies):
        total = gain_mine[stage]
        if stage == 0:
            copies[0].wait()
            return total + gain_land[0]
        copies[0].wait_send()
        copies[1].wait()
        copies[2].wait()
        slot = 3 * stage - 2
        return total + gain_land[slot] + gain_land[slot + 1] + gain_land[slot + 2]

    def products(half, targets):
        def rows_of(zl, _):
            at = pl.multiple_of(zl * 512 + half * 256, 256)
            xt[...] = xw_ref[:, pl.ds(at, 256)].T
            ct[...] = ctx_ref[:, pl.ds(at, 256)].T
            start = 0
            for g in range(3):
                left = jnp.dot(
                    xt[...], gp_ref[:, start : start + LANES[g]], preferred_element_type=jnp.float32
                )
                parts = []
                low, high = start + 2048, start + 2048 + LANES[g]
                if low < 3072:
                    parts.append(
                        jnp.dot(xt[...], gp_ref[:, low : min(high, 3072)], preferred_element_type=jnp.float32)
                    )
                if high > 3072:
                    parts.append(
                        jnp.dot(
                            ct[...], cw_ref[:, max(low, 3072) - 3072 : high - 3072], preferred_element_type=jnp.float32
                        )
                    )
                right = parts[0] if len(parts) == 1 else jnp.concatenate(parts, 1)
                both = jnp.concatenate([left.reshape(32, 8, LANES[g]), right.reshape(32, 8, LANES[g])], 1)
                targets[g][zl] = both.astype(jnp.bfloat16).reshape(2, 4, 4, 16, LANES[g])
                start += LANES[g]
            return 0

        lax.fori_loop(0, 2, rows_of, 0)

    gain_copies = gain_step(0, gg_ref[...])
    products(1 - core, sends)
    core_copies = [
        remote(sends[g], halves[g], core_send.at[g], core_recv.at[g], sibling) for g in range(3)
    ]
    products(core, owns)
    gain_total = gain_end(0, gain_copies)
    for g in range(3):
        core_copies[g].wait()
        bases[g][...] = (
            owns[g][...].astype(jnp.float32) + halves[g][...].astype(jnp.float32)
        ).astype(jnp.bfloat16)

    current = [(bases[g], ("zl", "zh", "x", "y")) for g in range(3)]
    for phase in range(3):
        gain_copies = gain_step(phase + 1, gain_total)
        flying = {}
        chunks = {}
        for g in range(3):
            axis = ORDERS[g][phase]
            ref, dims = current[g]
            m = me[axis]
            split = FIRST[g]
            ends = (pl.ds(0, split), pl.ds(split, LANES[g] - split))

            def chunk(step, half, ref=ref, dims=dims, m=m, axis=axis, ends=ends):
                t = (m + step + 4) % 4
                place = []
                for dim in dims:
                    if dim == axis:
                        place.append(t)
                    elif axis == "z" and dim == "zl":
                        place.append(t % 2)
                    elif axis == "z" and dim == "zh":
                        place.append(t // 2)
                    else:
                        place.append(slice(None))
                return ref.at[tuple(place) + (slice(None), ends[half])]

            chunks[g] = chunk
            land = landing[g, phase]

            def send(number, src, step, g=g, axis=axis, land=land, phase=phase):
                return remote(
                    src, land[number], ring_send.at[g, phase, number], ring_recv.at[g, phase, number], device(axis, step)
                )

            flying[g] = {
                0: send(0, chunk(2, 0), 1),
                3: send(3, chunk(2, 1), -1),
                1: send(1, chunk(1, 1), 1),
                4: send(4, chunk(-1, 0), -1),
            }
            flying[g]["send"] = send
        gain_copies = gain_relay(phase + 1, gain_copies)
        for g in range(3):
            land = landing[g, phase]
            for number, step, half, slot in ((0, 1, 0, 6), (3, -1, 1, 7)):
                flying[g][number].wait_recv()
                land[slot][...] = (
                    land[number][...].astype(jnp.float32) + chunks[g](step, half)[...].astype(jnp.float32)
                ).astype(jnp.bfloat16)
                flying[g][number + 2] = flying[g]["send"](number + 2, land[slot], step)
        gain_total = gain_end(phase + 1, gain_copies)
        for g in range(3):
            land = landing[g, phase]
            flying[g][1].wait()
            flying[g][4].wait()
            flying[g][2].wait()
            flying[g][5].wait()
            flying[g][0].wait_send()
            flying[g][3].wait_send()
            first = (
                chunks[g](0, 0)[...].astype(jnp.float32)
                + land[2][...].astype(jnp.float32)
                + land[4][...].astype(jnp.float32)
            )
            second = (
                chunks[g](0, 1)[...].astype(jnp.float32)
                + land[1][...].astype(jnp.float32)
                + land[5][...].astype(jnp.float32)
            )
            axis = ORDERS[g][phase]
            if phase < 2:
                gone = ("zl", "zh") if axis == "z" else (axis,)
                dims = tuple(d for d in current[g][1] if d not in gone)
                ref = finals[3 * phase + g]
                ref[..., : FIRST[g]] = first.astype(jnp.bfloat16)
                ref[..., FIRST[g] :] = second.astype(jnp.bfloat16)
                current[g] = (ref, dims)
            else:
                at = sum(LANES[:g])
                for value, low in ((first, at), (second, at + FIRST[g])):
                    value = value.astype(jnp.bfloat16)
                    wide = value.shape[1]
                    gi_out[:, low : low + wide] = value[:8]
                    inside = max(0, min(wide, 1024 - low))
                    if inside > 0:
                        gi_out[:, low + 2048 : low + 2048 + inside] = value[8:, :inside]
                    if inside < wide:
                        go_out[:, low + inside - 1024 : low + wide - 1024] = value[8:, inside:]
    gg_out[...] = gain_total


def reduce_sums(xw, cw, ctx, gp, gg):
    bf = jnp.bfloat16
    vm = pl.BlockSpec(memory_space=pltpu.VMEM)
    scratch = [pltpu.VMEM((256, 864), bf), pltpu.VMEM((256, 864), bf)]
    for _ in range(4):
        scratch += [pltpu.VMEM((2, 2, 4, 4, 16, wide), bf) for wide in LANES]
    sizes = {"zl": 2, "zh": 2, "x": 4, "y": 4}
    later = []
    for g in range(3):
        dims = ("zl", "zh", "x", "y")
        for phase in range(3):
            axis = ORDERS[g][phase]
            gone = ("zl", "zh") if axis == "z" else (axis,)
            dims = tuple(d for d in dims if d not in gone)
            lead = tuple(sizes[d] for d in dims)
            a, b = FIRST[g], LANES[g] - FIRST[g]
            scratch += [pltpu.VMEM(lead + (16, wide), bf) for wide in (a, b, a, b, a, b, a, b)]
            later.append((phase, g, lead))
    for phase in range(2):
        for g in range(3):
            lead = [item[2] for item in later if item[:2] == (phase, g)][0]
            scratch.append(pltpu.VMEM(lead + (16, LANES[g]), bf))
    scratch += [
        pltpu.VMEM((4, 8, 128), jnp.float32),
        pltpu.VMEM((10, 8, 128), jnp.float32),
        pltpu.SemaphoreType.DMA((3,)),
        pltpu.SemaphoreType.DMA((3,)),
        pltpu.SemaphoreType.DMA((3, 3, 6)),
        pltpu.SemaphoreType.DMA((3, 3, 6)),
        pltpu.SemaphoreType.DMA((10,)),
        pltpu.SemaphoreType.DMA((10,)),
    ]
    return pl.pallas_call(
        sums_kernel,
        in_specs=[vm] * 5,
        out_specs=[vm] * 3,
        out_shape=[
            jax.ShapeDtypeStruct((8, 3072), bf),
            jax.ShapeDtypeStruct((8, 1024), bf),
            jax.ShapeDtypeStruct((8, 128), jnp.float32),
        ],
        scratch_shapes=scratch,
        compiler_params=pltpu.CompilerParams(
            collective_id=0, has_side_effects=True, vmem_limit_bytes=60 * 2**20
        ),
    )(xw, cw, ctx, gp, gg)


def passed_along(block, axis, distance):
    count = lax.axis_size(axis)
    return lax.ppermute(block, axis, [((i - distance) % count, i) for i in range(count)])


def move_ahead(fields):
    strips = passed_along(jnp.stack([field[:, :SH] for field in fields]), "lat", -1)
    fields = [jnp.concatenate([field[:, SH:], strips[i]], 1) for i, field in enumerate(fields)]
    strips = passed_along(jnp.stack([field[:, :, :SW] for field in fields]), "lon", -1)
    return [jnp.concatenate([field[:, :, SW:], strips[i]], 2) for i, field in enumerate(fields)]


def move_behind(fields):
    strips = passed_along(jnp.stack([field[:, -SH:] for field in fields]), "lat", 1)
    fields = [jnp.concatenate([strips[i], field[:, :-SH]], 1) for i, field in enumerate(fields)]
    strips = passed_along(jnp.stack([field[:, :, -SW:] for field in fields]), "lon", 1)
    return [jnp.concatenate([strips[i], field[:, :, :-SW]], 2) for i, field in enumerate(fields)]


def local(tokens, norm_gain, attention_in, attention_out, head_bias, cotangent):
    shape = tokens.shape
    lat = lax.axis_index("lat")
    lon = lax.axis_index("lon")
    x, c = move_ahead([tokens, cotangent])
    masked = (lat == 3).astype(jnp.int32).reshape(1)
    out, gt, xw, cw, ctx, gp, gg = k2(
        masked,
        x.reshape(2, 432, D),
        c.reshape(2, 432, D),
        norm_gain,
        attention_in,
        attention_out,
        prep_bias(head_bias),
        jnp.asarray(mask_np()),
    )
    gi, go, gains = reduce_sums(xw, cw, ctx, gp, gg.reshape(8, 128))
    gain = lax.dynamic_slice(gains.reshape(1024), ((lat * 32 + lon) * 8,), (8,))
    out, gt = move_behind([out.reshape(shape), gt.reshape(shape)])
    return out, gt, gi, go, gain


def solution(mesh):
    split = P(None, "lat", "lon", None)
    both = ("lat", "lon")
    return jax.shard_map(
        local,
        mesh=mesh,
        in_specs=(split, P(), P(), P(), P(), split),
        out_specs=(split, split, P(both, None), P(both, None), P(both)),
        check_vma=False,
    )
```

```python
import jax
import jax.numpy as jnp
import numpy as np
from jax import lax
from jax.experimental import pallas as pl
from jax.experimental.pallas import tpu as pltpu
from jax.sharding import PartitionSpec as P

D = 1024
WINT = 144
PAIR = 288
OWN = 864
STRIP = 384
NT = (((1,), (1,)), ((), ()))
TN = (((0,), (0,)), ((), ()))
BF = jnp.bfloat16
F32 = jnp.float32

WINDOWS = ((0, 0), (1, 0), (2, 0), (2, 1), (0, 1), (1, 1))

AXES = ("x", "y", "z")
ORDERS = (("x", "y", "z"), ("y", "z", "x"), ("z", "x", "y"))
PIECES = (
    tuple((("in", 1024 * g, 512),) for g in range(3)),
    (
        (("in", 512, 512), ("out", 0, 512)),
        (("in", 1536, 512), ("out", 512, 256)),
        (("in", 2560, 512), ("out", 768, 256)),
    ),
)
LANES = tuple(tuple(sum(p[2] for p in group) // 2 for group in rnd) for rnd in PIECES)
FIRST = ((128, 128, 128), (256, 256, 128))
SIZES = {"zl": 2, "zh": 2, "x": 4, "y": 4}


def left_dims(dims, axis):
    gone = ("zl", "zh") if axis == "z" else (axis,)
    return tuple(d for d in dims if d not in gone)


def strip_cells():
    cells = [(l, r, c) for l in range(2) for r in range(3) for c in range(24)]
    cells += [(l, r, c) for l in range(2) for r in range(3, 15) for c in range(6)]
    cells += [(l, r, c) for l in range(2) for r in range(15, 18) for c in range(6)] + [None] * 12
    cells += [(l, r, c) for l in range(2) for r in range(3) for c in range(6)] + [None] * 12
    return cells


def window_cells():
    return [
        (l, 3 + 6 * i + a, 6 + 12 * j + b)
        for i, j in WINDOWS
        for l in range(2)
        for a in range(6)
        for b in range(12)
    ]


def received_cells():
    cells = []
    for n, cell in enumerate(strip_cells()):
        if cell is None:
            cells.append(None)
            continue
        l, r, c = cell
        if n < 144 or n >= 336:
            r += 18
        if n >= 144:
            c += 24
        cells.append((l, r, c))
    return cells


def one_hot(targets, sources):
    place = {}
    for n, cell in enumerate(sources):
        if cell is not None and cell not in place:
            place[cell] = n
    out = np.zeros((len(targets), len(sources)), np.float32)
    for n, cell in enumerate(targets):
        if cell is not None and cell in place:
            out[n, place[cell]] = 1
    return out


def permutations():
    own = [(l, r, c) for l in range(2) for r in range(18) for c in range(24)]
    strips = strip_cells()
    got = received_cells()
    win = window_cells()
    wide = own[64:368] + own[496:800]
    mid = own[72:360] + own[504:792]
    bottom = own[360:432] + own[792:864]
    top = own[:72] + own[432:504]
    return (
        one_hot(strips, own),
        one_hot(win[:288], wide),
        one_hot(win[288:576], own[352:432] + own[784:864] + got[:144] + got[288:]),
        one_hot(win[576:], wide + got[144:288]),
        one_hot(got[:144] + got[288:], win[288:576]),
        one_hot(got[144:288], win[576:]),
        one_hot(mid, win[:288] + win[576:] + strips[144:288]),
        one_hot(bottom, win[288:576] + strips[288:336]),
        one_hot(top, [c if c is not None and c[2] >= 6 else None for c in strips[:144]] + strips[336:]),
    )


def region_mask():
    region = np.array([a < 3 for l in range(2) for a in range(6) for b in range(12)])
    one = np.where(region[:, None] == region[None, :], 0.0, -1e9).astype(np.float32)
    return np.concatenate([one, one], 0)


def dg(a, b, dims):
    return lax.dot_general(a, b, dims, preferred_element_type=F32)


def dot(a, b):
    return jnp.dot(a, b, preferred_element_type=F32)


def mesh_place(core, x, y, z):
    return ((z % 2) * 2 + core, (z // 2) * 16 + x * 4 + y)


def block_kernel(
    tok_hbm, cot_hbm, gain_ref, win_hbm, wout_hbm, hb_hbm, mask_ref,
    pack_ref, p0_ref, p1_ref, p2_ref, r1_ref, r2_ref, imid_ref, ibot_ref, itop_ref,
    out_hbm, gt_hbm, gi_out, go_out, gg_out,
    *scratch,
):
    scratch = list(scratch)

    def take(count):
        out = scratch[:count]
        del scratch[:count]
        return out

    own_x, own_c, xw, cw, nw, nwt, ct, proj, gctx, win, wout, bias, mask = take(13)
    send_strip, recv_strip = take(4), take(4)
    sends = [take(3), take(3)]
    owns = [take(3), take(3)]
    halves = [take(3), take(3)]
    landing = {(r, g, p): take(8) for r in range(2) for g in range(3) for p in range(3)}
    middles = {(r, g, p): take(1)[0] for r in range(2) for g in range(3) for p in range(2)}
    gain_mine, gain_land = take(2)
    load_sem, strip_send, strip_recv, core_send, core_recv = take(5)
    ring_send, ring_recv, gain_send, gain_recv = take(4)

    lat = lax.axis_index("lat")
    lon = lax.axis_index("lon")
    core = lat % 2
    me = {"x": (lon // 4) % 4, "y": lon % 4, "z": (lon // 16) * 2 + lat // 2}

    def device(axis, step):
        at = dict(me)
        at[axis] = (me[axis] + step + 4) % 4
        return mesh_place(core, at["x"], at["y"], at["z"])

    sibling = mesh_place(1 - core, me["x"], me["y"], me["z"])

    def grid_place(a, b):
        return ((lat + a + 4) % 4, (lon + b + 32) % 32)

    loads = [
        pltpu.make_async_copy(src, dst, load_sem.at[n])
        for n, (src, dst) in enumerate(
            ((tok_hbm, own_x), (cot_hbm, own_c), (win_hbm, win), (wout_hbm, wout), (hb_hbm, bias))
        )
    ]
    for load in loads:
        load.start()

    barrier = pltpu.get_barrier_semaphore()
    partners = [sibling] + [device(a, s) for a in AXES for s in (1, -1)]
    partners += [grid_place(s * a, s * b) for a, b in ((1, 0), (0, 1), (1, 1)) for s in (1, -1)]
    for other in partners:
        pl.semaphore_signal(barrier, inc=1, device_id=other, device_id_type=pl.DeviceIdType.MESH)
    pl.semaphore_wait(barrier, len(partners))

    def remote(src, dst, send, recv, place):
        copy = pltpu.make_async_remote_copy(
            src_ref=src,
            dst_ref=dst,
            send_sem=send,
            recv_sem=recv,
            device_id=place,
            device_id_type=pl.DeviceIdType.MESH,
        )
        copy.start()
        return copy

    PARTS = ((0, 144, 1, 0), (144, 192, 0, 1), (336, 48, 1, 1))

    def send_strips(number, way, parts=(0, 1, 2)):
        copies = []
        for part in parts:
            low, size, a, b = PARTS[part]
            copies.append(
                remote(
                    send_strip[number].at[pl.ds(low, size)],
                    recv_strip[number].at[pl.ds(low, size)],
                    strip_send.at[number, part],
                    strip_recv.at[number, part],
                    grid_place(way * a, way * b),
                )
            )
        return copies

    strip_copies = []
    for number, own in ((0, own_x), (1, own_c)):
        loads[number].wait()
        send_strip[number][...] = dot(pack_ref[...], own[...]).astype(BF)
        strip_copies.append(send_strips(number, -1))

    def gathered(own, strip, s):
        if s == 1:
            parts = [own[352:432], own[784:864], strip[0:144], strip[288:384]]
            return dot(p1_ref[...], jnp.concatenate(parts, 0))
        parts = [own[64:368], own[496:800]]
        if s == 0:
            return dot(p0_ref[...], jnp.concatenate(parts, 0))
        return dot(p2_ref[...], jnp.concatenate(parts + [strip[144:288]], 0))

    def standardised(x):
        centred = x - jnp.mean(x, axis=-1, keepdims=True)
        inverse = lax.rsqrt(jnp.mean(centred * centred, axis=-1, keepdims=True) + 1e-5)
        return centred * inverse, inverse

    def gather_step(s):
        rows = slice(s * PAIR, (s + 1) * PAIR)
        x = gathered(own_x, recv_strip[0], s)
        xw[rows] = x.astype(BF)
        standard, _ = standardised(x)
        nw[rows] = (standard * gain_ref[...]).astype(BF)
        cw[rows] = gathered(own_c, recv_strip[1], s).astype(BF)

    def project(s, count):
        rows = slice(s * PAIR, s * PAIR + count)

        def columns(n, _):
            at = pl.ds(pl.multiple_of(n * 512, 512), 512)
            value = dot(nw[rows], win[:, at])
            proj[rows, at] = (value * jnp.where(n < 2, 0.125, 1.0)).astype(BF)
            return 0

        lax.fori_loop(0, 6, columns, 0)

        def outer(n, _):
            at = pl.ds(pl.multiple_of(n * 512, 512), 512)
            gctx[rows, at] = dg(cw[rows], wout[at, :], NT).astype(BF)
            return 0

        lax.fori_loop(0, 2, outer, 0)

    low_half = lax.broadcasted_iota(jnp.int32, (WINT, 128), 1) < 64
    zero = jnp.zeros((WINT, 128), BF)

    def unit(w, p, masked):
        rows = pl.ds(pl.multiple_of(w * WINT, 16), WINT)
        at_q = pl.ds(pl.multiple_of(p * 128, 128), 128)
        at_k = pl.ds(pl.multiple_of(1024 + p * 128, 128), 128)
        at_v = pl.ds(pl.multiple_of(2048 + p * 128, 128), 128)
        q, k, v, d = proj[rows, at_q], proj[rows, at_k], proj[rows, at_v], gctx[rows, at_q]
        ks = jnp.concatenate([jnp.where(low_half, k, zero), jnp.where(low_half, zero, k)], 0)
        vs = jnp.concatenate([jnp.where(low_half, v, zero), jnp.where(low_half, zero, v)], 0)
        offset = bias[pl.ds(2 * p, 2)]
        if masked is not None:
            offset = offset + mask[masked]
        st = dg(ks, q, NT).reshape(2, WINT, WINT) + offset
        powers = jnp.exp(st - jnp.max(st, axis=1, keepdims=True))
        weights = powers * (1.0 / jnp.sum(powers, axis=1, keepdims=True))
        wb = weights.astype(BF).reshape(PAIR, WINT)
        gctx[rows, at_q] = dg(wb, vs, TN).astype(BF)
        dw = dg(vs, d, NT).reshape(2, WINT, WINT)
        inner = jnp.sum(dw * weights, axis=1, keepdims=True)
        ds = (weights * (dw - inner)).astype(BF).reshape(PAIR, WINT)
        gv = dot(wb, d)
        gk = dot(ds, q)
        proj[rows, at_q] = (dg(ds, ks, TN) * 0.125).astype(BF)
        proj[rows, at_k] = jnp.where(low_half, gk[:WINT], gk[WINT:]).astype(BF)
        proj[rows, at_v] = jnp.where(low_half, gv[:WINT], gv[WINT:]).astype(BF)

    def late_windows(p):
        def two(t, _):
            masked = jnp.where(t == 0, 1, 0)
            unit(2 + 2 * t, p, masked)
            unit(3 + 2 * t, p, masked)
            return 0

        lax.fori_loop(0, 2, two, 0)

    def products(rnd, half, targets):
        def rows_of(zl, _):
            at = pl.multiple_of(zl * 512 + half * 256, 256)
            if rnd == 1:
                ct[...] = gctx[:, pl.ds(at, 256)].T
            for g in range(3):
                lane = 0
                for kind, first, width in PIECES[rnd][g]:
                    if kind == "in":
                        value = dot(nwt[pl.ds(at, 256), :], proj[:, first : first + width])
                    else:
                        value = dot(ct[...], cw[:, first : first + width])
                    value = value.reshape(32, 8, width)
                    wide = width // 2
                    both = jnp.concatenate([value[:, :, :wide], value[:, :, wide:]], 1)
                    targets[g][zl, :, :, :, :, lane : lane + wide] = both.astype(BF).reshape(2, 4, 4, 16, wide)
                    lane += wide
            return 0

        lax.fori_loop(0, 2, rows_of, 0)

    def start_core(rnd):
        return [
            remote(sends[rnd][g], halves[rnd][g], core_send.at[rnd, g], core_recv.at[rnd, g], sibling)
            for g in range(3)
        ]

    def end_core(rnd, copies):
        for g in range(3):
            copies[g].wait()
            owns[rnd][g][...] = (owns[rnd][g][...].astype(F32) + halves[rnd][g][...].astype(F32)).astype(BF)

    def source(rnd, g, phase):
        dims = ("zl", "zh", "x", "y")
        for axis in ORDERS[g][:phase]:
            dims = left_dims(dims, axis)
        return (owns[rnd][g] if phase == 0 else middles[rnd, g, phase - 1]), dims

    def chunk(rnd, g, phase, step, half):
        ref, dims = source(rnd, g, phase)
        axis = ORDERS[g][phase]
        t = (me[axis] + step + 4) % 4
        split = FIRST[rnd][g]
        end = (pl.ds(0, split), pl.ds(split, LANES[rnd][g] - split))[half]
        place = []
        for dim in dims:
            if dim == axis:
                place.append(t)
            elif axis == "z" and dim == "zl":
                place.append(t % 2)
            elif axis == "z" and dim == "zh":
                place.append(t // 2)
            else:
                place.append(slice(None))
        return ref.at[tuple(place) + (slice(None), end)]

    def ring(rnd, g, phase, number, src, step):
        return remote(
            src,
            landing[rnd, g, phase][number],
            ring_send.at[rnd, g, phase, number],
            ring_recv.at[rnd, g, phase, number],
            device(ORDERS[g][phase], step),
        )

    flying = {}

    def ring_start(rnd, phase):
        for g in range(3):
            flying[rnd, g] = {
                0: ring(rnd, g, phase, 0, chunk(rnd, g, phase, 2, 0), 1),
                3: ring(rnd, g, phase, 3, chunk(rnd, g, phase, 2, 1), -1),
                1: ring(rnd, g, phase, 1, chunk(rnd, g, phase, 1, 1), 1),
                4: ring(rnd, g, phase, 4, chunk(rnd, g, phase, -1, 0), -1),
            }

    def ring_relay(rnd, phase):
        for g in range(3):
            land = landing[rnd, g, phase]
            for number, step, half, slot in ((0, 1, 0, 6), (3, -1, 1, 7)):
                flying[rnd, g][number].wait_recv()
                land[slot][...] = (
                    land[number][...].astype(F32) + chunk(rnd, g, phase, step, half)[...].astype(F32)
                ).astype(BF)
                flying[rnd, g][number + 2] = ring(rnd, g, phase, number + 2, land[slot], step)

    def ring_end(rnd, phase):
        for g in range(3):
            land = landing[rnd, g, phase]
            copies = flying[rnd, g]
            for number in (1, 4, 2, 5):
                copies[number].wait()
            copies[0].wait_send()
            copies[3].wait_send()
            split = FIRST[rnd][g]
            for half, near, far in ((0, 4, 2), (1, 1, 5)):
                value = (
                    chunk(rnd, g, phase, 0, half)[...].astype(F32)
                    + land[near][...].astype(F32)
                    + land[far][...].astype(F32)
                ).astype(BF)
                start = half * split
                wide = value.shape[-1]
                if phase < 2:
                    middles[rnd, g, phase][..., start : start + wide] = value
                    continue
                lane = 0
                for kind, first, width in PIECES[rnd][g]:
                    low, high = max(start, lane), min(start + wide, lane + width // 2)
                    if low < high:
                        target = gi_out if kind == "in" else go_out
                        part = value[:, low - start : high - start]
                        at = first + low - lane
                        target[:, at : at + high - low] = part[:8]
                        at += width // 2
                        target[:, at : at + high - low] = part[8:]
                    lane += width // 2

    def gain_start(stage):
        if stage == 0:
            return [remote(gain_mine.at[0], gain_land.at[0], gain_send.at[0], gain_recv.at[0], sibling)]
        axis = AXES[stage - 1]
        slot = 3 * stage - 2
        return [
            remote(
                gain_mine.at[stage], gain_land.at[slot + n], gain_send.at[slot + n], gain_recv.at[slot + n], device(axis, s)
            )
            for n, s in ((0, 1), (1, -1))
        ]

    def gain_finish(stage, copies):
        total = gain_mine[stage]
        if stage == 0:
            copies[0].wait()
            return total + gain_land[0]
        slot = 3 * stage - 2
        copies[0].wait_recv()
        far = remote(
            gain_land.at[slot], gain_land.at[slot + 2], gain_send.at[slot + 2], gain_recv.at[slot + 2],
            device(AXES[stage - 1], 1),
        )
        copies[0].wait_send()
        copies[1].wait()
        far.wait()
        return total + gain_land[slot] + gain_land[slot + 1] + gain_land[slot + 2]

    def attended_step(s):
        rows = slice(s * PAIR, (s + 1) * PAIR)
        attended = dot(gctx[rows], wout[...]).astype(BF).astype(F32)
        xw_out[rows] = (xw[rows].astype(F32) + attended).astype(BF)

    def grad_step(s):
        rows = slice(s * PAIR, (s + 1) * PAIR)
        grad = dg(proj[rows], win[...], NT).astype(BF).astype(F32)
        standard, inverse = standardised(xw[rows].astype(F32))
        scaled = grad * gain_ref[...]
        first = jnp.mean(scaled, axis=-1, keepdims=True)
        second = jnp.mean(scaled * standard, axis=-1, keepdims=True)
        local = inverse * (scaled - first - standard * second)
        cw[rows] = (cw[rows].astype(F32) + local).astype(BF)
        return jnp.sum(grad * standard, axis=0, keepdims=True)

    def pack_back(number, final):
        both = dot(r1_ref[...], final[PAIR : 2 * PAIR]).astype(BF)
        send_strip[number][0:144] = both[:144]
        send_strip[number][288:384] = both[144:]
        send_strip[number][144:288] = dot(r2_ref[...], final[2 * PAIR :]).astype(BF)
        return send_strips(number, 1)

    def assemble(own, final, strip):
        value = dot(
            imid_ref[...], jnp.concatenate([final[:PAIR], final[2 * PAIR :], strip[144:288]], 0)
        ).astype(BF)
        own[72:360] = value[:288]
        own[504:792] = value[288:]
        value = dot(ibot_ref[...], jnp.concatenate([final[PAIR : 2 * PAIR], strip[288:336]], 0)).astype(BF)
        own[360:432] = value[:72]
        own[792:864] = value[72:]
        value = dot(itop_ref[...], jnp.concatenate([strip[0:144], strip[336:384]], 0)).astype(BF)
        own[0:72] = value[:72]
        own[432:504] = value[72:]

    xw_out = nw

    gather_step(0)
    for load in loads[2:]:
        load.wait()
    mask[0] = jnp.zeros((2, WINT, WINT), F32)
    mask[1] = jnp.where(lat == 3, 1.0, 0.0) * mask_ref[...].reshape(2, WINT, WINT)

    def turn(h, _):
        bias[h] = bias[h].T
        return 0

    lax.fori_loop(0, 16, turn, 0)
    project(0, PAIR)

    def early(p, _):
        unit(0, p, None)
        unit(1, p, None)
        return 0

    lax.fori_loop(0, 8, early, 0)
    for copies in strip_copies:
        for copy in copies:
            copy.wait()
    gather_step(1)
    gather_step(2)
    project(1, 2 * PAIR)

    def turn_rows(n, _):
        at = pl.ds(pl.multiple_of(n * 256, 256), 256)
        nwt[at, :] = nw[:, at].T
        return 0

    lax.fori_loop(0, 4, turn_rows, 0)

    def first_pairs(p, _):
        late_windows(p)
        return 0

    lax.fori_loop(0, 4, first_pairs, 0)
    products(0, 1 - core, sends[0])
    core_0 = start_core(0)
    products(0, core, owns[0])
    late_windows(4)
    end_core(0, core_0)
    ring_start(0, 0)
    late_windows(5)
    ring_relay(0, 0)
    late_windows(6)
    ring_end(0, 0)
    ring_start(0, 1)
    late_windows(7)
    ring_relay(0, 1)
    products(1, 1 - core, sends[1])
    core_1 = start_core(1)
    ring_end(0, 1)
    ring_start(0, 2)
    products(1, core, owns[1])
    ring_relay(0, 2)
    end_core(1, core_1)
    ring_start(1, 0)
    attended_step(1)
    attended_step(2)
    back_out = pack_back(2, xw_out)
    ring_end(0, 2)
    ring_relay(1, 0)
    gain = grad_step(1)
    gain += grad_step(2)
    back_grad = pack_back(3, cw)
    ring_end(1, 0)
    ring_start(1, 1)
    gain += grad_step(0)
    for n in range(8):
        gain_mine[0, n : n + 1, :] = gain[:, n * 128 : (n + 1) * 128]
    gain_copies = gain_start(0)
    ring_relay(1, 1)
    attended_step(0)
    gain_mine[1] = gain_finish(0, gain_copies)
    gain_copies = gain_start(1)
    ring_end(1, 1)
    ring_start(1, 2)
    for copy in back_out:
        copy.wait()
    assemble(own_x, xw_out, recv_strip[2])
    store_out = pltpu.make_async_copy(own_x, out_hbm, load_sem.at[0])
    store_out.start()
    gain_mine[2] = gain_finish(1, gain_copies)
    gain_copies = gain_start(2)
    ring_relay(1, 2)
    gain_mine[3] = gain_finish(2, gain_copies)
    gain_copies = gain_start(3)
    ring_end(1, 2)
    gg_out[...] = gain_finish(3, gain_copies)
    for copy in back_grad:
        copy.wait()
    assemble(own_c, cw, recv_strip[3])
    store_grad = pltpu.make_async_copy(own_c, gt_hbm, load_sem.at[1])
    store_grad.start()
    store_out.wait()
    store_grad.wait()


def block(tokens, cotangent, gain, attention_in, attention_out, head_bias):
    vm = pl.BlockSpec(memory_space=pltpu.VMEM)
    hbm = pl.BlockSpec(memory_space=pl.ANY)
    perms = [jnp.asarray(m, BF) for m in permutations()]
    wide = lambda rows, columns=D: pltpu.VMEM((rows, columns), BF)
    scratch = [wide(OWN) for _ in range(5)]
    scratch += [wide(D, OWN), wide(256, OWN), wide(OWN, 3 * D), wide(OWN), wide(D, 3 * D), wide(D)]
    scratch += [pltpu.VMEM((16, WINT, WINT), F32), pltpu.VMEM((2, 2, WINT, WINT), F32)]
    scratch += [wide(STRIP) for _ in range(8)]
    for _ in range(3):
        for r in range(2):
            scratch += [pltpu.VMEM((2, 2, 4, 4, 16, n), BF) for n in LANES[r]]
    middles = []
    for r in range(2):
        for g in range(3):
            dims = ("zl", "zh", "x", "y")
            a, b = FIRST[r][g], LANES[r][g] - FIRST[r][g]
            for phase in range(3):
                dims = left_dims(dims, ORDERS[g][phase])
                lead = tuple(SIZES[d] for d in dims)
                scratch += [pltpu.VMEM(lead + (16, n), BF) for n in (a, b, a, b, a, b, a, b)]
                if phase < 2:
                    middles.append(pltpu.VMEM(lead + (16, a + b), BF))
    scratch += middles
    scratch += [pltpu.VMEM((4, 8, 128), F32), pltpu.VMEM((10, 8, 128), F32)]
    dma = pltpu.SemaphoreType.DMA
    scratch += [dma((5,)), dma((4, 3)), dma((4, 3)), dma((2, 3)), dma((2, 3))]
    scratch += [dma((2, 3, 3, 6)), dma((2, 3, 3, 6)), dma((10,)), dma((10,))]
    return pl.pallas_call(
        block_kernel,
        in_specs=[hbm, hbm, vm, hbm, hbm, hbm, vm] + [vm] * 9,
        out_specs=[hbm, hbm, vm, vm, vm],
        out_shape=[
            jax.ShapeDtypeStruct((OWN, D), BF),
            jax.ShapeDtypeStruct((OWN, D), BF),
            jax.ShapeDtypeStruct((8, 3 * D), BF),
            jax.ShapeDtypeStruct((8, D), BF),
            jax.ShapeDtypeStruct((8, 128), F32),
        ],
        scratch_shapes=scratch,
        compiler_params=pltpu.CompilerParams(
            collective_id=0, has_side_effects=True, vmem_limit_bytes=63 * 2**20
        ),
    )(
        tokens, cotangent, gain.reshape(1, D), attention_in, attention_out, head_bias,
        jnp.asarray(region_mask()), *perms,
    )


def local(tokens, norm_gain, attention_in, attention_out, head_bias, cotangent):
    shape = tokens.shape
    lat = lax.axis_index("lat")
    lon = lax.axis_index("lon")
    out, gt, gi, go, gains = block(
        tokens.reshape(OWN, D), cotangent.reshape(OWN, D), norm_gain, attention_in, attention_out, head_bias
    )
    gain = lax.dynamic_slice(gains.reshape(1024), ((lat * 32 + lon) * 8,), (8,))
    return out.reshape(shape), gt.reshape(shape), gi, go, gain


def solution(mesh):
    split = P(None, "lat", "lon", None)
    both = ("lat", "lon")
    return jax.shard_map(
        local,
        mesh=mesh,
        in_specs=(split, P(), P(), P(), P(), split),
        out_specs=(split, split, P(both, None), P(both, None), P(both)),
        check_vma=False,
    )
```

```python
import jax
import jax.numpy as jnp
import numpy as np
from jax import lax
from jax.experimental import pallas as pl
from jax.experimental.pallas import tpu as pltpu
from jax.sharding import PartitionSpec as P

D = 1024
WINT = 144
PAIR = 288
OWN = 864
STRIP = 400
NT = (((1,), (1,)), ((), ()))
TN = (((0,), (0,)), ((), ()))
BF = jnp.bfloat16
F32 = jnp.float32

AXES = ("x", "y", "z")
ORDERS = (
    (("x", "y", "z"), ("y", "z", "x"), ("z", "x", "y")),
    (("x", "y", "z"), ("y", "z", "x"), ("z", "x", "y")),
    (("x", "z", "y"), ("z", "x", "y")),
)
PIECES = (
    tuple(("in", 1024 * g, 512) for g in range(3)),
    tuple(("in", 1024 * g + 512, 512) for g in range(3)),
    tuple(("out", 512 * g, 512) for g in range(2)),
)
LANES = 256
FIRST = 128
GROUPS = tuple((r, g) for r in range(3) for g in range(len(ORDERS[r])))
SIZES = {"zl": 2, "zh": 2, "x": 4, "y": 4}


def left_dims(dims, axis):
    gone = ("zl", "zh") if axis == "z" else (axis,)
    return tuple(d for d in dims if d not in gone)


def strip_cells(core):
    cells = [(l, r, c) for l in range(2) for r in range(3) for c in range(24)]
    cells += [(l, r, c) for l in range(2) for r in range(3, 9) for c in range(18, 24)] + [None] * 8
    first = 0 if core else 18
    cells += [(l, r, c) for l in range(2) for r in range(9, 15) for c in range(first, first + 6)] + [None] * 8
    cells += [(l, r, c) for l in range(2) for r in range(15, 18) for c in range(6)] + [None] * 12
    cells += [(l, r, c) for l in range(2) for r in range(3) for c in range(6)] + [None] * 12
    return cells


def received_cells(core):
    cells = []
    for n, cell in enumerate(strip_cells(core)):
        if cell is None:
            cells.append(None)
            continue
        l, r, c = cell
        if n < 144 or n >= 352:
            r += 18
        if n >= 144:
            c += 24 if c < 6 else -24
        cells.append((l, r, c))
    return cells


def window_cells(core):
    corners = ((3, 6), (9, 6), (15, 6), (15, 18), (3, -6), (9, 18 if core else -6))
    return [(l, r + a, c + b) for r, c in corners for l in range(2) for a in range(6) for b in range(12)]


def one_hot(targets, sources):
    place = {}
    for n, cell in enumerate(sources):
        if cell is not None and cell not in place:
            place[cell] = n
    out = np.zeros((len(targets), len(sources)), np.float32)
    for n, cell in enumerate(targets):
        if cell is not None and cell in place:
            out[n, place[cell]] = 1
    return out


def permutations():
    own = [(l, r, c) for l in range(2) for r in range(18) for c in range(24)]
    wide = own[64:368] + own[496:800]
    mid = own[72:360] + own[504:792]
    bottom = own[360:432] + own[792:864]
    top = own[:72] + own[432:504]
    every = []
    for core in range(2):
        strips = strip_cells(core)
        got = received_cells(core)
        win = window_cells(core)
        inner = [c if c is not None and c[2] >= 6 else None for c in strips[:144]]
        every.append(
            (
                one_hot(strips, own),
                one_hot(win[:288], wide),
                one_hot(win[288:576], own[352:432] + own[784:864] + got[:144] + got[304:]),
                one_hot(win[576:], wide + got[144:304]),
                one_hot(got[:144] + got[304:], win[288:576]),
                one_hot(got[144:304], win[576:]),
                one_hot(mid, win[:288] + win[576:] + strips[144:304]),
                one_hot(bottom, win[288:576] + strips[304:352]),
                one_hot(top, inner + strips[352:]),
            )
        )
    return tuple(np.stack(pair) for pair in zip(*every))


def region_mask():
    region = np.array([a < 3 for l in range(2) for a in range(6) for b in range(12)])
    one = np.where(region[:, None] == region[None, :], 0.0, -1e9).astype(np.float32)
    return np.concatenate([one, one], 0)


def dg(a, b, dims):
    return lax.dot_general(a, b, dims, preferred_element_type=F32)


def dot(a, b):
    return jnp.dot(a, b, preferred_element_type=F32)


def mesh_place(core, x, y, z):
    return ((z % 2) * 2 + core, (z // 2) * 16 + x * 4 + y)


def block_kernel(
    tok_hbm, cot_hbm, gain_ref, win_hbm, wout_hbm, hb_hbm, mask_ref,
    pack_hbm, p0_hbm, p1_hbm, p2_hbm, r1_hbm, r2_hbm, imid_hbm, ibot_hbm, itop_hbm,
    out_hbm, gt_hbm, gi_out, go_out, gg_out,
    *scratch,
):
    scratch = list(scratch)

    def take(count):
        out = scratch[:count]
        del scratch[:count]
        return out

    own_x, own_c, xw, cw, nw, nwt, proj, gctx, win, wout, bias, mask = take(12)
    perms = take(9)
    pack_ref, p0_ref, p1_ref, p2_ref, r1_ref, r2_ref, imid_ref, ibot_ref, itop_ref = perms
    send_strip, recv_strip = take(4), take(4)
    sends = {at: take(1)[0] for at in GROUPS}
    owns = {at: take(1)[0] for at in GROUPS}
    halves = {at: take(1)[0] for at in GROUPS}
    landing = {(r, g, p): take(8) for r, g in GROUPS for p in range(3)}
    middles = {(r, g, p): take(1)[0] for r, g in GROUPS for p in range(2)}
    gain_mine, gain_land = take(2)
    load_sem, strip_send, strip_recv, core_send, core_recv = take(5)
    ring_send, ring_recv, gain_send, gain_recv = take(4)

    lat = lax.axis_index("lat")
    lon = lax.axis_index("lon")
    core = lat % 2
    me = {"x": (lon // 4) % 4, "y": lon % 4, "z": (lon // 16) * 2 + lat // 2}

    def device(axis, step):
        at = dict(me)
        at[axis] = (me[axis] + step + 4) % 4
        return mesh_place(core, at["x"], at["y"], at["z"])

    sibling = mesh_place(1 - core, me["x"], me["y"], me["z"])

    def grid_place(a, b):
        return ((lat + a + 4) % 4, (lon + b + 32) % 32)

    loads = [
        pltpu.make_async_copy(src, dst, load_sem.at[n])
        for n, (src, dst) in enumerate(
            (
                (tok_hbm, own_x), (pack_hbm.at[core], pack_ref), (cot_hbm, own_c), (p0_hbm.at[core], p0_ref),
                (win_hbm, win), (wout_hbm, wout), (hb_hbm, bias), (p1_hbm.at[core], p1_ref), (p2_hbm.at[core], p2_ref),
                (r1_hbm.at[core], r1_ref), (r2_hbm.at[core], r2_ref), (imid_hbm.at[core], imid_ref),
                (ibot_hbm.at[core], ibot_ref), (itop_hbm.at[core], itop_ref),
            )
        )
    ]
    for load in loads:
        load.start()

    barrier = pltpu.get_barrier_semaphore()
    partners = [sibling] + [device(a, s) for a in AXES for s in (1, -1, 2)]
    partners += [grid_place(s * a, s * b) for a, b in ((1, 0), (0, 1), (1, 1)) for s in (1, -1)]
    for other in partners:
        pl.semaphore_signal(barrier, inc=1, device_id=other, device_id_type=pl.DeviceIdType.MESH)
    pl.semaphore_wait(barrier, len(partners))

    def remote(src, dst, send, recv, place):
        copy = pltpu.make_async_remote_copy(
            src_ref=src,
            dst_ref=dst,
            send_sem=send,
            recv_sem=recv,
            device_id=place,
            device_id_type=pl.DeviceIdType.MESH,
        )
        copy.start()
        return copy

    turned = jnp.where(core == 0, 1, -1)
    PARTS = ((0, 144, -1, 0), (144, 80, 0, 1), (224, 80, 0, turned), (304, 48, 0, -1), (352, 48, -1, -1))

    def send_strips(number, way, parts=range(5)):
        copies = []
        for part in parts:
            low, size, a, b = PARTS[part]
            copies.append(
                remote(
                    send_strip[number].at[pl.ds(low, size)],
                    recv_strip[number].at[pl.ds(low, size)],
                    strip_send.at[number, part],
                    strip_recv.at[number, part],
                    grid_place(way * a, way * b),
                )
            )
        return copies

    strip_copies = []
    loads[0].wait()
    loads[1].wait()
    for number, own in ((0, own_x), (1, own_c)):
        if number == 1:
            loads[2].wait()
        send_strip[number][...] = dot(pack_ref[...], own[...]).astype(BF)
        strip_copies.append(send_strips(number, 1))

    def gathered(own, strip, s):
        if s == 1:
            parts = [own[352:432], own[784:864], strip[0:144], strip[304:400]]
            return dot(p1_ref[...], jnp.concatenate(parts, 0))
        parts = [own[64:368], own[496:800]]
        if s == 0:
            return dot(p0_ref[...], jnp.concatenate(parts, 0))
        return dot(p2_ref[...], jnp.concatenate(parts + [strip[144:304]], 0))

    def standardised(x):
        centred = x - jnp.mean(x, axis=-1, keepdims=True)
        inverse = lax.rsqrt(jnp.mean(centred * centred, axis=-1, keepdims=True) + 1e-5)
        return centred * inverse, inverse

    def gather_tokens(s):
        rows = slice(s * PAIR, (s + 1) * PAIR)
        x = gathered(own_x, recv_strip[0], s)
        xw[rows] = x.astype(BF)
        standard, _ = standardised(x)
        nw[rows] = (standard * gain_ref[...]).astype(BF)

    def gather_cotangent(s):
        rows = slice(s * PAIR, (s + 1) * PAIR)
        cw[rows] = gathered(own_c, recv_strip[1], s).astype(BF)

    def project(s, count):
        rows = slice(s * PAIR, s * PAIR + count)

        def columns(n, _):
            at = pl.ds(pl.multiple_of(n * 512, 512), 512)
            value = dot(nw[rows], win[:, at])
            proj[rows, at] = (value * jnp.where(n < 2, 0.125, 1.0)).astype(BF)
            return 0

        lax.fori_loop(0, 6, columns, 0)

    def project_back(s, count):
        rows = slice(s * PAIR, s * PAIR + count)

        def outer(n, _):
            at = pl.ds(pl.multiple_of(n * 512, 512), 512)
            gctx[rows, at] = dg(cw[rows], wout[at, :], NT).astype(BF)
            return 0

        lax.fori_loop(0, 2, outer, 0)

    low_half = lax.broadcasted_iota(jnp.int32, (WINT, 128), 1) < 64
    zero = jnp.zeros((WINT, 128), BF)

    def unit(w, p, masked):
        rows = pl.ds(pl.multiple_of(w * WINT, 16), WINT)
        at_q = pl.ds(pl.multiple_of(p * 128, 128), 128)
        at_k = pl.ds(pl.multiple_of(1024 + p * 128, 128), 128)
        at_v = pl.ds(pl.multiple_of(2048 + p * 128, 128), 128)
        q, k, v, d = proj[rows, at_q], proj[rows, at_k], proj[rows, at_v], gctx[rows, at_q]
        ks = jnp.concatenate([jnp.where(low_half, k, zero), jnp.where(low_half, zero, k)], 0)
        vs = jnp.concatenate([jnp.where(low_half, v, zero), jnp.where(low_half, zero, v)], 0)
        offset = bias[pl.ds(2 * p, 2)]
        if masked is not None:
            offset = offset + mask[masked]
        st = dg(ks, q, NT).reshape(2, WINT, WINT) + offset
        powers = jnp.exp(st - jnp.max(st, axis=1, keepdims=True))
        weights = powers * (1.0 / jnp.sum(powers, axis=1, keepdims=True))
        wb = weights.astype(BF).reshape(PAIR, WINT)
        gctx[rows, at_q] = dg(wb, vs, TN).astype(BF)
        dw = dg(vs, d, NT).reshape(2, WINT, WINT)
        inner = jnp.sum(dw * weights, axis=1, keepdims=True)
        ds = (weights * (dw - inner)).astype(BF).reshape(PAIR, WINT)
        gv = dot(wb, d)
        gk = dot(ds, q)
        proj[rows, at_q] = (dg(ds, ks, TN) * 0.125).astype(BF)
        proj[rows, at_k] = jnp.where(low_half, gk[:WINT], gk[WINT:]).astype(BF)
        proj[rows, at_v] = jnp.where(low_half, gv[:WINT], gv[WINT:]).astype(BF)

    def late_windows(p):
        def two(t, _):
            masked = jnp.where(t == 0, 1, 0)
            unit(2 + 2 * t, p, masked)
            unit(3 + 2 * t, p, masked)
            return 0

        lax.fori_loop(0, 2, two, 0)

    def products(rnd, g, half, target):
        kind, first, width = PIECES[rnd][g]
        right = proj if kind == "in" else cw

        def rows_of(zl, _):
            at = pl.multiple_of(zl * 512 + half * 256, 256)
            value = dot(nwt[pl.ds(at, 256), :], right[:, first : first + width]).reshape(32, 8, width)
            both = jnp.concatenate([value[:, :, :LANES], value[:, :, LANES:]], 1)
            target[zl] = both.astype(BF).reshape(2, 4, 4, 16, LANES)
            return 0

        lax.fori_loop(0, 2, rows_of, 0)

    core_copies = {}

    def start_round(rnd):
        for g in range(len(ORDERS[rnd])):
            products(rnd, g, 1 - core, sends[rnd, g])
            core_copies[rnd, g] = remote(
                sends[rnd, g], halves[rnd, g], core_send.at[rnd, g], core_recv.at[rnd, g], sibling
            )

    def own_products(rnd):
        for g in range(len(ORDERS[rnd])):
            products(rnd, g, core, owns[rnd, g])

    def end_core(rnd):
        for g in range(len(ORDERS[rnd])):
            core_copies[rnd, g].wait()
            mine = owns[rnd, g]
            mine[...] = (mine[...].astype(F32) + halves[rnd, g][...].astype(F32)).astype(BF)
            ring_start_group(rnd, g, 0)

    def source(rnd, g, phase):
        dims = ("zl", "zh", "x", "y")
        for axis in ORDERS[rnd][g][:phase]:
            dims = left_dims(dims, axis)
        return (owns[rnd, g] if phase == 0 else middles[rnd, g, phase - 1]), dims

    def chunk(rnd, g, phase, step, half):
        ref, dims = source(rnd, g, phase)
        axis = ORDERS[rnd][g][phase]
        t = (me[axis] + step + 4) % 4
        end = pl.ds(half * FIRST, FIRST)
        place = []
        for dim in dims:
            if dim == axis:
                place.append(t)
            elif axis == "z" and dim == "zl":
                place.append(t % 2)
            elif axis == "z" and dim == "zh":
                place.append(t // 2)
            else:
                place.append(slice(None))
        return ref.at[tuple(place) + (slice(None), end)]

    def ring(rnd, g, phase, number, src, step):
        return remote(
            src,
            landing[rnd, g, phase][number],
            ring_send.at[rnd, g, phase, number],
            ring_recv.at[rnd, g, phase, number],
            device(ORDERS[rnd][g][phase], step),
        )

    flying = {}

    def ring_start_group(rnd, g, phase):
        flying[rnd, g] = {
            0: ring(rnd, g, phase, 0, chunk(rnd, g, phase, 2, 0), 1),
            3: ring(rnd, g, phase, 3, chunk(rnd, g, phase, 2, 1), -1),
            1: ring(rnd, g, phase, 1, chunk(rnd, g, phase, 1, 1), 1),
            4: ring(rnd, g, phase, 4, chunk(rnd, g, phase, -1, 0), -1),
        }

    def ring_relay(rnd, phase):
        for g in range(len(ORDERS[rnd])):
            land = landing[rnd, g, phase]
            for number, step, half, slot in ((0, 1, 0, 6), (3, -1, 1, 7)):
                flying[rnd, g][number].wait_recv()
                land[slot][...] = (
                    land[number][...].astype(F32) + chunk(rnd, g, phase, step, half)[...].astype(F32)
                ).astype(BF)
                flying[rnd, g][number + 2] = ring(rnd, g, phase, number + 2, land[slot], step)

    def ring_end(rnd, phase):
        for g in range(len(ORDERS[rnd])):
            land = landing[rnd, g, phase]
            copies = flying[rnd, g]
            for number in (1, 4, 2, 5):
                copies[number].wait()
            copies[0].wait_send()
            copies[3].wait_send()
            for half, near, far in ((0, 4, 2), (1, 1, 5)):
                value = (
                    chunk(rnd, g, phase, 0, half)[...].astype(F32)
                    + land[near][...].astype(F32)
                    + land[far][...].astype(F32)
                ).astype(BF)
                start = half * FIRST
                if phase < 2:
                    middles[rnd, g, phase][..., start : start + FIRST] = value
                    continue
                kind, first, _ = PIECES[rnd][g]
                target = gi_out if kind == "in" else go_out
                target[:, first + start : first + start + FIRST] = value[:8]
                target[:, first + LANES + start : first + LANES + start + FIRST] = value[8:]
            if phase < 2:
                ring_start_group(rnd, g, phase + 1)

    def gain_start(stage):
        if stage == 0:
            return [remote(gain_mine.at[0], gain_land.at[0], gain_send.at[0], gain_recv.at[0], sibling)]
        return [
            remote(
                gain_mine.at[stage],
                gain_land.at[3 * stage - 2 + n],
                gain_send.at[3 * stage - 2 + n],
                gain_recv.at[3 * stage - 2 + n],
                device(AXES[stage - 1], n + 1),
            )
            for n in range(3)
        ]

    def gain_finish(stage, copies):
        total = gain_mine[stage]
        for copy in copies:
            copy.wait()
        if stage == 0:
            return total + gain_land[0]
        slot = 3 * stage - 2
        return total + gain_land[slot] + gain_land[slot + 1] + gain_land[slot + 2]

    def attended_step(s):
        rows = slice(s * PAIR, (s + 1) * PAIR)
        attended = dot(gctx[rows], wout[...]).astype(BF).astype(F32)
        xw_out[rows] = (xw[rows].astype(F32) + attended).astype(BF)

    def grad_step(s):
        rows = slice(s * PAIR, (s + 1) * PAIR)
        grad = dg(proj[rows], win[...], NT).astype(BF).astype(F32)
        standard, inverse = standardised(xw[rows].astype(F32))
        scaled = grad * gain_ref[...]
        first = jnp.mean(scaled, axis=-1, keepdims=True)
        second = jnp.mean(scaled * standard, axis=-1, keepdims=True)
        local = inverse * (scaled - first - standard * second)
        cw[rows] = (cw[rows].astype(F32) + local).astype(BF)
        return jnp.sum(grad * standard, axis=0, keepdims=True)

    def pack_back(number, final):
        both = dot(r1_ref[...], final[PAIR : 2 * PAIR]).astype(BF)
        send_strip[number][0:144] = both[:144]
        send_strip[number][304:400] = both[144:]
        send_strip[number][144:304] = dot(r2_ref[...], final[2 * PAIR :]).astype(BF)
        return send_strips(number, -1)

    def assemble(own, final, strip):
        value = dot(
            imid_ref[...], jnp.concatenate([final[:PAIR], final[2 * PAIR :], strip[144:304]], 0)
        ).astype(BF)
        own[72:360] = value[:288]
        own[504:792] = value[288:]
        value = dot(ibot_ref[...], jnp.concatenate([final[PAIR : 2 * PAIR], strip[304:352]], 0)).astype(BF)
        own[360:432] = value[:72]
        own[792:864] = value[72:]
        value = dot(itop_ref[...], jnp.concatenate([strip[0:144], strip[352:400]], 0)).astype(BF)
        own[0:72] = value[:72]
        own[432:504] = value[72:]

    xw_out = nw

    loads[3].wait()
    gather_tokens(0)
    gather_cotangent(0)
    for load in loads[4:]:
        load.wait()
    mask[0] = jnp.zeros((2, WINT, WINT), F32)
    mask[1] = jnp.where(lat == 3, 1.0, 0.0) * mask_ref[...].reshape(2, WINT, WINT)

    def turn(h, _):
        bias[h] = bias[h].T
        return 0

    lax.fori_loop(0, 16, turn, 0)
    project(0, PAIR)
    project_back(0, PAIR)

    def early(p, _):
        unit(0, p, None)
        unit(1, p, None)
        return 0

    lax.fori_loop(0, 8, early, 0)
    for copy in strip_copies[0]:
        copy.wait()
    gather_tokens(1)
    gather_tokens(2)
    project(1, 2 * PAIR)

    def turn_rows(n, _):
        at = pl.ds(pl.multiple_of(n * 256, 256), 256)
        nwt[at, :] = nw[:, at].T
        return 0

    lax.fori_loop(0, 4, turn_rows, 0)
    for copy in strip_copies[1]:
        copy.wait()
    gather_cotangent(1)
    gather_cotangent(2)
    project_back(1, 2 * PAIR)

    def first_pairs(p, _):
        late_windows(p)
        return 0

    lax.fori_loop(0, 4, first_pairs, 0)
    start_round(0)
    own_products(0)
    late_windows(4)
    end_core(0)
    late_windows(5)
    ring_relay(0, 0)
    late_windows(6)
    ring_end(0, 0)
    late_windows(7)
    ring_relay(0, 1)
    start_round(1)
    ring_end(0, 1)
    own_products(1)
    ring_relay(0, 2)
    attended_step(1)
    attended_step(2)
    back_out = pack_back(2, xw_out)
    end_core(1)

    def turn_context(n, _):
        at = pl.ds(pl.multiple_of(n * 256, 256), 256)
        nwt[at, :] = gctx[:, at].T
        return 0

    lax.fori_loop(0, 4, turn_context, 0)
    start_round(2)
    own_products(2)
    gain = grad_step(1)
    ring_relay(1, 0)
    gain += grad_step(2)
    back_grad = pack_back(3, cw)
    end_core(2)
    gain += grad_step(0)
    for n in range(8):
        gain_mine[0, n : n + 1, :] = gain[:, n * 128 : (n + 1) * 128]
    gain_copies = gain_start(0)
    ring_end(1, 0)
    ring_relay(2, 0)
    attended_step(0)
    ring_end(0, 2)
    gain_mine[1] = gain_finish(0, gain_copies)
    gain_copies = gain_start(1)
    ring_relay(1, 1)
    ring_end(2, 0)
    for copy in back_out:
        copy.wait()
    assemble(own_x, xw_out, recv_strip[2])
    store_out = pltpu.make_async_copy(own_x, out_hbm, load_sem.at[0])
    store_out.start()
    gain_mine[2] = gain_finish(1, gain_copies)
    gain_copies = gain_start(2)
    ring_end(1, 1)
    ring_relay(2, 1)
    gain_mine[3] = gain_finish(2, gain_copies)
    gain_copies = gain_start(3)
    ring_relay(1, 2)
    ring_end(2, 1)
    for copy in back_grad:
        copy.wait()
    assemble(own_c, cw, recv_strip[3])
    store_grad = pltpu.make_async_copy(own_c, gt_hbm, load_sem.at[1])
    store_grad.start()
    ring_relay(2, 2)
    gg_out[...] = gain_finish(3, gain_copies)
    ring_end(1, 2)
    ring_end(2, 2)
    store_out.wait()
    store_grad.wait()


def block(tokens, cotangent, gain, attention_in, attention_out, head_bias):
    vm = pl.BlockSpec(memory_space=pltpu.VMEM)
    hbm = pl.BlockSpec(memory_space=pl.ANY)
    perms = [jnp.asarray(m, BF) for m in permutations()]
    wide = lambda rows, columns=D: pltpu.VMEM((rows, columns), BF)
    scratch = [wide(OWN) for _ in range(5)]
    scratch += [wide(D, OWN), wide(OWN, 3 * D), wide(OWN), wide(D, 3 * D), wide(D)]
    scratch += [pltpu.VMEM((16, WINT, WINT), F32), pltpu.VMEM((2, 2, WINT, WINT), F32)]
    scratch += [wide(*m.shape[1:]) for m in perms]
    scratch += [wide(STRIP) for _ in range(8)]
    scratch += [pltpu.VMEM((2, 2, 4, 4, 16, LANES), BF) for _ in range(3 * len(GROUPS))]
    middles = []
    for r, g in GROUPS:
        dims = ("zl", "zh", "x", "y")
        for phase in range(3):
            dims = left_dims(dims, ORDERS[r][g][phase])
            lead = tuple(SIZES[d] for d in dims)
            scratch += [pltpu.VMEM(lead + (16, FIRST), BF) for _ in range(8)]
            if phase < 2:
                middles.append(pltpu.VMEM(lead + (16, LANES), BF))
    scratch += middles
    scratch += [pltpu.VMEM((4, 8, 128), F32), pltpu.VMEM((10, 8, 128), F32)]
    dma = pltpu.SemaphoreType.DMA
    scratch += [dma((14,)), dma((4, 5)), dma((4, 5)), dma((3, 3)), dma((3, 3))]
    scratch += [dma((3, 3, 3, 6)), dma((3, 3, 3, 6)), dma((10,)), dma((10,))]
    return pl.pallas_call(
        block_kernel,
        in_specs=[hbm, hbm, vm, hbm, hbm, hbm, vm] + [hbm] * 9,
        out_specs=[hbm, hbm, vm, vm, vm],
        out_shape=[
            jax.ShapeDtypeStruct((OWN, D), BF),
            jax.ShapeDtypeStruct((OWN, D), BF),
            jax.ShapeDtypeStruct((8, 3 * D), BF),
            jax.ShapeDtypeStruct((8, D), BF),
            jax.ShapeDtypeStruct((8, 128), F32),
        ],
        scratch_shapes=scratch,
        compiler_params=pltpu.CompilerParams(
            collective_id=0, has_side_effects=True, vmem_limit_bytes=63 * 2**20
        ),
    )(
        tokens, cotangent, gain.reshape(1, D), attention_in, attention_out, head_bias,
        jnp.asarray(region_mask()), *perms,
    )


def local(tokens, norm_gain, attention_in, attention_out, head_bias, cotangent):
    shape = tokens.shape
    lat = lax.axis_index("lat")
    lon = lax.axis_index("lon")
    out, gt, gi, go, gains = block(
        tokens.reshape(OWN, D), cotangent.reshape(OWN, D), norm_gain, attention_in, attention_out, head_bias
    )
    gain = lax.dynamic_slice(gains.reshape(1024), ((lat * 32 + lon) * 8,), (8,))
    return out.reshape(shape), gt.reshape(shape), gi, go, gain


def solution(mesh):
    split = P(None, "lat", "lon", None)
    both = ("lat", "lon")
    return jax.shard_map(
        local,
        mesh=mesh,
        in_specs=(split, P(), P(), P(), P(), split),
        out_specs=(split, split, P(both, None), P(both, None), P(both)),
        check_vma=False,
    )
```

```python
import jax
import jax.numpy as jnp
import numpy as np
from jax import lax
from jax.experimental import pallas as pl
from jax.experimental.pallas import tpu as pltpu
from jax.sharding import PartitionSpec as P

D = 1024
WINT = 144
PAIR = 288
OWN = 864
STRIP = 400
NT = (((1,), (1,)), ((), ()))
TN = (((0,), (0,)), ((), ()))
BF = jnp.bfloat16
F32 = jnp.float32

AXES = ("x", "y", "z")
ORDERS = (
    (("x", "y", "z"), ("y", "z", "x"), ("z", "x", "y")),
    (("x", "y", "z"), ("y", "z", "x"), ("z", "x", "y")),
    (("x", "z", "y"), ("z", "x", "y")),
)
PIECES = (
    tuple(("in", 1024 * g, 512) for g in range(3)),
    tuple(("in", 1024 * g + 512, 512) for g in range(3)),
    tuple(("out", 512 * g, 512) for g in range(2)),
)
LANES = 256
FIRST = 128
GROUPS = tuple((r, g) for r in range(3) for g in range(len(ORDERS[r])))


def strip_cells(core):
    cells = [(l, r, c) for l in range(2) for r in range(3) for c in range(24)]
    cells += [(l, r, c) for l in range(2) for r in range(3, 9) for c in range(18, 24)] + [None] * 8
    first = 0 if core else 18
    cells += [(l, r, c) for l in range(2) for r in range(9, 15) for c in range(first, first + 6)] + [None] * 8
    cells += [(l, r, c) for l in range(2) for r in range(15, 18) for c in range(6)] + [None] * 12
    cells += [(l, r, c) for l in range(2) for r in range(3) for c in range(6)] + [None] * 12
    return cells


def received_cells(core):
    cells = []
    for n, cell in enumerate(strip_cells(core)):
        if cell is None:
            cells.append(None)
            continue
        l, r, c = cell
        if n < 144 or n >= 352:
            r += 18
        if n >= 144:
            c += 24 if c < 6 else -24
        cells.append((l, r, c))
    return cells


def window_cells(core):
    corners = ((3, 6), (9, 6), (15, 6), (15, 18), (3, -6), (9, 18 if core else -6))
    return [(l, r + a, c + b) for r, c in corners for l in range(2) for a in range(6) for b in range(12)]


def one_hot(targets, sources):
    place = {}
    for n, cell in enumerate(sources):
        if cell is not None and cell not in place:
            place[cell] = n
    out = np.zeros((len(targets), len(sources)), np.float32)
    for n, cell in enumerate(targets):
        if cell is not None and cell in place:
            out[n, place[cell]] = 1
    return out


def permutations():
    own = [(l, r, c) for l in range(2) for r in range(18) for c in range(24)]
    wide = own[64:368] + own[496:800]
    mid = own[72:360] + own[504:792]
    bottom = own[360:432] + own[792:864]
    top = own[:72] + own[432:504]
    every = []
    for core in range(2):
        strips = strip_cells(core)
        got = received_cells(core)
        win = window_cells(core)
        inner = [c if c is not None and c[2] >= 6 else None for c in strips[:144]]
        every.append(
            (
                one_hot(strips, own),
                one_hot(win[:288], wide),
                one_hot(win[288:576], own[352:432] + own[784:864] + got[:144] + got[304:]),
                one_hot(win[576:], wide + got[144:304]),
                one_hot(got[:144] + got[304:], win[288:576]),
                one_hot(got[144:304], win[576:]),
                one_hot(mid, win[:288] + win[576:] + strips[144:304]),
                one_hot(bottom, win[288:576] + strips[304:352]),
                one_hot(top, inner + strips[352:]),
            )
        )
    return tuple(np.stack(pair) for pair in zip(*every))


def region_mask():
    region = np.array([a < 3 for l in range(2) for a in range(6) for b in range(12)])
    one = np.where(region[:, None] == region[None, :], 0.0, -1e9).astype(np.float32)
    return np.concatenate([one, one], 0)


def dg(a, b, dims):
    return lax.dot_general(a, b, dims, preferred_element_type=F32)


def dot(a, b):
    return jnp.dot(a, b, preferred_element_type=F32)


def mesh_place(core, x, y, z):
    return ((z % 2) * 2 + core, (z // 2) * 16 + x * 4 + y)


def block_kernel(
    tok_hbm, cot_hbm, gain_ref, win_hbm, wout_hbm, hb_hbm, mask_ref,
    pack_hbm, p0_hbm, p1_hbm, p2_hbm, r1_hbm, r2_hbm, imid_hbm, ibot_hbm, itop_hbm,
    out_hbm, gt_hbm, gi_out, go_out, gg_out,
    *scratch,
):
    scratch = list(scratch)

    def take(count):
        out = scratch[:count]
        del scratch[:count]
        return out

    own_x, own_c, xw, cw, nw, nwt, ctxt, proj, gctx, win, wout, bias, mask = take(13)
    perms = take(9)
    pack_ref, p0_ref, p1_ref, p2_ref, r1_ref, r2_ref, imid_ref, ibot_ref, itop_ref = perms
    send_strip, recv_strip = take(4), take(4)
    sends = {at: take(1)[0] for at in GROUPS}
    owns = {at: take(1)[0] for at in GROUPS}
    halves = {at: take(1)[0] for at in GROUPS}
    landing = {(r, g, p): take(8) for r, g in GROUPS for p in range(3)}
    middles = {(r, g, p): take(1)[0] for r, g in GROUPS for p in range(2)}
    gain_mine, gain_land = take(2)
    load_sem, strip_send, strip_recv, core_send, core_recv = take(5)
    ring_send, ring_recv, gain_send, gain_recv = take(4)

    lat = lax.axis_index("lat")
    lon = lax.axis_index("lon")
    core = lat % 2
    me = {"x": (lon // 4) % 4, "y": lon % 4, "z": (lon // 16) * 2 + lat // 2}

    def device(axis, step):
        at = dict(me)
        at[axis] = (me[axis] + step + 4) % 4
        return mesh_place(core, at["x"], at["y"], at["z"])

    sibling = mesh_place(1 - core, me["x"], me["y"], me["z"])

    def grid_place(a, b):
        return ((lat + a + 4) % 4, (lon + b + 32) % 32)

    loads = [
        pltpu.make_async_copy(src, dst, load_sem.at[n])
        for n, (src, dst) in enumerate(
            (
                (tok_hbm, own_x), (pack_hbm.at[core], pack_ref), (cot_hbm, own_c), (p0_hbm.at[core], p0_ref),
                (win_hbm, win), (wout_hbm, wout), (hb_hbm, bias), (p1_hbm.at[core], p1_ref), (p2_hbm.at[core], p2_ref),
                (r1_hbm.at[core], r1_ref), (r2_hbm.at[core], r2_ref), (imid_hbm.at[core], imid_ref),
                (ibot_hbm.at[core], ibot_ref), (itop_hbm.at[core], itop_ref),
            )
        )
    ]
    for load in loads:
        load.start()

    barrier = pltpu.get_barrier_semaphore()
    partners = [sibling] + [device(a, s) for a in AXES for s in (1, -1, 2)]
    partners += [grid_place(s * a, s * b) for a, b in ((1, 0), (0, 1), (1, 1)) for s in (1, -1)]
    for other in partners:
        pl.semaphore_signal(barrier, inc=1, device_id=other, device_id_type=pl.DeviceIdType.MESH)
    pl.semaphore_wait(barrier, len(partners))

    def remote(src, dst, send, recv, place):
        copy = pltpu.make_async_remote_copy(
            src_ref=src,
            dst_ref=dst,
            send_sem=send,
            recv_sem=recv,
            device_id=place,
            device_id_type=pl.DeviceIdType.MESH,
        )
        copy.start()
        return copy

    turned = jnp.where(core == 0, 1, -1)
    PARTS = ((0, 144, -1, 0), (144, 80, 0, 1), (224, 80, 0, turned), (304, 48, 0, -1), (352, 48, -1, -1))

    def send_strips(number, way, parts=range(5)):
        copies = []
        for part in parts:
            low, size, a, b = PARTS[part]
            copies.append(
                remote(
                    send_strip[number].at[pl.ds(low, size)],
                    recv_strip[number].at[pl.ds(low, size)],
                    strip_send.at[number, part],
                    strip_recv.at[number, part],
                    grid_place(way * a, way * b),
                )
            )
        return copies

    strip_copies = []
    loads[0].wait()
    loads[1].wait()
    for number, own in ((0, own_x), (1, own_c)):
        if number == 1:
            loads[2].wait()
        send_strip[number][...] = dot(pack_ref[...], own[...]).astype(BF)
        strip_copies.append(send_strips(number, 1))

    def gathered(own, strip, s):
        if s == 1:
            parts = [own[352:432], own[784:864], strip[0:144], strip[304:400]]
            return dot(p1_ref[...], jnp.concatenate(parts, 0))
        parts = [own[64:368], own[496:800]]
        if s == 0:
            return dot(p0_ref[...], jnp.concatenate(parts, 0))
        return dot(p2_ref[...], jnp.concatenate(parts + [strip[144:304]], 0))

    def standardised(x):
        centred = x - jnp.mean(x, axis=-1, keepdims=True)
        inverse = lax.rsqrt(jnp.mean(centred * centred, axis=-1, keepdims=True) + 1e-5)
        return centred * inverse, inverse

    def gather_tokens(s):
        rows = slice(s * PAIR, (s + 1) * PAIR)
        x = gathered(own_x, recv_strip[0], s)
        xw[rows] = x.astype(BF)
        standard, _ = standardised(x)
        nw[rows] = (standard * gain_ref[...]).astype(BF)

    def gather_cotangent(s):
        rows = slice(s * PAIR, (s + 1) * PAIR)
        cw[rows] = gathered(own_c, recv_strip[1], s).astype(BF)

    def project(s, count):
        rows = slice(s * PAIR, s * PAIR + count)

        def columns(n, _):
            at = pl.ds(pl.multiple_of(n * 512, 512), 512)
            value = dot(nw[rows], win[:, at])
            proj[rows, at] = (value * jnp.where(n < 2, 0.125, 1.0)).astype(BF)
            return 0

        lax.fori_loop(0, 6, columns, 0)

    def project_back(s, count):
        rows = slice(s * PAIR, s * PAIR + count)

        def outer(n, _):
            at = pl.ds(pl.multiple_of(n * 512, 512), 512)
            gctx[rows, at] = dg(cw[rows], wout[at, :], NT).astype(BF)
            return 0

        lax.fori_loop(0, 2, outer, 0)

    low_half = lax.broadcasted_iota(jnp.int32, (WINT, 128), 1) < 64
    zero = jnp.zeros((WINT, 128), BF)

    def unit(w, p, masked):
        rows = pl.ds(pl.multiple_of(w * WINT, 16), WINT)
        at_q = pl.ds(pl.multiple_of(p * 128, 128), 128)
        at_k = pl.ds(pl.multiple_of(1024 + p * 128, 128), 128)
        at_v = pl.ds(pl.multiple_of(2048 + p * 128, 128), 128)
        q, k, v, d = proj[rows, at_q], proj[rows, at_k], proj[rows, at_v], gctx[rows, at_q]
        ks = jnp.concatenate([jnp.where(low_half, k, zero), jnp.where(low_half, zero, k)], 0)
        vs = jnp.concatenate([jnp.where(low_half, v, zero), jnp.where(low_half, zero, v)], 0)
        offset = bias[pl.ds(2 * p, 2)]
        if masked is not None:
            offset = offset + mask[masked]
        st = dg(ks, q, NT).reshape(2, WINT, WINT) + offset
        powers = jnp.exp(st - jnp.max(st, axis=1, keepdims=True))
        weights = powers * (1.0 / jnp.sum(powers, axis=1, keepdims=True))
        wb = weights.astype(BF).reshape(PAIR, WINT)
        gctx[rows, at_q] = dg(wb, vs, TN).astype(BF)
        dw = dg(vs, d, NT).reshape(2, WINT, WINT)
        inner = jnp.sum(dw * weights, axis=1, keepdims=True)
        ds = (weights * (dw - inner)).astype(BF).reshape(PAIR, WINT)
        gv = dot(wb, d)
        gk = dot(ds, q)
        proj[rows, at_q] = (dg(ds, ks, TN) * 0.125).astype(BF)
        proj[rows, at_k] = jnp.where(low_half, gk[:WINT], gk[WINT:]).astype(BF)
        proj[rows, at_v] = jnp.where(low_half, gv[:WINT], gv[WINT:]).astype(BF)

    def late_windows(p):
        def two(t, _):
            masked = jnp.where(t == 0, 1, 0)
            unit(2 + 2 * t, p, masked)
            unit(3 + 2 * t, p, masked)
            return 0

        lax.fori_loop(0, 2, two, 0)

    def products(rnd, g, half, target):
        kind, first, width = PIECES[rnd][g]
        right = proj if kind == "in" else cw

        order = ORDERS[rnd][g]
        left = nwt if kind == "in" else ctxt

        def rows_of(zl, _):
            at = pl.multiple_of(zl * 512 + half * 256, 256)
            value = dot(left[pl.ds(at, 256), :], right[:, first : first + width]).reshape(32, 8, width)
            both = jnp.concatenate([value[:, :, :LANES], value[:, :, LANES:]], 1).astype(BF)
            both = both.reshape(2, 4, 4, 16, LANES)
            for zh in range(2):
                z = 2 * zh + zl
                for end in range(2):
                    part = both[zh, :, :, :, end * FIRST : (end + 1) * FIRST]
                    if order.index("y") < order.index("x"):
                        part = jnp.swapaxes(part, 0, 1)
                    place = [end, slice(None), slice(None), slice(None)]
                    place[1 + order.index("z")] = z
                    target[tuple(place)] = part
            return 0

        lax.fori_loop(0, 2, rows_of, 0)

    core_copies = {}

    def start_round(rnd):
        for g in range(len(ORDERS[rnd])):
            products(rnd, g, 1 - core, sends[rnd, g])
            core_copies[rnd, g] = remote(
                sends[rnd, g], halves[rnd, g], core_send.at[rnd, g], core_recv.at[rnd, g], sibling
            )

    def own_products(rnd):
        for g in range(len(ORDERS[rnd])):
            products(rnd, g, core, owns[rnd, g])

    def end_core(rnd):
        for g in range(len(ORDERS[rnd])):
            core_copies[rnd, g].wait()
            mine = owns[rnd, g]
            mine[...] = (mine[...].astype(F32) + halves[rnd, g][...].astype(F32)).astype(BF)
            ring_start_group(rnd, g, 0)

    def chunk(rnd, g, phase, step, half):
        ref = owns[rnd, g] if phase == 0 else middles[rnd, g, phase - 1]
        return ref.at[half, (me[ORDERS[rnd][g][phase]] + step + 4) % 4]

    def ring(rnd, g, phase, number, src, step):
        return remote(
            src,
            landing[rnd, g, phase][number],
            ring_send.at[rnd, g, phase, number],
            ring_recv.at[rnd, g, phase, number],
            device(ORDERS[rnd][g][phase], step),
        )

    flying = {}

    def ring_start_group(rnd, g, phase):
        flying[rnd, g] = {
            0: ring(rnd, g, phase, 0, chunk(rnd, g, phase, 2, 0), 1),
            3: ring(rnd, g, phase, 3, chunk(rnd, g, phase, 2, 1), -1),
            1: ring(rnd, g, phase, 1, chunk(rnd, g, phase, 1, 1), 1),
            4: ring(rnd, g, phase, 4, chunk(rnd, g, phase, -1, 0), -1),
        }

    def ring_relay(rnd, phase):
        for g in range(len(ORDERS[rnd])):
            land = landing[rnd, g, phase]
            for number, step, half, slot in ((0, 1, 0, 6), (3, -1, 1, 7)):
                flying[rnd, g][number].wait_recv()
                land[slot][...] = (
                    land[number][...].astype(F32) + chunk(rnd, g, phase, step, half)[...].astype(F32)
                ).astype(BF)
                flying[rnd, g][number + 2] = ring(rnd, g, phase, number + 2, land[slot], step)

    def ring_end(rnd, phase):
        for g in range(len(ORDERS[rnd])):
            land = landing[rnd, g, phase]
            copies = flying[rnd, g]
            for number in (1, 4, 2, 5):
                copies[number].wait()
            copies[0].wait_send()
            copies[3].wait_send()
            for half, near, far in ((0, 4, 2), (1, 1, 5)):
                value = (
                    chunk(rnd, g, phase, 0, half)[...].astype(F32)
                    + land[near][...].astype(F32)
                    + land[far][...].astype(F32)
                ).astype(BF)
                start = half * FIRST
                if phase < 2:
                    middles[rnd, g, phase][half] = value
                    continue
                kind, first, _ = PIECES[rnd][g]
                target = gi_out if kind == "in" else go_out
                target[:, first + start : first + start + FIRST] = value[:8]
                target[:, first + LANES + start : first + LANES + start + FIRST] = value[8:]
            if phase < 2:
                ring_start_group(rnd, g, phase + 1)

    def gain_start(stage):
        if stage == 0:
            return [remote(gain_mine.at[0], gain_land.at[0], gain_send.at[0], gain_recv.at[0], sibling)]
        return [
            remote(
                gain_mine.at[stage],
                gain_land.at[3 * stage - 2 + n],
                gain_send.at[3 * stage - 2 + n],
                gain_recv.at[3 * stage - 2 + n],
                device(AXES[stage - 1], n + 1),
            )
            for n in range(3)
        ]

    def gain_finish(stage, copies):
        total = gain_mine[stage]
        for copy in copies:
            copy.wait()
        if stage == 0:
            return total + gain_land[0]
        slot = 3 * stage - 2
        return total + gain_land[slot] + gain_land[slot + 1] + gain_land[slot + 2]

    def attended_step(s):
        rows = slice(s * PAIR, (s + 1) * PAIR)
        attended = dot(gctx[rows], wout[...]).astype(BF).astype(F32)
        xw_out[rows] = (xw[rows].astype(F32) + attended).astype(BF)

    def grad_step(s):
        rows = slice(s * PAIR, (s + 1) * PAIR)
        grad = dg(proj[rows], win[...], NT).astype(BF).astype(F32)
        standard, inverse = standardised(xw[rows].astype(F32))
        scaled = grad * gain_ref[...]
        first = jnp.mean(scaled, axis=-1, keepdims=True)
        second = jnp.mean(scaled * standard, axis=-1, keepdims=True)
        local = inverse * (scaled - first - standard * second)
        cw[rows] = (cw[rows].astype(F32) + local).astype(BF)
        return jnp.sum(grad * standard, axis=0, keepdims=True)

    def pack_back(number, final):
        both = dot(r1_ref[...], final[PAIR : 2 * PAIR]).astype(BF)
        send_strip[number][0:144] = both[:144]
        send_strip[number][304:400] = both[144:]
        send_strip[number][144:304] = dot(r2_ref[...], final[2 * PAIR :]).astype(BF)
        return send_strips(number, -1)

    def assemble(own, final, strip):
        value = dot(
            imid_ref[...], jnp.concatenate([final[:PAIR], final[2 * PAIR :], strip[144:304]], 0)
        ).astype(BF)
        own[72:360] = value[:288]
        own[504:792] = value[288:]
        value = dot(ibot_ref[...], jnp.concatenate([final[PAIR : 2 * PAIR], strip[304:352]], 0)).astype(BF)
        own[360:432] = value[:72]
        own[792:864] = value[72:]
        value = dot(itop_ref[...], jnp.concatenate([strip[0:144], strip[352:400]], 0)).astype(BF)
        own[0:72] = value[:72]
        own[432:504] = value[72:]

    xw_out = nw

    loads[3].wait()
    gather_tokens(0)
    gather_cotangent(0)
    for load in loads[4:]:
        load.wait()
    mask[0] = jnp.zeros((2, WINT, WINT), F32)
    mask[1] = jnp.where(lat == 3, 1.0, 0.0) * mask_ref[...].reshape(2, WINT, WINT)

    def turn(h, _):
        bias[h] = bias[h].T
        return 0

    lax.fori_loop(0, 16, turn, 0)
    project(0, PAIR)
    project_back(0, PAIR)

    def early(p, _):
        unit(0, p, None)
        unit(1, p, None)
        return 0

    lax.fori_loop(0, 8, early, 0)
    for copy in strip_copies[0]:
        copy.wait()
    gather_tokens(1)
    gather_tokens(2)
    project(1, 2 * PAIR)

    def turn_rows(n, _):
        at = pl.ds(pl.multiple_of(n * 256, 256), 256)
        nwt[at, :] = nw[:, at].T
        return 0

    lax.fori_loop(0, 4, turn_rows, 0)
    for copy in strip_copies[1]:
        copy.wait()
    gather_cotangent(1)
    gather_cotangent(2)
    project_back(1, 2 * PAIR)

    def first_pairs(p, _):
        late_windows(p)
        return 0

    lax.fori_loop(0, 4, first_pairs, 0)
    start_round(0)
    own_products(0)
    late_windows(4)
    end_core(0)
    late_windows(5)
    ring_relay(0, 0)
    late_windows(6)
    ring_end(0, 0)
    late_windows(7)
    start_round(1)
    ring_relay(0, 1)

    def turn_context(n, _):
        at = pl.ds(pl.multiple_of(n * 256, 256), 256)
        ctxt[at, :] = gctx[:, at].T
        return 0

    lax.fori_loop(0, 4, turn_context, 0)
    start_round(2)
    own_products(1)
    ring_end(0, 1)
    attended_step(1)
    attended_step(2)
    back_out = pack_back(2, xw_out)
    end_core(1)
    own_products(2)
    gain = grad_step(1)
    end_core(2)
    ring_relay(0, 2)
    gain += grad_step(2)
    back_grad = pack_back(3, cw)
    ring_relay(1, 0)
    gain += grad_step(0)
    for n in range(8):
        gain_mine[0, n : n + 1, :] = gain[:, n * 128 : (n + 1) * 128]
    gain_copies = gain_start(0)
    ring_relay(2, 0)
    ring_end(1, 0)
    attended_step(0)
    gain_mine[1] = gain_finish(0, gain_copies)
    gain_copies = gain_start(1)
    ring_end(2, 0)
    ring_relay(1, 1)
    for copy in back_out:
        copy.wait()
    assemble(own_x, xw_out, recv_strip[2])
    store_out = pltpu.make_async_copy(own_x, out_hbm, load_sem.at[0])
    store_out.start()
    gain_mine[2] = gain_finish(1, gain_copies)
    gain_copies = gain_start(2)
    ring_relay(2, 1)
    ring_end(1, 1)
    gain_mine[3] = gain_finish(2, gain_copies)
    gain_copies = gain_start(3)
    ring_end(2, 1)
    ring_relay(1, 2)
    for copy in back_grad:
        copy.wait()
    assemble(own_c, cw, recv_strip[3])
    store_grad = pltpu.make_async_copy(own_c, gt_hbm, load_sem.at[1])
    store_grad.start()
    ring_relay(2, 2)
    gg_out[...] = gain_finish(3, gain_copies)
    ring_end(0, 2)
    ring_end(1, 2)
    ring_end(2, 2)
    store_out.wait()
    store_grad.wait()


def block(tokens, cotangent, gain, attention_in, attention_out, head_bias):
    vm = pl.BlockSpec(memory_space=pltpu.VMEM)
    hbm = pl.BlockSpec(memory_space=pl.ANY)
    perms = [jnp.asarray(m, BF) for m in permutations()]
    wide = lambda rows, columns=D: pltpu.VMEM((rows, columns), BF)
    scratch = [wide(OWN) for _ in range(5)]
    scratch += [wide(D, OWN), wide(D, OWN), wide(OWN, 3 * D), wide(OWN), wide(D, 3 * D), wide(D)]
    scratch += [pltpu.VMEM((16, WINT, WINT), F32), pltpu.VMEM((2, 2, WINT, WINT), F32)]
    scratch += [wide(*m.shape[1:]) for m in perms]
    scratch += [wide(STRIP) for _ in range(8)]
    scratch += [pltpu.VMEM((2, 4, 4, 4, 16, FIRST), BF) for _ in range(3 * len(GROUPS))]
    middles = []
    for r, g in GROUPS:
        for phase in range(3):
            lead = (4,) * (2 - phase)
            scratch += [pltpu.VMEM(lead + (16, FIRST), BF) for _ in range(8)]
            if phase < 2:
                middles.append(pltpu.VMEM((2,) + lead + (16, FIRST), BF))
    scratch += middles
    scratch += [pltpu.VMEM((4, 8, 128), F32), pltpu.VMEM((10, 8, 128), F32)]
    dma = pltpu.SemaphoreType.DMA
    scratch += [dma((14,)), dma((4, 5)), dma((4, 5)), dma((3, 3)), dma((3, 3))]
    scratch += [dma((3, 3, 3, 6)), dma((3, 3, 3, 6)), dma((10,)), dma((10,))]
    return pl.pallas_call(
        block_kernel,
        in_specs=[hbm, hbm, vm, hbm, hbm, hbm, vm] + [hbm] * 9,
        out_specs=[hbm, hbm, vm, vm, vm],
        out_shape=[
            jax.ShapeDtypeStruct((OWN, D), BF),
            jax.ShapeDtypeStruct((OWN, D), BF),
            jax.ShapeDtypeStruct((8, 3 * D), BF),
            jax.ShapeDtypeStruct((8, D), BF),
            jax.ShapeDtypeStruct((8, 128), F32),
        ],
        scratch_shapes=scratch,
        compiler_params=pltpu.CompilerParams(
            collective_id=0, has_side_effects=True, vmem_limit_bytes=63 * 2**20
        ),
    )(
        tokens, cotangent, gain.reshape(1, D), attention_in, attention_out, head_bias,
        jnp.asarray(region_mask()), *perms,
    )


def local(tokens, norm_gain, attention_in, attention_out, head_bias, cotangent):
    shape = tokens.shape
    lat = lax.axis_index("lat")
    lon = lax.axis_index("lon")
    out, gt, gi, go, gains = block(
        tokens.reshape(OWN, D), cotangent.reshape(OWN, D), norm_gain, attention_in, attention_out, head_bias
    )
    gain = lax.dynamic_slice(gains.reshape(1024), ((lat * 32 + lon) * 8,), (8,))
    return out.reshape(shape), gt.reshape(shape), gi, go, gain


def solution(mesh):
    split = P(None, "lat", "lon", None)
    both = ("lat", "lon")
    return jax.shard_map(
        local,
        mesh=mesh,
        in_specs=(split, P(), P(), P(), P(), split),
        out_specs=(split, split, P(both, None), P(both, None), P(both)),
        check_vma=False,
    )
```

```python
import jax
import jax.numpy as jnp
import numpy as np
from jax import lax
from jax.experimental import pallas as pl
from jax.experimental.pallas import tpu as pltpu
from jax.sharding import PartitionSpec as P

D = 1024
WINT = 144
PAIR = 288
OWN = 864
STRIP = 400
NT = (((1,), (1,)), ((), ()))
TN = (((0,), (0,)), ((), ()))
BF = jnp.bfloat16
F32 = jnp.float32

AXES = ("x", "y", "z")
ORDERS = (
    (("x", "y", "z"), ("y", "z", "x"), ("z", "x", "y")),
    (("x", "y", "z"), ("y", "z", "x"), ("z", "x", "y")),
    (("x", "z", "y"), ("z", "x", "y")),
)
PIECES = (
    tuple(("in", 1024 * g, 512) for g in range(3)),
    tuple(("in", 1024 * g + 512, 512) for g in range(3)),
    tuple(("out", 512 * g, 512) for g in range(2)),
)
LANES = 256
FIRST = 128
GROUPS = tuple((r, g) for r in range(3) for g in range(len(ORDERS[r])))


def strip_cells(core):
    cells = [(l, r, c) for l in range(2) for r in range(3) for c in range(24)]
    cells += [(l, r, c) for l in range(2) for r in range(3, 9) for c in range(18, 24)] + [None] * 8
    first = 0 if core else 18
    cells += [(l, r, c) for l in range(2) for r in range(9, 15) for c in range(first, first + 6)] + [None] * 8
    cells += [(l, r, c) for l in range(2) for r in range(15, 18) for c in range(6)] + [None] * 12
    cells += [(l, r, c) for l in range(2) for r in range(3) for c in range(6)] + [None] * 12
    return cells


def received_cells(core):
    cells = []
    for n, cell in enumerate(strip_cells(core)):
        if cell is None:
            cells.append(None)
            continue
        l, r, c = cell
        if n < 144 or n >= 352:
            r += 18
        if n >= 144:
            c += 24 if c < 6 else -24
        cells.append((l, r, c))
    return cells


def window_cells(core):
    corners = ((3, 6), (9, 6), (15, 6), (15, 18), (3, -6), (9, 18 if core else -6))
    return [(l, r + a, c + b) for r, c in corners for l in range(2) for a in range(6) for b in range(12)]


def one_hot(targets, sources):
    place = {}
    for n, cell in enumerate(sources):
        if cell is not None and cell not in place:
            place[cell] = n
    out = np.zeros((len(targets), len(sources)), np.float32)
    for n, cell in enumerate(targets):
        if cell is not None and cell in place:
            out[n, place[cell]] = 1
    return out


def permutations():
    own = [(l, r, c) for l in range(2) for r in range(18) for c in range(24)]
    wide = own[64:368] + own[496:800]
    mid = own[72:360] + own[504:792]
    bottom = own[360:432] + own[792:864]
    top = own[:72] + own[432:504]
    every = []
    for core in range(2):
        strips = strip_cells(core)
        got = received_cells(core)
        win = window_cells(core)
        inner = [c if c is not None and c[2] >= 6 else None for c in strips[:144]]
        every.append(
            (
                one_hot(strips, own),
                one_hot(win[:288], wide),
                one_hot(win[288:576], own[352:432] + own[784:864] + got[:144] + got[304:]),
                one_hot(win[576:], wide + got[144:304]),
                one_hot(got[:144] + got[304:], win[288:576]),
                one_hot(got[144:304], win[576:]),
                one_hot(mid, win[:288] + win[576:] + strips[144:304]),
                one_hot(bottom, win[288:576] + strips[304:352]),
                one_hot(top, inner + strips[352:]),
            )
        )
    return tuple(np.stack(pair) for pair in zip(*every))


def region_mask():
    region = np.array([a < 3 for l in range(2) for a in range(6) for b in range(12)])
    one = np.where(region[:, None] == region[None, :], 0.0, -1e9).astype(np.float32)
    return np.concatenate([one] * 4, 1)


def dg(a, b, dims):
    return lax.dot_general(a, b, dims, preferred_element_type=F32)


def dot(a, b):
    return jnp.dot(a, b, preferred_element_type=F32)


def mesh_place(core, x, y, z):
    return ((z % 2) * 2 + core, (z // 2) * 16 + x * 4 + y)


def block_kernel(
    tok_hbm, cot_hbm, gain_ref, win_hbm, wout_hbm, hb_hbm, mask_ref,
    pack_hbm, p0_hbm, p1_hbm, p2_hbm, r1_hbm, r2_hbm, imid_hbm, ibot_hbm, itop_hbm,
    out_hbm, gt_hbm, gi_out, go_out, gg_out,
    *scratch,
):
    scratch = list(scratch)

    def take(count):
        out = scratch[:count]
        del scratch[:count]
        return out

    own_x, own_c, xw, cw, nw, nwt, proj, gctx, win, wout, raw, bias, mask = take(13)
    perms = take(9)
    pack_ref, p0_ref, p1_ref, p2_ref, r1_ref, r2_ref, imid_ref, ibot_ref, itop_ref = perms
    send_strip, recv_strip = take(2) * 2, take(4)
    sends = {at: take(1)[0] for at in GROUPS}
    owns = {at: take(1)[0] for at in GROUPS}
    halves = {at: take(1)[0] for at in GROUPS}
    landing = {(r, g, p): take(3 if p else 8) for r, g in GROUPS for p in range(3)}
    middles = {(r, g, p): take(1)[0] for r, g in GROUPS for p in range(2)}
    gain_mine, gain_land = take(2)
    load_sem, strip_send, strip_recv, core_send, core_recv = take(5)
    ring_send, ring_recv, gain_send, gain_recv = take(4)

    lat = lax.axis_index("lat")
    lon = lax.axis_index("lon")
    core = lat % 2
    me = {"x": (lon // 4) % 4, "y": lon % 4, "z": (lon // 16) * 2 + lat // 2}

    def device(axis, step):
        at = dict(me)
        at[axis] = (me[axis] + step + 4) % 4
        return mesh_place(core, at["x"], at["y"], at["z"])

    sibling = mesh_place(1 - core, me["x"], me["y"], me["z"])

    def grid_place(a, b):
        return ((lat + a + 4) % 4, (lon + b + 32) % 32)

    loads = [
        pltpu.make_async_copy(src, dst, load_sem.at[n])
        for n, (src, dst) in enumerate(
            (
                (tok_hbm, own_x), (pack_hbm.at[core], pack_ref), (cot_hbm, own_c), (p0_hbm.at[core], p0_ref),
                (hb_hbm, raw), (win_hbm, win), (wout_hbm, wout), (p1_hbm.at[core], p1_ref), (p2_hbm.at[core], p2_ref),
                (r1_hbm.at[core], r1_ref), (r2_hbm.at[core], r2_ref), (imid_hbm.at[core], imid_ref),
                (ibot_hbm.at[core], ibot_ref), (itop_hbm.at[core], itop_ref),
            )
        )
    ]
    for load in loads[:4]:
        load.start()

    barrier = pltpu.get_barrier_semaphore()
    partners = [sibling] + [device(a, s) for a in AXES for s in (1, -1, 2)]
    partners += [grid_place(s * a, s * b) for a, b in ((1, 0), (0, 1), (1, 1)) for s in (1, -1)]
    for other in partners:
        pl.semaphore_signal(barrier, inc=1, device_id=other, device_id_type=pl.DeviceIdType.MESH)
    pl.semaphore_wait(barrier, len(partners))

    def remote(src, dst, send, recv, place):
        copy = pltpu.make_async_remote_copy(
            src_ref=src,
            dst_ref=dst,
            send_sem=send,
            recv_sem=recv,
            device_id=place,
            device_id_type=pl.DeviceIdType.MESH,
        )
        copy.start()
        return copy

    turned = jnp.where(core == 0, 1, -1)
    PARTS = ((0, 144, -1, 0), (144, 80, 0, 1), (224, 80, 0, turned), (304, 48, 0, -1), (352, 48, -1, -1))

    def send_strips(number, way, parts=range(5)):
        copies = []
        for part in parts:
            low, size, a, b = PARTS[part]
            copies.append(
                remote(
                    send_strip[number].at[pl.ds(low, size)],
                    recv_strip[number].at[pl.ds(low, size)],
                    strip_send.at[number, part],
                    strip_recv.at[number, part],
                    grid_place(way * a, way * b),
                )
            )
        return copies

    strip_copies = []
    loads[0].wait()
    loads[1].wait()
    for load in loads[4:7]:
        load.start()
    for number, own in ((0, own_x), (1, own_c)):
        if number == 1:
            loads[2].wait()
        send_strip[number][...] = dot(pack_ref[...], own[...]).astype(BF)
        strip_copies.append(send_strips(number, 1))

    def gathered(own, strip, s):
        if s == 1:
            parts = [own[352:432], own[784:864], strip[0:144], strip[304:400]]
            return dot(p1_ref[...], jnp.concatenate(parts, 0))
        parts = [own[64:368], own[496:800]]
        if s == 0:
            return dot(p0_ref[...], jnp.concatenate(parts, 0))
        return dot(p2_ref[...], jnp.concatenate(parts + [strip[144:304]], 0))

    def standardised(x):
        centred = x - jnp.mean(x, axis=-1, keepdims=True)
        inverse = lax.rsqrt(jnp.mean(centred * centred, axis=-1, keepdims=True) + 1e-5)
        return centred * inverse, inverse

    def gather_tokens(s):
        rows = slice(s * PAIR, (s + 1) * PAIR)
        x = gathered(own_x, recv_strip[0], s)
        xw[rows] = x.astype(BF)
        standard, _ = standardised(x)
        nw[rows] = (standard * gain_ref[...]).astype(BF)

    def gather_cotangent(s):
        rows = slice(s * PAIR, (s + 1) * PAIR)
        cw[rows] = gathered(own_c, recv_strip[1], s).astype(BF)

    def project(s, count):
        rows = slice(s * PAIR, s * PAIR + count)

        def columns(n, _):
            at = pl.ds(pl.multiple_of(n * 512, 512), 512)
            value = dot(nw[rows], win[:, at])
            proj[rows, at] = (value * jnp.where(n < 2, 0.125, 1.0)).astype(BF)
            return 0

        lax.fori_loop(0, 6, columns, 0)

    def project_back(s, count):
        rows = slice(s * PAIR, s * PAIR + count)

        def outer(n, _):
            at = pl.ds(pl.multiple_of(n * 512, 512), 512)
            gctx[rows, at] = dg(cw[rows], wout[at, :], NT).astype(BF)
            return 0

        lax.fori_loop(0, 2, outer, 0)

    head = lax.broadcasted_iota(jnp.int32, (WINT, 256), 1) // 64
    low_half = lax.broadcasted_iota(jnp.int32, (WINT, 128), 1) < 64
    zero = jnp.zeros((WINT, 256), BF)

    def stacked(a):
        return jnp.concatenate([jnp.where(head == h, a, zero) for h in range(4)], 0)

    def by_query(scores, a):
        turned = scores.T
        parts = []
        for n in range(2):
            both = dot(turned[n * PAIR : (n + 1) * PAIR], a[:, n * 128 : (n + 1) * 128])
            parts.append(jnp.where(low_half, both[:WINT], both[WINT:]))
        return jnp.concatenate(parts, 1)

    def unit(w, p, masked):
        rows = pl.ds(pl.multiple_of(w * WINT, 16), WINT)
        at_q = pl.ds(pl.multiple_of(p * 256, 256), 256)
        at_k = pl.ds(pl.multiple_of(1024 + p * 256, 256), 256)
        at_v = pl.ds(pl.multiple_of(2048 + p * 256, 256), 256)
        q, k, v, d = proj[rows, at_q], proj[rows, at_k], proj[rows, at_v], gctx[rows, at_q]
        qs, ds = stacked(q), stacked(d)
        offset = bias[p]
        if masked:
            offset = offset + mask[...]
        st = dg(k, qs, NT) + offset
        powers = jnp.exp(st - jnp.max(st, axis=0, keepdims=True))
        weights = powers * (1.0 / jnp.sum(powers, axis=0, keepdims=True))
        wb = weights.astype(BF)
        dw = dg(v, ds, NT)
        inner = jnp.sum(dw * weights, axis=0, keepdims=True)
        gs = (weights * (dw - inner)).astype(BF)
        gctx[rows, at_q] = by_query(wb, v).astype(BF)
        proj[rows, at_q] = (by_query(gs, k) * 0.125).astype(BF)
        proj[rows, at_k] = dot(gs, qs).astype(BF)
        proj[rows, at_v] = dot(wb, ds).astype(BF)

    def late_windows(p, t):
        unit(2 + 2 * t, p, t == 0)
        unit(3 + 2 * t, p, t == 0)

    def products(rnd, g, half, target):
        kind, first, width = PIECES[rnd][g]
        right = proj if kind == "in" else cw

        order = ORDERS[rnd][g]

        def rows_of(zl, _):
            at = pl.multiple_of(zl * 512 + half * 256, 256)
            value = dot(nwt[pl.ds(at, 256), :], right[:, first : first + width]).reshape(32, 8, width)
            both = jnp.concatenate([value[:, :, :LANES], value[:, :, LANES:]], 1).astype(BF)
            both = both.reshape(2, 4, 4, 16, LANES)
            for zh in range(2):
                z = 2 * zh + zl
                for end in range(2):
                    part = both[zh, :, :, :, end * FIRST : (end + 1) * FIRST]
                    if order.index("y") < order.index("x"):
                        part = jnp.swapaxes(part, 0, 1)
                    place = [end, slice(None), slice(None), slice(None)]
                    place[1 + order.index("z")] = z
                    target[tuple(place)] = part
            return 0

        lax.fori_loop(0, 2, rows_of, 0)

    core_copies = {}

    def start_round(rnd):
        for g in range(len(ORDERS[rnd])):
            products(rnd, g, 1 - core, sends[rnd, g])
            core_copies[rnd, g] = remote(
                sends[rnd, g], halves[rnd, g], core_send.at[rnd, g], core_recv.at[rnd, g], sibling
            )

    def own_products(rnd):
        for g in range(len(ORDERS[rnd])):
            products(rnd, g, core, owns[rnd, g])

    def end_core(rnd):
        for g in range(len(ORDERS[rnd])):
            core_copies[rnd, g].wait()
            mine = owns[rnd, g]
            mine[...] = (mine[...].astype(F32) + halves[rnd, g][...].astype(F32)).astype(BF)
            ring_start_group(rnd, g, 0)

    def chunk(rnd, g, phase, step, half):
        ref = owns[rnd, g] if phase == 0 else middles[rnd, g, phase - 1]
        return ref.at[half, (me[ORDERS[rnd][g][phase]] + step + 4) % 4]

    def ring(rnd, g, phase, number, src, step):
        return remote(
            src,
            landing[rnd, g, phase][number],
            ring_send.at[rnd, g, phase, number],
            ring_recv.at[rnd, g, phase, number],
            device(ORDERS[rnd][g][phase], step),
        )

    flying = {}

    def ring_start_group(rnd, g, phase):
        if phase == 0:
            flying[rnd, g] = {
                0: ring(rnd, g, phase, 0, chunk(rnd, g, phase, 2, 0), 1),
                3: ring(rnd, g, phase, 3, chunk(rnd, g, phase, 2, 1), -1),
                1: ring(rnd, g, phase, 1, chunk(rnd, g, phase, 1, 1), 1),
                4: ring(rnd, g, phase, 4, chunk(rnd, g, phase, -1, 0), -1),
            }
            return
        flying[rnd, g] = {
            n: ring(rnd, g, phase, n, chunk(rnd, g, phase, n + 1, slice(None)), n + 1) for n in range(3)
        }

    def ring_relay(rnd):
        for g in range(len(ORDERS[rnd])):
            land = landing[rnd, g, 0]
            for number, step, half, slot in ((0, 1, 0, 6), (3, -1, 1, 7)):
                flying[rnd, g][number].wait_recv()
                land[slot][...] = (
                    land[number][...].astype(F32) + chunk(rnd, g, 0, step, half)[...].astype(F32)
                ).astype(BF)
                flying[rnd, g][number + 2] = ring(rnd, g, 0, number + 2, land[slot], step)

    def ring_end(rnd, phase):
        for g in range(len(ORDERS[rnd])):
            land = landing[rnd, g, phase]
            copies = flying[rnd, g]
            if phase == 0:
                for number in (1, 4, 2, 5):
                    copies[number].wait()
                copies[0].wait_send()
                copies[3].wait_send()
                for half, near, far in ((0, 4, 2), (1, 1, 5)):
                    middles[rnd, g, phase][half] = (
                        chunk(rnd, g, phase, 0, half)[...].astype(F32)
                        + land[near][...].astype(F32)
                        + land[far][...].astype(F32)
                    ).astype(BF)
                ring_start_group(rnd, g, 1)
                continue
            for number in range(3):
                copies[number].wait()
            value = chunk(rnd, g, phase, 0, slice(None))[...].astype(F32)
            for number in range(3):
                value = value + land[number][...].astype(F32)
            value = value.astype(BF)
            if phase == 1:
                middles[rnd, g, phase][...] = value
                ring_start_group(rnd, g, 2)
                continue
            kind, first, _ = PIECES[rnd][g]
            target = gi_out if kind == "in" else go_out
            for half in range(2):
                at = first + half * FIRST
                target[:, at : at + FIRST] = value[half, :8]
                target[:, at + LANES : at + LANES + FIRST] = value[half, 8:]

    def gain_start(stage):
        if stage == 0:
            return [remote(gain_mine.at[0], gain_land.at[0], gain_send.at[0], gain_recv.at[0], sibling)]
        return [
            remote(
                gain_mine.at[stage],
                gain_land.at[3 * stage - 2 + n],
                gain_send.at[3 * stage - 2 + n],
                gain_recv.at[3 * stage - 2 + n],
                device(AXES[stage - 1], n + 1),
            )
            for n in range(3)
        ]

    def gain_finish(stage, copies):
        total = gain_mine[stage]
        for copy in copies:
            copy.wait()
        if stage == 0:
            return total + gain_land[0]
        slot = 3 * stage - 2
        return total + gain_land[slot] + gain_land[slot + 1] + gain_land[slot + 2]

    def attended_step(s):
        rows = slice(s * PAIR, (s + 1) * PAIR)
        attended = dot(gctx[rows], wout[...]).astype(BF).astype(F32)
        xw_out[rows] = (xw[rows].astype(F32) + attended).astype(BF)

    def grad_step(s):
        rows = slice(s * PAIR, (s + 1) * PAIR)
        grad = dg(proj[rows], win[...], NT).astype(BF).astype(F32)
        standard, inverse = standardised(xw[rows].astype(F32))
        scaled = grad * gain_ref[...]
        first = jnp.mean(scaled, axis=-1, keepdims=True)
        second = jnp.mean(scaled * standard, axis=-1, keepdims=True)
        local = inverse * (scaled - first - standard * second)
        cw[rows] = (cw[rows].astype(F32) + local).astype(BF)
        return jnp.sum(grad * standard, axis=0, keepdims=True)

    def pack_back(number, final):
        both = dot(r1_ref[...], final[PAIR : 2 * PAIR]).astype(BF)
        send_strip[number][0:144] = both[:144]
        send_strip[number][304:400] = both[144:]
        send_strip[number][144:304] = dot(r2_ref[...], final[2 * PAIR :]).astype(BF)
        return send_strips(number, -1)

    def assemble(own, final, strip):
        value = dot(
            imid_ref[...], jnp.concatenate([final[:PAIR], final[2 * PAIR :], strip[144:304]], 0)
        ).astype(BF)
        own[72:360] = value[:288]
        own[504:792] = value[288:]
        value = dot(ibot_ref[...], jnp.concatenate([final[PAIR : 2 * PAIR], strip[304:352]], 0)).astype(BF)
        own[360:432] = value[:72]
        own[792:864] = value[72:]
        value = dot(itop_ref[...], jnp.concatenate([strip[0:144], strip[352:400]], 0)).astype(BF)
        own[0:72] = value[:72]
        own[432:504] = value[72:]

    xw_out = nw

    loads[3].wait()
    gather_tokens(0)
    gather_cotangent(0)
    loads[4].wait()
    mask[...] = jnp.where(lat == 3, 1.0, 0.0) * mask_ref[...]

    def turn(p, _):
        for h in range(4):
            bias[p, :, h * WINT : (h + 1) * WINT] = raw[4 * p + h].T
        return 0

    lax.fori_loop(0, 4, turn, 0)
    loads[5].wait()
    project(0, PAIR)
    loads[6].wait()
    project_back(0, PAIR)
    for load in loads[7:]:
        load.start()

    def early(p, _):
        unit(0, p, False)
        unit(1, p, False)
        return 0

    lax.fori_loop(0, 4, early, 0)
    for load in loads[7:]:
        load.wait()
    for copy in strip_copies[0]:
        copy.wait()
    gather_tokens(1)
    gather_tokens(2)
    project(1, 2 * PAIR)

    def turn_rows(n, _):
        at = pl.ds(pl.multiple_of(n * 256, 256), 256)
        nwt[at, :] = nw[:, at].T
        return 0

    lax.fori_loop(0, 4, turn_rows, 0)
    for copy in strip_copies[1]:
        copy.wait()
    gather_cotangent(1)
    gather_cotangent(2)
    project_back(1, 2 * PAIR)

    def first_pairs(p, _):
        late_windows(p, 0)
        late_windows(p, 1)
        return 0

    lax.fori_loop(0, 2, first_pairs, 0)
    start_round(0)
    own_products(0)
    late_windows(2, 0)
    end_core(0)
    late_windows(2, 1)
    ring_relay(0)
    late_windows(3, 0)
    ring_end(0, 0)
    late_windows(3, 1)
    start_round(1)
    own_products(1)
    ring_end(0, 1)

    def turn_context(n, _):
        at = pl.ds(pl.multiple_of(n * 256, 256), 256)
        nwt[at, :] = gctx[:, at].T
        return 0

    lax.fori_loop(0, 4, turn_context, 0)
    start_round(2)
    attended_step(1)
    attended_step(2)
    back_out = pack_back(2, xw_out)
    end_core(1)
    own_products(2)
    gain = grad_step(1)
    end_core(2)
    gain += grad_step(2)
    back_grad = pack_back(3, cw)
    ring_end(0, 2)
    ring_relay(1)
    gain += grad_step(0)
    for n in range(8):
        gain_mine[0, n : n + 1, :] = gain[:, n * 128 : (n + 1) * 128]
    gain_copies = gain_start(0)
    ring_relay(2)
    attended_step(0)
    ring_end(1, 0)
    gain_mine[1] = gain_finish(0, gain_copies)
    gain_copies = gain_start(1)
    for copy in back_out:
        copy.wait()
    assemble(own_x, xw_out, recv_strip[2])
    store_out = pltpu.make_async_copy(own_x, out_hbm, load_sem.at[0])
    store_out.start()
    ring_end(2, 0)
    gain_mine[2] = gain_finish(1, gain_copies)
    gain_copies = gain_start(2)
    ring_end(1, 1)
    for copy in back_grad:
        copy.wait()
    assemble(own_c, cw, recv_strip[3])
    store_grad = pltpu.make_async_copy(own_c, gt_hbm, load_sem.at[1])
    store_grad.start()
    ring_end(2, 1)
    gain_mine[3] = gain_finish(2, gain_copies)
    gain_copies = gain_start(3)
    ring_end(1, 2)
    gg_out[...] = gain_finish(3, gain_copies)
    ring_end(2, 2)
    store_out.wait()
    store_grad.wait()


def block(tokens, cotangent, gain, attention_in, attention_out, head_bias):
    vm = pl.BlockSpec(memory_space=pltpu.VMEM)
    hbm = pl.BlockSpec(memory_space=pl.ANY)
    perms = [jnp.asarray(m, BF) for m in permutations()]
    wide = lambda rows, columns=D: pltpu.VMEM((rows, columns), BF)
    scratch = [wide(OWN) for _ in range(5)]
    scratch += [wide(D, OWN), wide(OWN, 3 * D), wide(OWN), wide(D, 3 * D), wide(D)]
    scratch += [pltpu.VMEM((16, WINT, WINT), F32), pltpu.VMEM((4, WINT, 4 * WINT), F32), pltpu.VMEM((WINT, 4 * WINT), F32)]
    scratch += [wide(*m.shape[1:]) for m in perms]
    scratch += [wide(STRIP) for _ in range(6)]
    scratch += [pltpu.VMEM((2, 4, 4, 4, 16, FIRST), BF) for _ in range(3 * len(GROUPS))]
    middles = []
    for r, g in GROUPS:
        for phase in range(3):
            lead = (4,) * (2 - phase)
            if phase == 0:
                scratch += [pltpu.VMEM(lead + (16, FIRST), BF) for _ in range(8)]
            else:
                scratch += [pltpu.VMEM((2,) + lead + (16, FIRST), BF) for _ in range(3)]
            if phase < 2:
                middles.append(pltpu.VMEM((2,) + lead + (16, FIRST), BF))
    scratch += middles
    scratch += [pltpu.VMEM((4, 8, 128), F32), pltpu.VMEM((10, 8, 128), F32)]
    dma = pltpu.SemaphoreType.DMA
    scratch += [dma((14,)), dma((4, 5)), dma((4, 5)), dma((3, 3)), dma((3, 3))]
    scratch += [dma((3, 3, 3, 6)), dma((3, 3, 3, 6)), dma((10,)), dma((10,))]
    return pl.pallas_call(
        block_kernel,
        in_specs=[hbm, hbm, vm, hbm, hbm, hbm, vm] + [hbm] * 9,
        out_specs=[hbm, hbm, vm, vm, vm],
        out_shape=[
            jax.ShapeDtypeStruct((OWN, D), BF),
            jax.ShapeDtypeStruct((OWN, D), BF),
            jax.ShapeDtypeStruct((8, 3 * D), BF),
            jax.ShapeDtypeStruct((8, D), BF),
            jax.ShapeDtypeStruct((8, 128), F32),
        ],
        scratch_shapes=scratch,
        compiler_params=pltpu.CompilerParams(
            collective_id=0, has_side_effects=True, vmem_limit_bytes=63 * 2**20
        ),
    )(
        tokens, cotangent, gain.reshape(1, D), attention_in, attention_out, head_bias,
        jnp.asarray(region_mask()), *perms,
    )


def local(tokens, norm_gain, attention_in, attention_out, head_bias, cotangent):
    shape = tokens.shape
    lat = lax.axis_index("lat")
    lon = lax.axis_index("lon")
    out, gt, gi, go, gains = block(
        tokens.reshape(OWN, D), cotangent.reshape(OWN, D), norm_gain, attention_in, attention_out, head_bias
    )
    gain = lax.dynamic_slice(gains.reshape(1024), ((lat * 32 + lon) * 8,), (8,))
    return out.reshape(shape), gt.reshape(shape), gi, go, gain


def solution(mesh):
    split = P(None, "lat", "lon", None)
    both = ("lat", "lon")
    return jax.shard_map(
        local,
        mesh=mesh,
        in_specs=(split, P(), P(), P(), P(), split),
        out_specs=(split, split, P(both, None), P(both, None), P(both)),
        check_vma=False,
    )
```

```python
import jax
import jax.numpy as jnp
import numpy as np
from jax import lax
from jax.experimental import pallas as pl
from jax.experimental.pallas import tpu as pltpu
from jax.sharding import PartitionSpec as P

D = 1024
WINT = 144
PAIR = 288
OWN = 864
STRIP = 400
NT = (((1,), (1,)), ((), ()))
TN = (((0,), (0,)), ((), ()))
BF = jnp.bfloat16
F32 = jnp.float32

AXES = ("x", "y", "z")
ORDERS = (
    (("x", "y", "z"), ("y", "z", "x"), ("z", "x", "y")),
    (("x", "y", "z"), ("y", "z", "x"), ("z", "x", "y")),
    (("x", "z", "y"), ("z", "x", "y")),
)
PIECES = (
    tuple(("in", 1024 * g, 512) for g in range(3)),
    tuple(("in", 1024 * g + 512, 512) for g in range(3)),
    tuple(("out", 512 * g, 512) for g in range(2)),
)
LANES = 256
FIRST = 128
GROUPS = tuple((r, g) for r in range(3) for g in range(len(ORDERS[r])))


def strip_cells(core):
    cells = [(l, r, c) for l in range(2) for r in range(3) for c in range(24)]
    cells += [(l, r, c) for l in range(2) for r in range(3, 9) for c in range(18, 24)] + [None] * 8
    first = 0 if core else 18
    cells += [(l, r, c) for l in range(2) for r in range(9, 15) for c in range(first, first + 6)] + [None] * 8
    cells += [(l, r, c) for l in range(2) for r in range(15, 18) for c in range(6)] + [None] * 12
    cells += [(l, r, c) for l in range(2) for r in range(3) for c in range(6)] + [None] * 12
    return cells


def received_cells(core):
    cells = []
    for n, cell in enumerate(strip_cells(core)):
        if cell is None:
            cells.append(None)
            continue
        l, r, c = cell
        if n < 144 or n >= 352:
            r += 18
        if n >= 144:
            c += 24 if c < 6 else -24
        cells.append((l, r, c))
    return cells


def window_cells(core):
    corners = ((3, 6), (9, 6), (15, 6), (15, 18), (3, -6), (9, 18 if core else -6))
    return [(l, r + a, c + b) for r, c in corners for l in range(2) for a in range(6) for b in range(12)]


def one_hot(targets, sources):
    place = {}
    for n, cell in enumerate(sources):
        if cell is not None and cell not in place:
            place[cell] = n
    out = np.zeros((len(targets), len(sources)), np.float32)
    for n, cell in enumerate(targets):
        if cell is not None and cell in place:
            out[n, place[cell]] = 1
    return out


def permutations():
    own = [(l, r, c) for l in range(2) for r in range(18) for c in range(24)]
    wide = own[64:368] + own[496:800]
    mid = own[72:360] + own[504:792]
    bottom = own[360:432] + own[792:864]
    top = own[:72] + own[432:504]
    every = []
    for core in range(2):
        strips = strip_cells(core)
        got = received_cells(core)
        win = window_cells(core)
        inner = [c if c is not None and c[2] >= 6 else None for c in strips[:144]]
        every.append(
            (
                one_hot(strips, own),
                one_hot(win[:288], wide),
                one_hot(win[288:576], own[352:432] + own[784:864] + got[:144] + got[304:]),
                one_hot(win[576:], wide + got[144:304]),
                one_hot(got[:144] + got[304:], win[288:576]),
                one_hot(got[144:304], win[576:]),
                one_hot(mid, win[:288] + win[576:] + strips[144:304]),
                one_hot(bottom, win[288:576] + strips[304:352]),
                one_hot(top, inner + strips[352:]),
            )
        )
    return tuple(np.stack(pair) for pair in zip(*every))


def region_mask():
    region = np.array([a < 3 for l in range(2) for a in range(6) for b in range(12)])
    one = np.where(region[:, None] == region[None, :], 0.0, -1e9).astype(np.float32)
    return np.concatenate([one] * 4, 1)


def dg(a, b, dims):
    return lax.dot_general(a, b, dims, preferred_element_type=F32)


def dot(a, b):
    return jnp.dot(a, b, preferred_element_type=F32)


def mesh_place(core, x, y, z):
    return ((z % 2) * 2 + core, (z // 2) * 16 + x * 4 + y)


def block_kernel(
    tok_hbm, cot_hbm, gain_ref, win_hbm, wout_hbm, hb_hbm, mask_ref,
    pack_hbm, p0_hbm, p1_hbm, p2_hbm, r1_hbm, r2_hbm, imid_hbm, ibot_hbm, itop_hbm,
    out_hbm, gt_hbm, gi_out, go_out, gg_out,
    *scratch,
):
    scratch = list(scratch)

    def take(count):
        out = scratch[:count]
        del scratch[:count]
        return out

    own_x, own_c, xw, cw, nw, nwt, proj, gctx, win, wout, raw, bias, mask = take(13)
    perms = take(9)
    pack_ref, p0_ref, p1_ref, p2_ref, r1_ref, r2_ref, imid_ref, ibot_ref, itop_ref = perms
    send_strip, recv_strip = take(2) * 2, take(4)
    sends = {at: take(1)[0] for at in GROUPS}
    owns = {at: take(1)[0] for at in GROUPS}
    halves = {at: take(1)[0] for at in GROUPS}
    landing = {(r, g, p): take(3 if p else 8) for r, g in GROUPS for p in range(3)}
    middles = {(r, g, p): take(1)[0] for r, g in GROUPS for p in range(2)}
    gain_mine, gain_land = take(2)
    load_sem, strip_send, strip_recv, core_send, core_recv = take(5)
    ring_send, ring_recv, gain_send, gain_recv = take(4)

    lat = lax.axis_index("lat")
    lon = lax.axis_index("lon")
    core = lat % 2
    me = {"x": (lon // 4) % 4, "y": lon % 4, "z": (lon // 16) * 2 + lat // 2}

    def device(axis, step):
        at = dict(me)
        at[axis] = (me[axis] + step + 4) % 4
        return mesh_place(core, at["x"], at["y"], at["z"])

    sibling = mesh_place(1 - core, me["x"], me["y"], me["z"])

    def grid_place(a, b):
        return ((lat + a + 4) % 4, (lon + b + 32) % 32)

    loads = [
        pltpu.make_async_copy(src, dst, load_sem.at[n])
        for n, (src, dst) in enumerate(
            (
                (tok_hbm, own_x), (pack_hbm.at[core], pack_ref), (cot_hbm, own_c), (p0_hbm.at[core], p0_ref),
                (hb_hbm, raw), (win_hbm, win), (wout_hbm, wout), (p1_hbm.at[core], p1_ref), (p2_hbm.at[core], p2_ref),
                (r1_hbm.at[core], r1_ref), (r2_hbm.at[core], r2_ref), (imid_hbm.at[core], imid_ref),
                (ibot_hbm.at[core], ibot_ref), (itop_hbm.at[core], itop_ref),
            )
        )
    ]
    for load in loads[:4]:
        load.start()

    barrier = pltpu.get_barrier_semaphore()
    partners = [sibling] + [device(a, s) for a in AXES for s in (1, -1, 2)]
    partners += [grid_place(s * a, s * b) for a, b in ((1, 0), (0, 1), (1, 1)) for s in (1, -1)]
    for other in partners:
        pl.semaphore_signal(barrier, inc=1, device_id=other, device_id_type=pl.DeviceIdType.MESH)
    pl.semaphore_wait(barrier, len(partners))

    def remote(src, dst, send, recv, place):
        copy = pltpu.make_async_remote_copy(
            src_ref=src,
            dst_ref=dst,
            send_sem=send,
            recv_sem=recv,
            device_id=place,
            device_id_type=pl.DeviceIdType.MESH,
        )
        copy.start()
        return copy

    turned = jnp.where(core == 0, 1, -1)
    PARTS = ((0, 144, -1, 0), (144, 80, 0, 1), (224, 80, 0, turned), (304, 48, 0, -1), (352, 48, -1, -1))

    def send_strips(number, way, parts=range(5)):
        copies = []
        for part in parts:
            low, size, a, b = PARTS[part]
            copies.append(
                remote(
                    send_strip[number].at[pl.ds(low, size)],
                    recv_strip[number].at[pl.ds(low, size)],
                    strip_send.at[number, part],
                    strip_recv.at[number, part],
                    grid_place(way * a, way * b),
                )
            )
        return copies

    strip_copies = []
    loads[0].wait()
    loads[1].wait()
    for load in loads[4:7]:
        load.start()
    for number, own in ((0, own_x), (1, own_c)):
        if number == 1:
            loads[2].wait()
        send_strip[number][...] = dot(pack_ref[...], own[...]).astype(BF)
        strip_copies.append(send_strips(number, 1))

    def gathered(own, strip, s):
        if s == 1:
            parts = [own[352:432], own[784:864], strip[0:144], strip[304:400]]
            return dot(p1_ref[...], jnp.concatenate(parts, 0))
        parts = [own[64:368], own[496:800]]
        if s == 0:
            return dot(p0_ref[...], jnp.concatenate(parts, 0))
        return dot(p2_ref[...], jnp.concatenate(parts + [strip[144:304]], 0))

    def standardised(x):
        centred = x - jnp.mean(x, axis=-1, keepdims=True)
        inverse = lax.rsqrt(jnp.mean(centred * centred, axis=-1, keepdims=True) + 1e-5)
        return centred * inverse, inverse

    def gather_tokens(s):
        rows = slice(s * PAIR, (s + 1) * PAIR)
        x = gathered(own_x, recv_strip[0], s)
        xw[rows] = x.astype(BF)
        standard, _ = standardised(x)
        nw[rows] = (standard * gain_ref[...]).astype(BF)

    def gather_cotangent(s):
        rows = slice(s * PAIR, (s + 1) * PAIR)
        cw[rows] = gathered(own_c, recv_strip[1], s).astype(BF)

    def project(s, count):
        rows = slice(s * PAIR, s * PAIR + count)

        def columns(n, _):
            at = pl.ds(pl.multiple_of(n * 512, 512), 512)
            value = dot(nw[rows], win[:, at])
            proj[rows, at] = (value * jnp.where(n < 2, 0.125, 1.0)).astype(BF)
            return 0

        lax.fori_loop(0, 6, columns, 0)

    def project_back(s, count):
        rows = slice(s * PAIR, s * PAIR + count)

        def outer(n, _):
            at = pl.ds(pl.multiple_of(n * 512, 512), 512)
            gctx[rows, at] = dg(cw[rows], wout[at, :], NT).astype(BF)
            return 0

        lax.fori_loop(0, 2, outer, 0)

    head = lax.broadcasted_iota(jnp.int32, (WINT, 256), 1) // 64
    low_half = lax.broadcasted_iota(jnp.int32, (WINT, 128), 1) < 64
    zero = jnp.zeros((WINT, 256), BF)

    def stacked(a):
        return jnp.concatenate([jnp.where(head == h, a, zero) for h in range(4)], 0)

    def by_query(scores, a):
        turned = scores.T
        parts = []
        for n in range(2):
            both = dot(turned[n * PAIR : (n + 1) * PAIR], a[:, n * 128 : (n + 1) * 128])
            parts.append(jnp.where(low_half, both[:WINT], both[WINT:]))
        return jnp.concatenate(parts, 1)

    def unit(w, p, masked):
        rows = pl.ds(pl.multiple_of(w * WINT, 16), WINT)
        at_q = pl.ds(pl.multiple_of(p * 256, 256), 256)
        at_k = pl.ds(pl.multiple_of(1024 + p * 256, 256), 256)
        at_v = pl.ds(pl.multiple_of(2048 + p * 256, 256), 256)
        q, k, v, d = proj[rows, at_q], proj[rows, at_k], proj[rows, at_v], gctx[rows, at_q]
        qs, ds = stacked(q), stacked(d)
        offset = bias[p]
        if masked:
            offset = offset + mask[...]
        st = dg(k, qs, NT) + offset
        powers = jnp.exp(st - jnp.max(st, axis=0, keepdims=True))
        weights = powers * (1.0 / jnp.sum(powers, axis=0, keepdims=True))
        wb = weights.astype(BF)
        dw = dg(v, ds, NT)
        inner = jnp.sum(dw * weights, axis=0, keepdims=True)
        gs = (weights * (dw - inner)).astype(BF)
        gctx[rows, at_q] = by_query(wb, v).astype(BF)
        proj[rows, at_q] = (by_query(gs, k) * 0.125).astype(BF)
        proj[rows, at_k] = dot(gs, qs).astype(BF)
        proj[rows, at_v] = dot(wb, ds).astype(BF)

    def late_windows(p, t):
        unit(2 + 2 * t, p, t == 0)
        unit(3 + 2 * t, p, t == 0)

    def products(rnd, g, half, target):
        kind, first, width = PIECES[rnd][g]
        right = proj if kind == "in" else cw

        order = ORDERS[rnd][g]

        def rows_of(zl, _):
            at = pl.multiple_of(zl * 512 + half * 256, 256)
            value = dot(nwt[pl.ds(at, 256), :], right[:, first : first + width]).reshape(32, 8, width)
            both = jnp.concatenate([value[:, :, :LANES], value[:, :, LANES:]], 1).astype(BF)
            both = both.reshape(2, 4, 4, 16, LANES)
            for zh in range(2):
                z = 2 * zh + zl
                for end in range(2):
                    part = both[zh, :, :, :, end * FIRST : (end + 1) * FIRST]
                    if order.index("y") < order.index("x"):
                        part = jnp.swapaxes(part, 0, 1)
                    place = [end, slice(None), slice(None), slice(None)]
                    place[1 + order.index("z")] = z
                    target[tuple(place)] = part
            return 0

        lax.fori_loop(0, 2, rows_of, 0)

    core_copies = {}

    def start_round(rnd):
        for g in range(len(ORDERS[rnd])):
            products(rnd, g, 1 - core, sends[rnd, g])
            core_copies[rnd, g] = remote(
                sends[rnd, g], halves[rnd, g], core_send.at[rnd, g], core_recv.at[rnd, g], sibling
            )

    def own_products(rnd):
        for g in range(len(ORDERS[rnd])):
            products(rnd, g, core, owns[rnd, g])

    def end_core(rnd):
        for g in range(len(ORDERS[rnd])):
            core_copies[rnd, g].wait()
            mine = owns[rnd, g]
            mine[...] = (mine[...].astype(F32) + halves[rnd, g][...].astype(F32)).astype(BF)
            ring_start_group(rnd, g, 0)

    def chunk(rnd, g, phase, step, half):
        ref = owns[rnd, g] if phase == 0 else middles[rnd, g, phase - 1]
        return ref.at[half, (me[ORDERS[rnd][g][phase]] + step + 4) % 4]

    def ring(rnd, g, phase, number, src, step):
        return remote(
            src,
            landing[rnd, g, phase][number],
            ring_send.at[rnd, g, phase, number],
            ring_recv.at[rnd, g, phase, number],
            device(ORDERS[rnd][g][phase], step),
        )

    flying = {}

    def ring_start_group(rnd, g, phase):
        if phase == 0:
            flying[rnd, g] = {
                0: ring(rnd, g, phase, 0, chunk(rnd, g, phase, 2, 0), 1),
                3: ring(rnd, g, phase, 3, chunk(rnd, g, phase, 2, 1), -1),
                1: ring(rnd, g, phase, 1, chunk(rnd, g, phase, 1, 1), 1),
                4: ring(rnd, g, phase, 4, chunk(rnd, g, phase, -1, 0), -1),
            }
            return
        flying[rnd, g] = {
            n: ring(rnd, g, phase, n, chunk(rnd, g, phase, n + 1, slice(None)), n + 1) for n in range(3)
        }

    def ring_relay(rnd):
        for g in range(len(ORDERS[rnd])):
            land = landing[rnd, g, 0]
            for number, step, half, slot in ((0, 1, 0, 6), (3, -1, 1, 7)):
                flying[rnd, g][number].wait_recv()
                land[slot][...] = (
                    land[number][...].astype(F32) + chunk(rnd, g, 0, step, half)[...].astype(F32)
                ).astype(BF)
                flying[rnd, g][number + 2] = ring(rnd, g, 0, number + 2, land[slot], step)

    def ring_end(rnd, phase):
        for g in range(len(ORDERS[rnd])):
            land = landing[rnd, g, phase]
            copies = flying[rnd, g]
            if phase == 0:
                for number in (1, 4, 2, 5):
                    copies[number].wait()
                copies[0].wait_send()
                copies[3].wait_send()
                for half, near, far in ((0, 4, 2), (1, 1, 5)):
                    middles[rnd, g, phase][half] = (
                        chunk(rnd, g, phase, 0, half)[...].astype(F32)
                        + land[near][...].astype(F32)
                        + land[far][...].astype(F32)
                    ).astype(BF)
                ring_start_group(rnd, g, 1)
                continue
            for number in range(3):
                copies[number].wait()
            value = chunk(rnd, g, phase, 0, slice(None))[...].astype(F32)
            for number in range(3):
                value = value + land[number][...].astype(F32)
            value = value.astype(BF)
            if phase == 1:
                middles[rnd, g, phase][...] = value
                ring_start_group(rnd, g, 2)
                continue
            kind, first, _ = PIECES[rnd][g]
            target = gi_out if kind == "in" else go_out
            for half in range(2):
                at = first + half * FIRST
                target[:, at : at + FIRST] = value[half, :8]
                target[:, at + LANES : at + LANES + FIRST] = value[half, 8:]

    def gain_start(stage):
        if stage == 0:
            return [remote(gain_mine.at[0], gain_land.at[0], gain_send.at[0], gain_recv.at[0], sibling)]
        return [
            remote(
                gain_mine.at[stage],
                gain_land.at[3 * stage - 2 + n],
                gain_send.at[3 * stage - 2 + n],
                gain_recv.at[3 * stage - 2 + n],
                device(AXES[stage - 1], n + 1),
            )
            for n in range(3)
        ]

    def gain_finish(stage, copies):
        total = gain_mine[stage]
        for copy in copies:
            copy.wait()
        if stage == 0:
            return total + gain_land[0]
        slot = 3 * stage - 2
        return total + gain_land[slot] + gain_land[slot + 1] + gain_land[slot + 2]

    def attended_step(s):
        rows = slice(s * PAIR, (s + 1) * PAIR)
        attended = dot(gctx[rows], wout[...]).astype(BF).astype(F32)
        xw_out[rows] = (xw[rows].astype(F32) + attended).astype(BF)

    def grad_step(s):
        rows = slice(s * PAIR, (s + 1) * PAIR)
        grad = dg(proj[rows], win[...], NT).astype(BF).astype(F32)
        standard, inverse = standardised(xw[rows].astype(F32))
        scaled = grad * gain_ref[...]
        first = jnp.mean(scaled, axis=-1, keepdims=True)
        second = jnp.mean(scaled * standard, axis=-1, keepdims=True)
        local = inverse * (scaled - first - standard * second)
        cw[rows] = (cw[rows].astype(F32) + local).astype(BF)
        return jnp.sum(grad * standard, axis=0, keepdims=True)

    def pack_back(number, final):
        both = dot(r1_ref[...], final[PAIR : 2 * PAIR]).astype(BF)
        send_strip[number][0:144] = both[:144]
        send_strip[number][304:400] = both[144:]
        send_strip[number][144:304] = dot(r2_ref[...], final[2 * PAIR :]).astype(BF)
        return send_strips(number, -1)

    def assemble(own, final, strip):
        value = dot(
            imid_ref[...], jnp.concatenate([final[:PAIR], final[2 * PAIR :], strip[144:304]], 0)
        ).astype(BF)
        own[72:360] = value[:288]
        own[504:792] = value[288:]
        value = dot(ibot_ref[...], jnp.concatenate([final[PAIR : 2 * PAIR], strip[304:352]], 0)).astype(BF)
        own[360:432] = value[:72]
        own[792:864] = value[72:]
        value = dot(itop_ref[...], jnp.concatenate([strip[0:144], strip[352:400]], 0)).astype(BF)
        own[0:72] = value[:72]
        own[432:504] = value[72:]

    xw_out = nw

    loads[3].wait()
    gather_tokens(0)
    gather_cotangent(0)
    loads[4].wait()
    mask[...] = jnp.where(lat == 3, 1.0, 0.0) * mask_ref[...]

    def turn(p, _):
        for h in range(4):
            bias[p, :, h * WINT : (h + 1) * WINT] = raw[4 * p + h].T
        return 0

    lax.fori_loop(0, 4, turn, 0)
    loads[5].wait()
    project(0, PAIR)
    loads[6].wait()
    project_back(0, PAIR)
    for load in loads[7:]:
        load.start()

    def early(p, _):
        unit(0, p, False)
        unit(1, p, False)
        return 0

    lax.fori_loop(0, 4, early, 0)
    for load in loads[7:]:
        load.wait()
    for copy in strip_copies[0]:
        copy.wait()
    gather_tokens(1)
    gather_tokens(2)
    project(1, 2 * PAIR)

    def turn_rows(n, _):
        at = pl.ds(pl.multiple_of(n * 256, 256), 256)
        nwt[at, :] = nw[:, at].T
        return 0

    lax.fori_loop(0, 4, turn_rows, 0)
    for copy in strip_copies[1]:
        copy.wait()
    gather_cotangent(1)
    gather_cotangent(2)
    project_back(1, 2 * PAIR)

    def first_pairs(p, _):
        late_windows(p, 0)
        late_windows(p, 1)
        return 0

    lax.fori_loop(0, 2, first_pairs, 0)
    start_round(0)
    own_products(0)
    for p in (2, 3):
        for t in range(2):
            late_windows(p, t)
    start_round(1)
    end_core(0)
    own_products(1)

    def turn_context(n, _):
        at = pl.ds(pl.multiple_of(n * 256, 256), 256)
        nwt[at, :] = gctx[:, at].T
        return 0

    lax.fori_loop(0, 4, turn_context, 0)
    start_round(2)
    attended_step(1)
    attended_step(2)
    back_out = pack_back(2, xw_out)
    ring_relay(0)
    end_core(1)
    own_products(2)
    gain = grad_step(1)
    end_core(2)
    ring_end(0, 0)
    gain += grad_step(2)
    back_grad = pack_back(3, cw)
    ring_relay(1)
    gain += grad_step(0)
    for n in range(8):
        gain_mine[0, n : n + 1, :] = gain[:, n * 128 : (n + 1) * 128]
    gain_copies = gain_start(0)
    ring_relay(2)
    ring_end(0, 1)
    attended_step(0)
    ring_end(1, 0)
    gain_mine[1] = gain_finish(0, gain_copies)
    gain_copies = gain_start(1)
    for copy in back_out:
        copy.wait()
    assemble(own_x, xw_out, recv_strip[2])
    store_out = pltpu.make_async_copy(own_x, out_hbm, load_sem.at[0])
    store_out.start()
    ring_end(2, 0)
    gain_mine[2] = gain_finish(1, gain_copies)
    gain_copies = gain_start(2)
    ring_end(1, 1)
    for copy in back_grad:
        copy.wait()
    assemble(own_c, cw, recv_strip[3])
    store_grad = pltpu.make_async_copy(own_c, gt_hbm, load_sem.at[1])
    store_grad.start()
    ring_end(2, 1)
    gain_mine[3] = gain_finish(2, gain_copies)
    gain_copies = gain_start(3)
    ring_end(0, 2)
    ring_end(1, 2)
    ring_end(2, 2)
    gg_out[...] = gain_finish(3, gain_copies)
    store_out.wait()
    store_grad.wait()


def block(tokens, cotangent, gain, attention_in, attention_out, head_bias):
    vm = pl.BlockSpec(memory_space=pltpu.VMEM)
    hbm = pl.BlockSpec(memory_space=pl.ANY)
    perms = [jnp.asarray(m, BF) for m in permutations()]
    wide = lambda rows, columns=D: pltpu.VMEM((rows, columns), BF)
    scratch = [wide(OWN) for _ in range(5)]
    scratch += [wide(D, OWN), wide(OWN, 3 * D), wide(OWN), wide(D, 3 * D), wide(D)]
    scratch += [pltpu.VMEM((16, WINT, WINT), F32), pltpu.VMEM((4, WINT, 4 * WINT), F32), pltpu.VMEM((WINT, 4 * WINT), F32)]
    scratch += [wide(*m.shape[1:]) for m in perms]
    scratch += [wide(STRIP) for _ in range(6)]
    scratch += [pltpu.VMEM((2, 4, 4, 4, 16, FIRST), BF) for _ in range(3 * len(GROUPS))]
    middles = []
    for r, g in GROUPS:
        for phase in range(3):
            lead = (4,) * (2 - phase)
            if phase == 0:
                scratch += [pltpu.VMEM(lead + (16, FIRST), BF) for _ in range(8)]
            else:
                scratch += [pltpu.VMEM((2,) + lead + (16, FIRST), BF) for _ in range(3)]
            if phase < 2:
                middles.append(pltpu.VMEM((2,) + lead + (16, FIRST), BF))
    scratch += middles
    scratch += [pltpu.VMEM((4, 8, 128), F32), pltpu.VMEM((10, 8, 128), F32)]
    dma = pltpu.SemaphoreType.DMA
    scratch += [dma((14,)), dma((4, 5)), dma((4, 5)), dma((3, 3)), dma((3, 3))]
    scratch += [dma((3, 3, 3, 6)), dma((3, 3, 3, 6)), dma((10,)), dma((10,))]
    return pl.pallas_call(
        block_kernel,
        in_specs=[hbm, hbm, vm, hbm, hbm, hbm, vm] + [hbm] * 9,
        out_specs=[hbm, hbm, vm, vm, vm],
        out_shape=[
            jax.ShapeDtypeStruct((OWN, D), BF),
            jax.ShapeDtypeStruct((OWN, D), BF),
            jax.ShapeDtypeStruct((8, 3 * D), BF),
            jax.ShapeDtypeStruct((8, D), BF),
            jax.ShapeDtypeStruct((8, 128), F32),
        ],
        scratch_shapes=scratch,
        compiler_params=pltpu.CompilerParams(
            collective_id=0, has_side_effects=True, vmem_limit_bytes=63 * 2**20
        ),
    )(
        tokens, cotangent, gain.reshape(1, D), attention_in, attention_out, head_bias,
        jnp.asarray(region_mask()), *perms,
    )


def finish_kernel(out_ref, gt_ref, gi_ref, go_ref, gg_ref, out_final, gt_final, gi_final, go_final, gain_final):
    out_final[...] = out_ref[...]
    gt_final[...] = gt_ref[...]
    gi_final[...] = gi_ref[...]
    go_final[...] = go_ref[...]
    at = (lax.axis_index("lat") * 32 + lax.axis_index("lon")) * 8
    place = lax.broadcasted_iota(jnp.int32, (8, 128), 0) * 128 + lax.broadcasted_iota(jnp.int32, (8, 128), 1)
    for n in range(8):
        gain_final[n] = jnp.sum(jnp.where(place == at + n, gg_ref[...], 0.0))


def finish(*results):
    vm = pl.BlockSpec(memory_space=pltpu.VMEM)
    rows = pl.BlockSpec((PAIR, D), lambda i: (i, 0))
    return pl.pallas_call(
        finish_kernel,
        grid=(3,),
        in_specs=[rows, rows, vm, vm, vm],
        out_specs=[rows, rows, vm, vm, pl.BlockSpec(memory_space=pltpu.SMEM)],
        out_shape=[
            jax.ShapeDtypeStruct((OWN, D), BF),
            jax.ShapeDtypeStruct((OWN, D), BF),
            jax.ShapeDtypeStruct((8, 3 * D), BF),
            jax.ShapeDtypeStruct((8, D), BF),
            jax.ShapeDtypeStruct((8,), F32),
        ],
    )(*results)


def local(tokens, norm_gain, attention_in, attention_out, head_bias, cotangent):
    shape = tokens.shape
    out, gt, gi, go, gain = finish(
        *block(
            tokens.reshape(OWN, D), cotangent.reshape(OWN, D), norm_gain, attention_in, attention_out, head_bias
        )
    )
    return out.reshape(shape), gt.reshape(shape), gi, go, gain


def solution(mesh):
    split = P(None, "lat", "lon", None)
    both = ("lat", "lon")
    return jax.shard_map(
        local,
        mesh=mesh,
        in_specs=(split, P(), P(), P(), P(), split),
        out_specs=(split, split, P(both, None), P(both, None), P(both)),
        check_vma=False,
    )
```

```python
import jax
import jax.numpy as jnp
import numpy as np
from jax import lax
from jax.experimental import pallas as pl
from jax.experimental.pallas import tpu as pltpu
from jax.sharding import PartitionSpec as P

D = 1024
WINT = 144
PAIR = 288
OWN = 864
STRIP = 400
NT = (((1,), (1,)), ((), ()))
TN = (((0,), (0,)), ((), ()))
BF = jnp.bfloat16
F32 = jnp.float32

AXES = ("x", "y", "z")
ORDERS = (
    (("x", "y", "z"), ("y", "z", "x"), ("z", "x", "y")),
    (("x", "y", "z"), ("y", "z", "x"), ("z", "x", "y")),
    (("x", "z", "y"), ("z", "x", "y")),
)
PIECES = (
    tuple(("in", 1024 * g, 512) for g in range(3)),
    tuple(("in", 1024 * g + 512, 512) for g in range(3)),
    tuple(("out", 512 * g, 512) for g in range(2)),
)
LANES = 256
FIRST = 128
GROUPS = tuple((r, g) for r in range(3) for g in range(len(ORDERS[r])))


def strip_cells(core):
    cells = [(l, r, c) for l in range(2) for r in range(3) for c in range(24)]
    cells += [(l, r, c) for l in range(2) for r in range(3, 9) for c in range(18, 24)] + [None] * 8
    first = 0 if core else 18
    cells += [(l, r, c) for l in range(2) for r in range(9, 15) for c in range(first, first + 6)] + [None] * 8
    cells += [(l, r, c) for l in range(2) for r in range(15, 18) for c in range(6)] + [None] * 12
    cells += [(l, r, c) for l in range(2) for r in range(3) for c in range(6)] + [None] * 12
    return cells


def received_cells(core):
    cells = []
    for n, cell in enumerate(strip_cells(core)):
        if cell is None:
            cells.append(None)
            continue
        l, r, c = cell
        if n < 144 or n >= 352:
            r += 18
        if n >= 144:
            c += 24 if c < 6 else -24
        cells.append((l, r, c))
    return cells


def window_cells(core):
    corners = ((3, 6), (9, 6), (15, 6), (15, 18), (3, -6), (9, 18 if core else -6))
    return [(l, r + a, c + b) for r, c in corners for l in range(2) for a in range(6) for b in range(12)]


def one_hot(targets, sources):
    place = {}
    for n, cell in enumerate(sources):
        if cell is not None and cell not in place:
            place[cell] = n
    out = np.zeros((len(targets), len(sources)), np.float32)
    for n, cell in enumerate(targets):
        if cell is not None and cell in place:
            out[n, place[cell]] = 1
    return out


def permutations():
    own = [(l, r, c) for l in range(2) for r in range(18) for c in range(24)]
    wide = own[64:368] + own[496:800]
    mid = own[72:360] + own[504:792]
    bottom = own[360:432] + own[792:864]
    top = own[:72] + own[432:504]
    every = []
    for core in range(2):
        strips = strip_cells(core)
        got = received_cells(core)
        win = window_cells(core)
        inner = [c if c is not None and c[2] >= 6 else None for c in strips[:144]]
        every.append(
            (
                one_hot(strips, own),
                one_hot(win[:288], wide),
                one_hot(win[288:576], own[352:432] + own[784:864] + got[:144] + got[304:]),
                one_hot(win[576:], wide + got[144:304]),
                one_hot(got[:144] + got[304:], win[288:576]),
                one_hot(got[144:304], win[576:]),
                one_hot(mid, win[:288] + win[576:] + strips[144:304]),
                one_hot(bottom, win[288:576] + strips[304:352]),
                one_hot(top, inner + strips[352:]),
            )
        )
    return tuple(np.stack(pair) for pair in zip(*every))


def region_mask():
    region = np.array([a < 3 for l in range(2) for a in range(6) for b in range(12)])
    one = np.where(region[:, None] == region[None, :], 0.0, -1e9).astype(np.float32)
    return np.concatenate([one] * 4, 1)


def dg(a, b, dims):
    return lax.dot_general(a, b, dims, preferred_element_type=F32)


def dot(a, b):
    return jnp.dot(a, b, preferred_element_type=F32)


def mesh_place(core, x, y, z):
    return ((z % 2) * 2 + core, (z // 2) * 16 + x * 4 + y)


def block_kernel(
    tok_hbm, cot_hbm, gain_ref, win_hbm, wout_hbm, hb_hbm, mask_ref,
    pack_hbm, p0_hbm, p1_hbm, p2_hbm, r1_hbm, r2_hbm, imid_hbm, ibot_hbm, itop_hbm,
    out_hbm, gt_hbm, gi_out, go_out, gg_out,
    *scratch,
):
    scratch = list(scratch)

    def take(count):
        out = scratch[:count]
        del scratch[:count]
        return out

    own_x, own_c, xw, cw, nw, nwt, proj, gctx, win, wout, raw, bias, mask = take(13)
    perms = take(9)
    pack_ref, p0_ref, p1_ref, p2_ref, r1_ref, r2_ref, imid_ref, ibot_ref, itop_ref = perms
    send_strip, recv_strip = take(2) * 2, take(4)
    sends = {at: take(1)[0] for at in GROUPS}
    owns = {at: take(1)[0] for at in GROUPS}
    halves = {at: take(1)[0] for at in GROUPS}
    landing = {(r, g, p): take(3 if p else 8) for r, g in GROUPS for p in range(3)}
    middles = {(r, g, p): take(1)[0] for r, g in GROUPS for p in range(2)}
    gain_mine, gain_land = take(2)
    load_sem, strip_send, strip_recv, core_send, core_recv = take(5)
    ring_send, ring_recv, gain_send, gain_recv = take(4)

    lat = lax.axis_index("lat")
    lon = lax.axis_index("lon")
    core = lat % 2
    me = {"x": (lon // 4) % 4, "y": lon % 4, "z": (lon // 16) * 2 + lat // 2}

    def device(axis, step):
        at = dict(me)
        at[axis] = (me[axis] + step + 4) % 4
        return mesh_place(core, at["x"], at["y"], at["z"])

    sibling = mesh_place(1 - core, me["x"], me["y"], me["z"])

    def grid_place(a, b):
        return ((lat + a + 4) % 4, (lon + b + 32) % 32)

    loads = [
        pltpu.make_async_copy(src, dst, load_sem.at[n])
        for n, (src, dst) in enumerate(
            (
                (tok_hbm, own_x), (pack_hbm.at[core], pack_ref), (cot_hbm, own_c), (p0_hbm.at[core], p0_ref),
                (hb_hbm, raw), (win_hbm, win), (wout_hbm, wout), (p1_hbm.at[core], p1_ref), (p2_hbm.at[core], p2_ref),
                (r1_hbm.at[core], r1_ref), (r2_hbm.at[core], r2_ref), (imid_hbm.at[core], imid_ref),
                (ibot_hbm.at[core], ibot_ref), (itop_hbm.at[core], itop_ref),
            )
        )
    ]
    for load in loads[:4]:
        load.start()

    barrier = pltpu.get_barrier_semaphore()
    partners = [sibling] + [device(a, s) for a in AXES for s in (1, -1, 2)]
    partners += [grid_place(s * a, s * b) for a, b in ((1, 0), (0, 1), (1, 1)) for s in (1, -1)]
    for other in partners:
        pl.semaphore_signal(barrier, inc=1, device_id=other, device_id_type=pl.DeviceIdType.MESH)
    pl.semaphore_wait(barrier, len(partners))

    def remote(src, dst, send, recv, place):
        copy = pltpu.make_async_remote_copy(
            src_ref=src,
            dst_ref=dst,
            send_sem=send,
            recv_sem=recv,
            device_id=place,
            device_id_type=pl.DeviceIdType.MESH,
        )
        copy.start()
        return copy

    turned = jnp.where(core == 0, 1, -1)
    PARTS = ((0, 144, -1, 0), (144, 80, 0, 1), (224, 80, 0, turned), (304, 48, 0, -1), (352, 48, -1, -1))

    def send_strips(number, way, parts=range(5)):
        copies = []
        for part in parts:
            low, size, a, b = PARTS[part]
            copies.append(
                remote(
                    send_strip[number].at[pl.ds(low, size)],
                    recv_strip[number].at[pl.ds(low, size)],
                    strip_send.at[number, part],
                    strip_recv.at[number, part],
                    grid_place(way * a, way * b),
                )
            )
        return copies

    strip_copies = []
    loads[0].wait()
    loads[1].wait()
    for load in loads[4:7]:
        load.start()
    for number, own in ((0, own_x), (1, own_c)):
        if number == 1:
            loads[2].wait()
        send_strip[number][...] = dot(pack_ref[...], own[...]).astype(BF)
        strip_copies.append(send_strips(number, 1))

    def gathered(own, strip, s):
        if s == 1:
            parts = [own[352:432], own[784:864], strip[0:144], strip[304:400]]
            return dot(p1_ref[...], jnp.concatenate(parts, 0))
        parts = [own[64:368], own[496:800]]
        if s == 0:
            return dot(p0_ref[...], jnp.concatenate(parts, 0))
        return dot(p2_ref[...], jnp.concatenate(parts + [strip[144:304]], 0))

    def standardised(x):
        centred = x - jnp.mean(x, axis=-1, keepdims=True)
        inverse = lax.rsqrt(jnp.mean(centred * centred, axis=-1, keepdims=True) + 1e-5)
        return centred * inverse, inverse

    def gather_tokens(s):
        rows = slice(s * PAIR, (s + 1) * PAIR)
        x = gathered(own_x, recv_strip[0], s)
        xw[rows] = x.astype(BF)
        standard, _ = standardised(x)
        nw[rows] = (standard * gain_ref[...]).astype(BF)

    def gather_cotangent(s):
        rows = slice(s * PAIR, (s + 1) * PAIR)
        cw[rows] = gathered(own_c, recv_strip[1], s).astype(BF)

    def project(s, count):
        rows = slice(s * PAIR, s * PAIR + count)

        def columns(n, _):
            at = pl.ds(pl.multiple_of(n * 512, 512), 512)
            value = dot(nw[rows], win[:, at])
            proj[rows, at] = (value * jnp.where(n < 2, 0.125, 1.0)).astype(BF)
            return 0

        lax.fori_loop(0, 6, columns, 0)

    def project_back(s, count):
        rows = slice(s * PAIR, s * PAIR + count)

        def outer(n, _):
            at = pl.ds(pl.multiple_of(n * 512, 512), 512)
            gctx[rows, at] = dg(cw[rows], wout[at, :], NT).astype(BF)
            return 0

        lax.fori_loop(0, 2, outer, 0)

    head = lax.broadcasted_iota(jnp.int32, (WINT, 256), 1) // 64
    low_half = lax.broadcasted_iota(jnp.int32, (WINT, 128), 1) < 64
    zero = jnp.zeros((WINT, 256), BF)

    def stacked(a):
        return jnp.concatenate([jnp.where(head == h, a, zero) for h in range(4)], 0)

    def by_query(scores, a):
        turned = scores.T
        parts = []
        for n in range(2):
            both = dot(turned[n * PAIR : (n + 1) * PAIR], a[:, n * 128 : (n + 1) * 128])
            parts.append(jnp.where(low_half, both[:WINT], both[WINT:]))
        return jnp.concatenate(parts, 1)

    def unit(w, p, masked):
        rows = pl.ds(pl.multiple_of(w * WINT, 16), WINT)
        at_q = pl.ds(pl.multiple_of(p * 256, 256), 256)
        at_k = pl.ds(pl.multiple_of(1024 + p * 256, 256), 256)
        at_v = pl.ds(pl.multiple_of(2048 + p * 256, 256), 256)
        q, k, v, d = proj[rows, at_q], proj[rows, at_k], proj[rows, at_v], gctx[rows, at_q]
        qs, ds = stacked(q), stacked(d)
        offset = bias[p]
        if masked:
            offset = offset + mask[...]
        st = dg(k, qs, NT) + offset
        powers = jnp.exp(st - jnp.max(st, axis=0, keepdims=True))
        weights = powers * (1.0 / jnp.sum(powers, axis=0, keepdims=True))
        wb = weights.astype(BF)
        dw = dg(v, ds, NT)
        inner = jnp.sum(dw * weights, axis=0, keepdims=True)
        gs = (weights * (dw - inner)).astype(BF)
        gctx[rows, at_q] = by_query(wb, v).astype(BF)
        proj[rows, at_q] = (by_query(gs, k) * 0.125).astype(BF)
        proj[rows, at_k] = dot(gs, qs).astype(BF)
        proj[rows, at_v] = dot(wb, ds).astype(BF)

    def late_windows(p, t):
        unit(2 + 2 * t, p, t == 0)
        unit(3 + 2 * t, p, t == 0)

    def products(rnd, g, half, target):
        kind, first, width = PIECES[rnd][g]
        right = proj if kind == "in" else cw

        order = ORDERS[rnd][g]

        def rows_of(zl, _):
            at = pl.multiple_of(zl * 512 + half * 256, 256)
            value = dot(nwt[pl.ds(at, 256), :], right[:, first : first + width]).reshape(32, 8, width)
            both = jnp.concatenate([value[:, :, :LANES], value[:, :, LANES:]], 1).astype(BF)
            both = both.reshape(2, 4, 4, 16, LANES)
            for zh in range(2):
                z = 2 * zh + zl
                for end in range(2):
                    part = both[zh, :, :, :, end * FIRST : (end + 1) * FIRST]
                    if order.index("y") < order.index("x"):
                        part = jnp.swapaxes(part, 0, 1)
                    place = [end, slice(None), slice(None), slice(None)]
                    place[1 + order.index("z")] = z
                    target[tuple(place)] = part
            return 0

        lax.fori_loop(0, 2, rows_of, 0)

    core_copies = {}

    def start_round(rnd):
        for g in range(len(ORDERS[rnd])):
            products(rnd, g, 1 - core, sends[rnd, g])
            core_copies[rnd, g] = remote(
                sends[rnd, g], halves[rnd, g], core_send.at[rnd, g], core_recv.at[rnd, g], sibling
            )

    def own_products(rnd):
        for g in range(len(ORDERS[rnd])):
            products(rnd, g, core, owns[rnd, g])

    def end_core(rnd):
        for g in range(len(ORDERS[rnd])):
            core_copies[rnd, g].wait()
            mine = owns[rnd, g]
            mine[...] = (mine[...].astype(F32) + halves[rnd, g][...].astype(F32)).astype(BF)
            ring_start_group(rnd, g, 0)

    def chunk(rnd, g, phase, step, half):
        ref = owns[rnd, g] if phase == 0 else middles[rnd, g, phase - 1]
        return ref.at[half, (me[ORDERS[rnd][g][phase]] + step + 4) % 4]

    def ring(rnd, g, phase, number, src, step):
        return remote(
            src,
            landing[rnd, g, phase][number],
            ring_send.at[GROUPS.index((rnd, g)), (0, 6, 9)[phase] + number],
            ring_recv.at[GROUPS.index((rnd, g)), (0, 6, 9)[phase] + number],
            device(ORDERS[rnd][g][phase], step),
        )

    flying = {}

    def ring_start_group(rnd, g, phase):
        if phase == 0:
            flying[rnd, g] = {
                0: ring(rnd, g, phase, 0, chunk(rnd, g, phase, 2, 0), 1),
                3: ring(rnd, g, phase, 3, chunk(rnd, g, phase, 2, 1), -1),
                1: ring(rnd, g, phase, 1, chunk(rnd, g, phase, 1, 1), 1),
                4: ring(rnd, g, phase, 4, chunk(rnd, g, phase, -1, 0), -1),
            }
            return
        flying[rnd, g] = {
            n: ring(rnd, g, phase, n, chunk(rnd, g, phase, n + 1, slice(None)), n + 1) for n in range(3)
        }

    def ring_relay(rnd):
        for g in range(len(ORDERS[rnd])):
            land = landing[rnd, g, 0]
            for number, step, half, slot in ((0, 1, 0, 6), (3, -1, 1, 7)):
                flying[rnd, g][number].wait_recv()
                land[slot][...] = (
                    land[number][...].astype(F32) + chunk(rnd, g, 0, step, half)[...].astype(F32)
                ).astype(BF)
                flying[rnd, g][number + 2] = ring(rnd, g, 0, number + 2, land[slot], step)

    def ring_end(rnd, phase):
        for g in range(len(ORDERS[rnd])):
            land = landing[rnd, g, phase]
            copies = flying[rnd, g]
            if phase == 0:
                for number in (1, 4, 2, 5):
                    copies[number].wait()
                copies[0].wait_send()
                copies[3].wait_send()
                for half, near, far in ((0, 4, 2), (1, 1, 5)):
                    middles[rnd, g, phase][half] = (
                        chunk(rnd, g, phase, 0, half)[...].astype(F32)
                        + land[near][...].astype(F32)
                        + land[far][...].astype(F32)
                    ).astype(BF)
                ring_start_group(rnd, g, 1)
                continue
            for number in range(3):
                copies[number].wait()
            value = chunk(rnd, g, phase, 0, slice(None))[...].astype(F32)
            for number in range(3):
                value = value + land[number][...].astype(F32)
            value = value.astype(BF)
            if phase == 1:
                middles[rnd, g, phase][...] = value
                ring_start_group(rnd, g, 2)
                continue
            kind, first, _ = PIECES[rnd][g]
            target = gi_out if kind == "in" else go_out
            for half in range(2):
                at = first + half * FIRST
                target[:, at : at + FIRST] = value[half, :8]
                target[:, at + LANES : at + LANES + FIRST] = value[half, 8:]

    def gain_start(stage):
        if stage == 0:
            return [remote(gain_mine.at[0], gain_land.at[0], gain_send.at[0], gain_recv.at[0], sibling)]
        return [
            remote(
                gain_mine.at[stage],
                gain_land.at[3 * stage - 2 + n],
                gain_send.at[3 * stage - 2 + n],
                gain_recv.at[3 * stage - 2 + n],
                device(AXES[stage - 1], n + 1),
            )
            for n in range(3)
        ]

    def gain_finish(stage, copies):
        total = gain_mine[stage]
        for copy in copies:
            copy.wait()
        if stage == 0:
            return total + gain_land[0]
        slot = 3 * stage - 2
        return total + gain_land[slot] + gain_land[slot + 1] + gain_land[slot + 2]

    def attended_step(s):
        rows = slice(s * PAIR, (s + 1) * PAIR)
        attended = dot(gctx[rows], wout[...]).astype(BF).astype(F32)
        xw_out[rows] = (xw[rows].astype(F32) + attended).astype(BF)

    def grad_step(s):
        rows = slice(s * PAIR, (s + 1) * PAIR)
        grad = dg(proj[rows], win[...], NT).astype(BF).astype(F32)
        standard, inverse = standardised(xw[rows].astype(F32))
        scaled = grad * gain_ref[...]
        first = jnp.mean(scaled, axis=-1, keepdims=True)
        second = jnp.mean(scaled * standard, axis=-1, keepdims=True)
        local = inverse * (scaled - first - standard * second)
        cw[rows] = (cw[rows].astype(F32) + local).astype(BF)
        return jnp.sum(grad * standard, axis=0, keepdims=True)

    def pack_back(number, final):
        both = dot(r1_ref[...], final[PAIR : 2 * PAIR]).astype(BF)
        send_strip[number][0:144] = both[:144]
        send_strip[number][304:400] = both[144:]
        send_strip[number][144:304] = dot(r2_ref[...], final[2 * PAIR :]).astype(BF)
        return send_strips(number, -1)

    def assemble(own, final, strip):
        value = dot(
            imid_ref[...], jnp.concatenate([final[:PAIR], final[2 * PAIR :], strip[144:304]], 0)
        ).astype(BF)
        own[72:360] = value[:288]
        own[504:792] = value[288:]
        value = dot(ibot_ref[...], jnp.concatenate([final[PAIR : 2 * PAIR], strip[304:352]], 0)).astype(BF)
        own[360:432] = value[:72]
        own[792:864] = value[72:]
        value = dot(itop_ref[...], jnp.concatenate([strip[0:144], strip[352:400]], 0)).astype(BF)
        own[0:72] = value[:72]
        own[432:504] = value[72:]

    xw_out = nw

    loads[3].wait()
    gather_tokens(0)
    gather_cotangent(0)
    loads[4].wait()
    mask[...] = jnp.where(lat == 3, 1.0, 0.0) * mask_ref[...]

    def turn(p, _):
        for h in range(4):
            bias[p, :, h * WINT : (h + 1) * WINT] = raw[4 * p + h].T
        return 0

    lax.fori_loop(0, 4, turn, 0)
    loads[5].wait()
    project(0, PAIR)
    loads[6].wait()
    project_back(0, PAIR)
    for load in loads[7:]:
        load.start()

    def early(p, _):
        unit(0, p, False)
        unit(1, p, False)
        return 0

    lax.fori_loop(0, 4, early, 0)
    for load in loads[7:]:
        load.wait()
    for copy in strip_copies[0]:
        copy.wait()
    gather_tokens(1)
    gather_tokens(2)
    project(1, 2 * PAIR)

    def turn_rows(n, _):
        at = pl.ds(pl.multiple_of(n * 256, 256), 256)
        nwt[at, :] = nw[:, at].T
        return 0

    lax.fori_loop(0, 4, turn_rows, 0)
    for copy in strip_copies[1]:
        copy.wait()
    gather_cotangent(1)
    gather_cotangent(2)
    project_back(1, 2 * PAIR)

    def first_pairs(p, _):
        late_windows(p, 0)
        late_windows(p, 1)
        return 0

    lax.fori_loop(0, 2, first_pairs, 0)
    start_round(0)
    own_products(0)
    for p in (2, 3):
        for t in range(2):
            late_windows(p, t)
    start_round(1)
    end_core(0)
    own_products(1)

    def turn_context(n, _):
        at = pl.ds(pl.multiple_of(n * 256, 256), 256)
        nwt[at, :] = gctx[:, at].T
        return 0

    lax.fori_loop(0, 4, turn_context, 0)
    start_round(2)
    own_products(2)
    end_core(1)
    ring_relay(0)
    attended_step(1)
    attended_step(2)
    back_out = pack_back(2, xw_out)
    end_core(2)
    gain = grad_step(1)
    ring_relay(1)
    ring_end(0, 0)
    gain += grad_step(2)
    back_grad = pack_back(3, cw)
    ring_relay(2)
    ring_end(1, 0)
    gain += grad_step(0)
    for n in range(8):
        gain_mine[0, n : n + 1, :] = gain[:, n * 128 : (n + 1) * 128]
    gain_copies = gain_start(0)
    ring_end(0, 1)
    ring_end(2, 0)
    attended_step(0)
    gain_mine[1] = gain_finish(0, gain_copies)
    gain_copies = gain_start(1)
    ring_end(1, 1)
    for copy in back_out:
        copy.wait()
    assemble(own_x, xw_out, recv_strip[2])
    store_out = pltpu.make_async_copy(own_x, out_hbm, load_sem.at[0])
    store_out.start()
    gain_mine[2] = gain_finish(1, gain_copies)
    gain_copies = gain_start(2)
    ring_end(2, 1)
    for copy in back_grad:
        copy.wait()
    assemble(own_c, cw, recv_strip[3])
    store_grad = pltpu.make_async_copy(own_c, gt_hbm, load_sem.at[1])
    store_grad.start()
    gain_mine[3] = gain_finish(2, gain_copies)
    gain_copies = gain_start(3)
    ring_end(0, 2)
    ring_end(1, 2)
    ring_end(2, 2)
    gg_out[...] = gain_finish(3, gain_copies)
    store_out.wait()
    store_grad.wait()


def block(tokens, cotangent, gain, attention_in, attention_out, head_bias):
    vm = pl.BlockSpec(memory_space=pltpu.VMEM)
    hbm = pl.BlockSpec(memory_space=pl.ANY)
    perms = [jnp.asarray(m, BF) for m in permutations()]
    wide = lambda rows, columns=D: pltpu.VMEM((rows, columns), BF)
    scratch = [wide(OWN) for _ in range(5)]
    scratch += [wide(D, OWN), wide(OWN, 3 * D), wide(OWN), wide(D, 3 * D), wide(D)]
    scratch += [pltpu.VMEM((16, WINT, WINT), F32), pltpu.VMEM((4, WINT, 4 * WINT), F32), pltpu.VMEM((WINT, 4 * WINT), F32)]
    scratch += [wide(*m.shape[1:]) for m in perms]
    scratch += [wide(STRIP) for _ in range(6)]
    scratch += [pltpu.VMEM((2, 4, 4, 4, 16, FIRST), BF) for _ in range(3 * len(GROUPS))]
    middles = []
    for r, g in GROUPS:
        for phase in range(3):
            lead = (4,) * (2 - phase)
            if phase == 0:
                scratch += [pltpu.VMEM(lead + (16, FIRST), BF) for _ in range(8)]
            else:
                scratch += [pltpu.VMEM((2,) + lead + (16, FIRST), BF) for _ in range(3)]
            if phase < 2:
                middles.append(pltpu.VMEM((2,) + lead + (16, FIRST), BF))
    scratch += middles
    scratch += [pltpu.VMEM((4, 8, 128), F32), pltpu.VMEM((10, 8, 128), F32)]
    dma = pltpu.SemaphoreType.DMA
    scratch += [dma((14,)), dma((4, 5)), dma((4, 5)), dma((3, 3)), dma((3, 3))]
    scratch += [dma((len(GROUPS), 12)), dma((len(GROUPS), 12)), dma((10,)), dma((10,))]
    return pl.pallas_call(
        block_kernel,
        in_specs=[hbm, hbm, vm, hbm, hbm, hbm, vm] + [hbm] * 9,
        out_specs=[hbm, hbm, vm, vm, vm],
        out_shape=[
            jax.ShapeDtypeStruct((OWN, D), BF),
            jax.ShapeDtypeStruct((OWN, D), BF),
            jax.ShapeDtypeStruct((8, 3 * D), BF),
            jax.ShapeDtypeStruct((8, D), BF),
            jax.ShapeDtypeStruct((8, 128), F32),
        ],
        scratch_shapes=scratch,
        compiler_params=pltpu.CompilerParams(
            collective_id=0, has_side_effects=True, vmem_limit_bytes=63 * 2**20
        ),
    )(
        tokens, cotangent, gain.reshape(1, D), attention_in, attention_out, head_bias,
        jnp.asarray(region_mask()), *perms,
    )


def finish_kernel(out_ref, gt_ref, gi_ref, go_ref, gg_ref, out_final, gt_final, gi_final, go_final, gain_final):
    out_final[...] = out_ref[...]
    gt_final[...] = gt_ref[...]
    gi_final[...] = gi_ref[...]
    go_final[...] = go_ref[...]
    at = (lax.axis_index("lat") * 32 + lax.axis_index("lon")) * 8
    place = lax.broadcasted_iota(jnp.int32, (8, 128), 0) * 128 + lax.broadcasted_iota(jnp.int32, (8, 128), 1)
    for n in range(8):
        gain_final[n] = jnp.sum(jnp.where(place == at + n, gg_ref[...], 0.0))


def finish(*results):
    vm = pl.BlockSpec(memory_space=pltpu.VMEM)
    rows = pl.BlockSpec((PAIR, D), lambda i: (i, 0))
    return pl.pallas_call(
        finish_kernel,
        grid=(3,),
        in_specs=[rows, rows, vm, vm, vm],
        out_specs=[rows, rows, vm, vm, pl.BlockSpec(memory_space=pltpu.SMEM)],
        out_shape=[
            jax.ShapeDtypeStruct((OWN, D), BF),
            jax.ShapeDtypeStruct((OWN, D), BF),
            jax.ShapeDtypeStruct((8, 3 * D), BF),
            jax.ShapeDtypeStruct((8, D), BF),
            jax.ShapeDtypeStruct((8,), F32),
        ],
    )(*results)


def local(tokens, norm_gain, attention_in, attention_out, head_bias, cotangent):
    shape = tokens.shape
    out, gt, gi, go, gain = finish(
        *block(
            tokens.reshape(OWN, D), cotangent.reshape(OWN, D), norm_gain, attention_in, attention_out, head_bias
        )
    )
    return out.reshape(shape), gt.reshape(shape), gi, go, gain


def solution(mesh):
    split = P(None, "lat", "lon", None)
    both = ("lat", "lon")
    return jax.shard_map(
        local,
        mesh=mesh,
        in_specs=(split, P(), P(), P(), P(), split),
        out_specs=(split, split, P(both, None), P(both, None), P(both)),
        check_vma=False,
    )
```

```python
import jax
import jax.numpy as jnp
import numpy as np
from jax import lax
from jax.experimental import pallas as pl
from jax.experimental.pallas import tpu as pltpu
from jax.sharding import PartitionSpec as P

D = 1024
WINT = 144
PAIR = 288
OWN = 864
STRIP = 400
NT = (((1,), (1,)), ((), ()))
TN = (((0,), (0,)), ((), ()))
BF = jnp.bfloat16
F32 = jnp.float32

AXES = ("x", "y", "z")
ORDERS = (
    (("x", "y", "z"), ("y", "z", "x"), ("z", "x", "y")),
    (("x", "y", "z"), ("y", "z", "x"), ("z", "x", "y")),
    (("x", "z", "y"), ("z", "x", "y")),
)
PIECES = (
    tuple(("in", 1024 * g, 512) for g in range(3)),
    tuple(("in", 1024 * g + 512, 512) for g in range(3)),
    tuple(("out", 512 * g, 512) for g in range(2)),
)
LANES = 256
FIRST = 128
GROUPS = tuple((r, g) for r in range(3) for g in range(len(ORDERS[r])))


def strip_cells(core):
    cells = [(l, r, c) for l in range(2) for r in range(3) for c in range(24)]
    cells += [(l, r, c) for l in range(2) for r in range(3, 9) for c in range(18, 24)] + [None] * 8
    first = 0 if core else 18
    cells += [(l, r, c) for l in range(2) for r in range(9, 15) for c in range(first, first + 6)] + [None] * 8
    cells += [(l, r, c) for l in range(2) for r in range(15, 18) for c in range(6)] + [None] * 12
    cells += [(l, r, c) for l in range(2) for r in range(3) for c in range(6)] + [None] * 12
    return cells


def received_cells(core):
    cells = []
    for n, cell in enumerate(strip_cells(core)):
        if cell is None:
            cells.append(None)
            continue
        l, r, c = cell
        if n < 144 or n >= 352:
            r += 18
        if n >= 144:
            c += 24 if c < 6 else -24
        cells.append((l, r, c))
    return cells


def window_cells(core):
    corners = ((3, 6), (9, 6), (15, 6), (15, 18), (3, -6), (9, 18 if core else -6))
    return [(l, r + a, c + b) for r, c in corners for l in range(2) for a in range(6) for b in range(12)]


def one_hot(targets, sources):
    place = {}
    for n, cell in enumerate(sources):
        if cell is not None and cell not in place:
            place[cell] = n
    out = np.zeros((len(targets), len(sources)), np.float32)
    for n, cell in enumerate(targets):
        if cell is not None and cell in place:
            out[n, place[cell]] = 1
    return out


def permutations():
    own = [(l, r, c) for l in range(2) for r in range(18) for c in range(24)]
    wide = own[64:368] + own[496:800]
    mid = own[72:360] + own[504:792]
    bottom = own[360:432] + own[792:864]
    top = own[:72] + own[432:504]
    every = []
    for core in range(2):
        strips = strip_cells(core)
        got = received_cells(core)
        win = window_cells(core)
        inner = [c if c is not None and c[2] >= 6 else None for c in strips[:144]]
        every.append(
            (
                one_hot(strips, own),
                one_hot(win[:288], wide),
                one_hot(win[288:576], own[352:432] + own[784:864] + got[:144] + got[304:]),
                one_hot(win[576:], wide + got[144:304]),
                one_hot(got[:144] + got[304:], win[288:576]),
                one_hot(got[144:304], win[576:]),
                one_hot(mid, win[:288] + win[576:] + strips[144:304]),
                one_hot(bottom, win[288:576] + strips[304:352]),
                one_hot(top, inner + strips[352:]),
            )
        )
    return tuple(np.stack(pair) for pair in zip(*every))


def region_mask():
    region = np.array([a < 3 for l in range(2) for a in range(6) for b in range(12)])
    one = np.where(region[:, None] == region[None, :], 0.0, -1e9).astype(np.float32)
    return np.concatenate([one] * 4, 1)


def dg(a, b, dims):
    return lax.dot_general(a, b, dims, preferred_element_type=F32)


def dot(a, b):
    return jnp.dot(a, b, preferred_element_type=F32)


def mesh_place(core, x, y, z):
    return ((z % 2) * 2 + core, (z // 2) * 16 + x * 4 + y)


def block_kernel(
    tok_hbm, cot_hbm, gain_ref, win_hbm, wout_hbm, hb_hbm, mask_ref,
    pack_hbm, p0_hbm, p1_hbm, p2_hbm, r1_hbm, r2_hbm, imid_hbm, ibot_hbm, itop_hbm,
    out_hbm, gt_hbm, gi_out, go_out, gg_out,
    *scratch,
):
    scratch = list(scratch)

    def take(count):
        out = scratch[:count]
        del scratch[:count]
        return out

    own_x, own_c, xw, cw, nw, nwt, proj, gctx, win, wout, raw, bias, mask = take(13)
    perms = take(9)
    pack_ref, p0_ref, p1_ref, p2_ref, r1_ref, r2_ref, imid_ref, ibot_ref, itop_ref = perms
    send_strip, recv_strip = take(2) * 2, take(4)
    sends = {at: take(1)[0] for at in GROUPS}
    owns = {at: take(1)[0] for at in GROUPS}
    halves = {at: take(1)[0] for at in GROUPS}
    landing = {(r, g, p): take(3 if p else 8) for r, g in GROUPS for p in range(3)}
    middles = {(r, g, p): take(1)[0] for r, g in GROUPS for p in range(2)}
    gain_mine, gain_land = take(2)
    load_sem, strip_send, strip_recv, core_send, core_recv = take(5)
    ring_send, ring_recv, gain_send, gain_recv = take(4)

    lat = lax.axis_index("lat")
    lon = lax.axis_index("lon")
    core = lat % 2
    me = {"x": (lon // 4) % 4, "y": lon % 4, "z": (lon // 16) * 2 + lat // 2}

    def device(axis, step):
        at = dict(me)
        at[axis] = (me[axis] + step + 4) % 4
        return mesh_place(core, at["x"], at["y"], at["z"])

    sibling = mesh_place(1 - core, me["x"], me["y"], me["z"])

    def grid_place(a, b):
        return ((lat + a + 4) % 4, (lon + b + 32) % 32)

    loads = [
        pltpu.make_async_copy(src, dst, load_sem.at[n])
        for n, (src, dst) in enumerate(
            (
                (tok_hbm, own_x), (pack_hbm.at[core], pack_ref), (cot_hbm, own_c), (p0_hbm.at[core], p0_ref),
                (hb_hbm, raw), (win_hbm, win), (wout_hbm, wout), (p1_hbm.at[core], p1_ref), (p2_hbm.at[core], p2_ref),
                (r1_hbm.at[core], r1_ref), (r2_hbm.at[core], r2_ref), (imid_hbm.at[core], imid_ref),
                (ibot_hbm.at[core], ibot_ref), (itop_hbm.at[core], itop_ref),
            )
        )
    ]
    for load in loads[:4]:
        load.start()

    barrier = pltpu.get_barrier_semaphore()
    partners = [sibling] + [device(a, s) for a in AXES for s in (1, -1, 2)]
    partners += [grid_place(s * a, s * b) for a, b in ((1, 0), (0, 1), (1, 1)) for s in (1, -1)]
    for other in partners:
        pl.semaphore_signal(barrier, inc=1, device_id=other, device_id_type=pl.DeviceIdType.MESH)
    pl.semaphore_wait(barrier, len(partners))

    def remote(src, dst, send, recv, place):
        copy = pltpu.make_async_remote_copy(
            src_ref=src,
            dst_ref=dst,
            send_sem=send,
            recv_sem=recv,
            device_id=place,
            device_id_type=pl.DeviceIdType.MESH,
        )
        copy.start()
        return copy

    turned = jnp.where(core == 0, 1, -1)
    PARTS = ((0, 144, -1, 0), (144, 80, 0, 1), (224, 80, 0, turned), (304, 48, 0, -1), (352, 48, -1, -1))

    def send_strips(number, way, parts=range(5)):
        copies = []
        for part in parts:
            low, size, a, b = PARTS[part]
            copies.append(
                remote(
                    send_strip[number].at[pl.ds(low, size)],
                    recv_strip[number].at[pl.ds(low, size)],
                    strip_send.at[number, part],
                    strip_recv.at[number, part],
                    grid_place(way * a, way * b),
                )
            )
        return copies

    strip_copies = []
    loads[0].wait()
    loads[1].wait()
    for load in loads[4:7]:
        load.start()
    for number, own in ((0, own_x), (1, own_c)):
        if number == 1:
            loads[2].wait()
        send_strip[number][...] = dot(pack_ref[...], own[...]).astype(BF)
        strip_copies.append(send_strips(number, 1))

    def gathered(own, strip, s):
        if s == 1:
            parts = [own[352:432], own[784:864], strip[0:144], strip[304:400]]
            return dot(p1_ref[...], jnp.concatenate(parts, 0))
        parts = [own[64:368], own[496:800]]
        if s == 0:
            return dot(p0_ref[...], jnp.concatenate(parts, 0))
        return dot(p2_ref[...], jnp.concatenate(parts + [strip[144:304]], 0))

    def standardised(x):
        centred = x - jnp.mean(x, axis=-1, keepdims=True)
        inverse = lax.rsqrt(jnp.mean(centred * centred, axis=-1, keepdims=True) + 1e-5)
        return centred * inverse, inverse

    def gather_tokens(s):
        rows = slice(s * PAIR, (s + 1) * PAIR)
        x = gathered(own_x, recv_strip[0], s)
        xw[rows] = x.astype(BF)
        standard, _ = standardised(x)
        nw[rows] = (standard * gain_ref[...]).astype(BF)

    def gather_cotangent(s):
        rows = slice(s * PAIR, (s + 1) * PAIR)
        cw[rows] = gathered(own_c, recv_strip[1], s).astype(BF)

    def project(s, count):
        rows = slice(s * PAIR, s * PAIR + count)

        def columns(n, _):
            at = pl.ds(pl.multiple_of(n * 512, 512), 512)
            value = dot(nw[rows], win[:, at])
            proj[rows, at] = (value * jnp.where(n < 2, 0.125, 1.0)).astype(BF)
            return 0

        lax.fori_loop(0, 6, columns, 0)

    def project_back(s, count):
        rows = slice(s * PAIR, s * PAIR + count)

        def outer(n, _):
            at = pl.ds(pl.multiple_of(n * 512, 512), 512)
            gctx[rows, at] = dg(cw[rows], wout[at, :], NT).astype(BF)
            return 0

        lax.fori_loop(0, 2, outer, 0)

    head = lax.broadcasted_iota(jnp.int32, (WINT, 256), 1) // 64
    low_half = lax.broadcasted_iota(jnp.int32, (WINT, 128), 1) < 64
    zero = jnp.zeros((WINT, 256), BF)

    def stacked(a):
        return jnp.concatenate([jnp.where(head == h, a, zero) for h in range(4)], 0)

    def by_query(scores, a):
        turned = scores.T
        parts = []
        for n in range(2):
            both = dot(turned[n * PAIR : (n + 1) * PAIR], a[:, n * 128 : (n + 1) * 128])
            parts.append(jnp.where(low_half, both[:WINT], both[WINT:]))
        return jnp.concatenate(parts, 1)

    def unit(w, p, masked):
        rows = pl.ds(pl.multiple_of(w * WINT, 16), WINT)
        at_q = pl.ds(pl.multiple_of(p * 256, 256), 256)
        at_k = pl.ds(pl.multiple_of(1024 + p * 256, 256), 256)
        at_v = pl.ds(pl.multiple_of(2048 + p * 256, 256), 256)
        q, k, v, d = proj[rows, at_q], proj[rows, at_k], proj[rows, at_v], gctx[rows, at_q]
        qs, ds = stacked(q), stacked(d)
        offset = bias[p]
        if masked:
            offset = offset + mask[...]
        st = dg(k, qs, NT) + offset
        powers = jnp.exp(st - jnp.max(st, axis=0, keepdims=True))
        weights = powers * (1.0 / jnp.sum(powers, axis=0, keepdims=True))
        wb = weights.astype(BF)
        dw = dg(v, ds, NT)
        inner = jnp.sum(dw * weights, axis=0, keepdims=True)
        gs = (weights * (dw - inner)).astype(BF)
        gctx[rows, at_q] = by_query(wb, v).astype(BF)
        proj[rows, at_q] = (by_query(gs, k) * 0.125).astype(BF)
        proj[rows, at_k] = dot(gs, qs).astype(BF)
        proj[rows, at_v] = dot(wb, ds).astype(BF)

    def late_windows(p, t):
        unit(2 + 2 * t, p, t == 0)
        unit(3 + 2 * t, p, t == 0)

    def products(rnd, g, half, target):
        kind, first, width = PIECES[rnd][g]
        right = proj if kind == "in" else cw

        order = ORDERS[rnd][g]

        def rows_of(zl, _):
            at = pl.multiple_of(zl * 512 + half * 256, 256)
            value = dot(nwt[pl.ds(at, 256), :], right[:, first : first + width]).reshape(32, 8, width)
            both = jnp.concatenate([value[:, :, :LANES], value[:, :, LANES:]], 1).astype(BF)
            both = both.reshape(2, 4, 4, 16, LANES)
            for zh in range(2):
                z = 2 * zh + zl
                for end in range(2):
                    part = both[zh, :, :, :, end * FIRST : (end + 1) * FIRST]
                    if order.index("y") < order.index("x"):
                        part = jnp.swapaxes(part, 0, 1)
                    place = [end, slice(None), slice(None), slice(None)]
                    place[1 + order.index("z")] = z
                    target[tuple(place)] = part
            return 0

        lax.fori_loop(0, 2, rows_of, 0)

    core_copies = {}

    def start_round(rnd):
        for g in range(len(ORDERS[rnd])):
            products(rnd, g, 1 - core, sends[rnd, g])
            core_copies[rnd, g] = remote(
                sends[rnd, g], halves[rnd, g], core_send.at[rnd, g], core_recv.at[rnd, g], sibling
            )

    def own_products(rnd):
        for g in range(len(ORDERS[rnd])):
            products(rnd, g, core, owns[rnd, g])

    def end_core(rnd):
        for g in range(len(ORDERS[rnd])):
            core_copies[rnd, g].wait()
            mine = owns[rnd, g]
            mine[...] = (mine[...].astype(F32) + halves[rnd, g][...].astype(F32)).astype(BF)
            ring_start_group(rnd, g, 0)

    def chunk(rnd, g, phase, step, half):
        ref = owns[rnd, g] if phase == 0 else middles[rnd, g, phase - 1]
        return ref.at[half, (me[ORDERS[rnd][g][phase]] + step + 4) % 4]

    def ring(rnd, g, phase, number, src, step):
        return remote(
            src,
            landing[rnd, g, phase][number],
            ring_send.at[GROUPS.index((rnd, g)), (0, 6, 9)[phase] + number],
            ring_recv.at[GROUPS.index((rnd, g)), (0, 6, 9)[phase] + number],
            device(ORDERS[rnd][g][phase], step),
        )

    flying = {}

    def ring_start_group(rnd, g, phase):
        if phase == 0:
            flying[rnd, g] = {
                0: ring(rnd, g, phase, 0, chunk(rnd, g, phase, 2, 0), 1),
                3: ring(rnd, g, phase, 3, chunk(rnd, g, phase, 2, 1), -1),
                1: ring(rnd, g, phase, 1, chunk(rnd, g, phase, 1, 1), 1),
                4: ring(rnd, g, phase, 4, chunk(rnd, g, phase, -1, 0), -1),
            }
            return
        flying[rnd, g] = {
            n: ring(rnd, g, phase, n, chunk(rnd, g, phase, n + 1, slice(None)), n + 1) for n in range(3)
        }

    def ring_relay(rnd):
        for g in range(len(ORDERS[rnd])):
            land = landing[rnd, g, 0]
            for number, step, half, slot in ((0, 1, 0, 6), (3, -1, 1, 7)):
                flying[rnd, g][number].wait_recv()
                land[slot][...] = (
                    land[number][...].astype(F32) + chunk(rnd, g, 0, step, half)[...].astype(F32)
                ).astype(BF)
                flying[rnd, g][number + 2] = ring(rnd, g, 0, number + 2, land[slot], step)

    def ring_end(rnd, phase):
        for g in range(len(ORDERS[rnd])):
            land = landing[rnd, g, phase]
            copies = flying[rnd, g]
            if phase == 0:
                for number in (1, 4, 2, 5):
                    copies[number].wait()
                copies[0].wait_send()
                copies[3].wait_send()
                for half, near, far in ((0, 4, 2), (1, 1, 5)):
                    middles[rnd, g, phase][half] = (
                        chunk(rnd, g, phase, 0, half)[...].astype(F32)
                        + land[near][...].astype(F32)
                        + land[far][...].astype(F32)
                    ).astype(BF)
                ring_start_group(rnd, g, 1)
                continue
            for number in range(3):
                copies[number].wait()
            value = chunk(rnd, g, phase, 0, slice(None))[...].astype(F32)
            for number in range(3):
                value = value + land[number][...].astype(F32)
            value = value.astype(BF)
            if phase == 1:
                middles[rnd, g, phase][...] = value
                ring_start_group(rnd, g, 2)
                continue
            kind, first, _ = PIECES[rnd][g]
            target = gi_out if kind == "in" else go_out
            for half in range(2):
                at = first + half * FIRST
                target[:, at : at + FIRST] = value[half, :8]
                target[:, at + LANES : at + LANES + FIRST] = value[half, 8:]

    def gain_start(stage):
        if stage == 0:
            return [remote(gain_mine.at[0], gain_land.at[0], gain_send.at[0], gain_recv.at[0], sibling)]
        return [
            remote(
                gain_mine.at[stage],
                gain_land.at[3 * stage - 2 + n],
                gain_send.at[3 * stage - 2 + n],
                gain_recv.at[3 * stage - 2 + n],
                device(AXES[stage - 1], n + 1),
            )
            for n in range(3)
        ]

    def gain_finish(stage, copies):
        total = gain_mine[stage]
        for copy in copies:
            copy.wait()
        if stage == 0:
            return total + gain_land[0]
        slot = 3 * stage - 2
        return total + gain_land[slot] + gain_land[slot + 1] + gain_land[slot + 2]

    def attended_step(s):
        rows = slice(s * PAIR, (s + 1) * PAIR)
        attended = dot(gctx[rows], wout[...]).astype(BF).astype(F32)
        xw_out[rows] = (xw[rows].astype(F32) + attended).astype(BF)

    def grad_step(s):
        rows = slice(s * PAIR, (s + 1) * PAIR)
        grad = dg(proj[rows], win[...], NT).astype(BF).astype(F32)
        standard, inverse = standardised(xw[rows].astype(F32))
        scaled = grad * gain_ref[...]
        first = jnp.mean(scaled, axis=-1, keepdims=True)
        second = jnp.mean(scaled * standard, axis=-1, keepdims=True)
        local = inverse * (scaled - first - standard * second)
        cw[rows] = (cw[rows].astype(F32) + local).astype(BF)
        return jnp.sum(grad * standard, axis=0, keepdims=True)

    def pack_back(number, final):
        both = dot(r1_ref[...], final[PAIR : 2 * PAIR]).astype(BF)
        send_strip[number][0:144] = both[:144]
        send_strip[number][304:400] = both[144:]
        send_strip[number][144:304] = dot(r2_ref[...], final[2 * PAIR :]).astype(BF)
        return send_strips(number, -1)

    def assemble(own, final, strip):
        value = dot(
            imid_ref[...], jnp.concatenate([final[:PAIR], final[2 * PAIR :], strip[144:304]], 0)
        ).astype(BF)
        own[72:360] = value[:288]
        own[504:792] = value[288:]
        value = dot(ibot_ref[...], jnp.concatenate([final[PAIR : 2 * PAIR], strip[304:352]], 0)).astype(BF)
        own[360:432] = value[:72]
        own[792:864] = value[72:]
        value = dot(itop_ref[...], jnp.concatenate([strip[0:144], strip[352:400]], 0)).astype(BF)
        own[0:72] = value[:72]
        own[432:504] = value[72:]

    xw_out = nw

    loads[3].wait()
    gather_tokens(0)
    gather_cotangent(0)
    loads[4].wait()
    mask[...] = jnp.where(lat == 3, 1.0, 0.0) * mask_ref[...]

    def turn(p, _):
        for h in range(4):
            bias[p, :, h * WINT : (h + 1) * WINT] = raw[4 * p + h].T
        return 0

    lax.fori_loop(0, 4, turn, 0)
    loads[5].wait()
    project(0, PAIR)
    loads[6].wait()
    project_back(0, PAIR)
    for load in loads[7:]:
        load.start()

    def early(p, _):
        unit(0, p, False)
        unit(1, p, False)
        return 0

    lax.fori_loop(0, 4, early, 0)
    for load in loads[7:]:
        load.wait()
    for copy in strip_copies[0]:
        copy.wait()
    gather_tokens(1)
    gather_tokens(2)
    project(1, 2 * PAIR)

    def turn_rows(n, _):
        at = pl.ds(pl.multiple_of(n * 256, 256), 256)
        nwt[at, :] = nw[:, at].T
        return 0

    lax.fori_loop(0, 4, turn_rows, 0)
    for copy in strip_copies[1]:
        copy.wait()
    gather_cotangent(1)
    gather_cotangent(2)
    project_back(1, 2 * PAIR)

    def first_pairs(p, _):
        late_windows(p, 0)
        late_windows(p, 1)
        return 0

    lax.fori_loop(0, 2, first_pairs, 0)
    start_round(0)
    own_products(0)
    late_windows(2, 0)
    late_windows(2, 1)
    end_core(0)
    late_windows(3, 0)
    late_windows(3, 1)
    start_round(1)
    own_products(1)

    def turn_context(n, _):
        at = pl.ds(pl.multiple_of(n * 256, 256), 256)
        nwt[at, :] = gctx[:, at].T
        return 0

    lax.fori_loop(0, 4, turn_context, 0)
    start_round(2)
    attended_step(1)
    attended_step(2)
    back_out = pack_back(2, xw_out)
    ring_relay(0)
    end_core(1)
    own_products(2)
    gain = grad_step(1)
    end_core(2)
    ring_end(0, 0)
    gain += grad_step(2)
    back_grad = pack_back(3, cw)
    ring_relay(1)
    gain += grad_step(0)
    for n in range(8):
        gain_mine[0, n : n + 1, :] = gain[:, n * 128 : (n + 1) * 128]
    gain_copies = gain_start(0)
    ring_relay(2)
    ring_end(0, 1)
    attended_step(0)
    ring_end(1, 0)
    gain_mine[1] = gain_finish(0, gain_copies)
    gain_copies = gain_start(1)
    for copy in back_out:
        copy.wait()
    assemble(own_x, xw_out, recv_strip[2])
    store_out = pltpu.make_async_copy(own_x, out_hbm, load_sem.at[0])
    store_out.start()
    ring_end(2, 0)
    gain_mine[2] = gain_finish(1, gain_copies)
    gain_copies = gain_start(2)
    ring_end(1, 1)
    for copy in back_grad:
        copy.wait()
    assemble(own_c, cw, recv_strip[3])
    store_grad = pltpu.make_async_copy(own_c, gt_hbm, load_sem.at[1])
    store_grad.start()
    ring_end(2, 1)
    gain_mine[3] = gain_finish(2, gain_copies)
    gain_copies = gain_start(3)
    ring_end(0, 2)
    ring_end(1, 2)
    ring_end(2, 2)
    gg_out[...] = gain_finish(3, gain_copies)
    store_out.wait()
    store_grad.wait()


def block(tokens, cotangent, gain, attention_in, attention_out, head_bias):
    vm = pl.BlockSpec(memory_space=pltpu.VMEM)
    hbm = pl.BlockSpec(memory_space=pl.ANY)
    perms = [jnp.asarray(m, BF) for m in permutations()]
    wide = lambda rows, columns=D: pltpu.VMEM((rows, columns), BF)
    scratch = [wide(OWN) for _ in range(5)]
    scratch += [wide(D, OWN), wide(OWN, 3 * D), wide(OWN), wide(D, 3 * D), wide(D)]
    scratch += [pltpu.VMEM((16, WINT, WINT), F32), pltpu.VMEM((4, WINT, 4 * WINT), F32), pltpu.VMEM((WINT, 4 * WINT), F32)]
    scratch += [wide(*m.shape[1:]) for m in perms]
    scratch += [wide(STRIP) for _ in range(6)]
    scratch += [pltpu.VMEM((2, 4, 4, 4, 16, FIRST), BF) for _ in range(3 * len(GROUPS))]
    middles = []
    for r, g in GROUPS:
        for phase in range(3):
            lead = (4,) * (2 - phase)
            if phase == 0:
                scratch += [pltpu.VMEM(lead + (16, FIRST), BF) for _ in range(8)]
            else:
                scratch += [pltpu.VMEM((2,) + lead + (16, FIRST), BF) for _ in range(3)]
            if phase < 2:
                middles.append(pltpu.VMEM((2,) + lead + (16, FIRST), BF))
    scratch += middles
    scratch += [pltpu.VMEM((4, 8, 128), F32), pltpu.VMEM((10, 8, 128), F32)]
    dma = pltpu.SemaphoreType.DMA
    scratch += [dma((14,)), dma((4, 5)), dma((4, 5)), dma((3, 3)), dma((3, 3))]
    scratch += [dma((len(GROUPS), 12)), dma((len(GROUPS), 12)), dma((10,)), dma((10,))]
    return pl.pallas_call(
        block_kernel,
        in_specs=[hbm, hbm, vm, hbm, hbm, hbm, vm] + [hbm] * 9,
        out_specs=[hbm, hbm, vm, vm, vm],
        out_shape=[
            jax.ShapeDtypeStruct((OWN, D), BF),
            jax.ShapeDtypeStruct((OWN, D), BF),
            jax.ShapeDtypeStruct((8, 3 * D), BF),
            jax.ShapeDtypeStruct((8, D), BF),
            jax.ShapeDtypeStruct((8, 128), F32),
        ],
        scratch_shapes=scratch,
        compiler_params=pltpu.CompilerParams(
            collective_id=0, has_side_effects=True, vmem_limit_bytes=63 * 2**20
        ),
    )(
        tokens, cotangent, gain.reshape(1, D), attention_in, attention_out, head_bias,
        jnp.asarray(region_mask()), *perms,
    )


def finish_kernel(out_ref, gt_ref, gi_ref, go_ref, gg_ref, out_final, gt_final, gi_final, go_final, gain_final):
    out_final[...] = out_ref[...]
    gt_final[...] = gt_ref[...]
    gi_final[...] = gi_ref[...]
    go_final[...] = go_ref[...]
    at = (lax.axis_index("lat") * 32 + lax.axis_index("lon")) * 8
    place = lax.broadcasted_iota(jnp.int32, (8, 128), 0) * 128 + lax.broadcasted_iota(jnp.int32, (8, 128), 1)
    for n in range(8):
        gain_final[n] = jnp.sum(jnp.where(place == at + n, gg_ref[...], 0.0))


def finish(*results):
    vm = pl.BlockSpec(memory_space=pltpu.VMEM)
    rows = pl.BlockSpec((432, D), lambda i: (i, 0))
    return pl.pallas_call(
        finish_kernel,
        grid=(2,),
        in_specs=[rows, rows, vm, vm, vm],
        out_specs=[rows, rows, vm, vm, pl.BlockSpec(memory_space=pltpu.SMEM)],
        out_shape=[
            jax.ShapeDtypeStruct((OWN, D), BF),
            jax.ShapeDtypeStruct((OWN, D), BF),
            jax.ShapeDtypeStruct((8, 3 * D), BF),
            jax.ShapeDtypeStruct((8, D), BF),
            jax.ShapeDtypeStruct((8,), F32),
        ],
        compiler_params=pltpu.CompilerParams(vmem_limit_bytes=32 * 2**20),
    )(*results)


def local(tokens, norm_gain, attention_in, attention_out, head_bias, cotangent):
    shape = tokens.shape
    out, gt, gi, go, gain = finish(
        *block(
            tokens.reshape(OWN, D), cotangent.reshape(OWN, D), norm_gain, attention_in, attention_out, head_bias
        )
    )
    return out.reshape(shape), gt.reshape(shape), gi, go, gain


def solution(mesh):
    split = P(None, "lat", "lon", None)
    both = ("lat", "lon")
    return jax.shard_map(
        local,
        mesh=mesh,
        in_specs=(split, P(), P(), P(), P(), split),
        out_specs=(split, split, P(both, None), P(both, None), P(both)),
        check_vma=False,
    )
```
